128 devices in a mesh: row: 2 (over x_hi), col: 64 (over x_lo, y, z, core).
Axes of the slice: x: 4 (x_hi: 2, x_lo: 2; x = x_hi * 2 + x_lo), y: 4, z: 4, core: 2. Of those that a mesh axis runs over, the one named last changes fastest.
Arguments:
- tokens: bfloat16 [2, 24576, 768], P('row', 'col'), may hold values from -6 to 6
- attn_gain: bfloat16 [768], replicated, may hold values from 0.099609375 to 1.8984375
- query_weight: bfloat16 [768, 768], replicated, may hold values from -0.21875 to 0.21875
- key_weight: bfloat16 [768, 768], replicated, may hold values from -0.21875 to 0.21875
- value_weight: bfloat16 [768, 768], replicated, may hold values from -0.21875 to 0.21875
- output_weight: bfloat16 [768, 768], replicated, may hold values from -2.5 to 2.5
- ffn_gain: bfloat16 [768], replicated, may hold values from 0.099609375 to 1.8984375
- gate_weight: bfloat16 [768, 2048], replicated, may hold values from -0.21875 to 0.21875
- up_weight: bfloat16 [768, 2048], replicated, may hold values from -0.21875 to 0.21875
- down_weight: bfloat16 [2048, 768], replicated, may hold values from -0.125 to 0.125
- relative_table: bfloat16 [32, 12], replicated, may hold values from -3 to 3
- layout_table: bfloat16 [32, 12], replicated, may hold values from -3 to 3
- cotangent: bfloat16 [2, 24576, 768], P('row', 'col'), may hold values from -6 to 6
- rel_bucket: int32 [2, 24576, 768], P('row', 'col'), may hold values from 0 to 32, as said below
- layout_bucket: int32 [2, 24576, 768], P('row', 'col'), may hold values from 0 to 31
- halo_index: int32 [2, 64, 4, 96], P('row', 'col'), may hold values from -1 to 383, as said below
Outputs:
- layer_out: bfloat16 [2, 24576, 768], P('row', 'col')
- input_grad: bfloat16 [2, 24576, 768], P('row', 'col')
- attn_gain_grad: float32 [768], replicated
- query_grad: float32 [768, 768], replicated
- key_grad: float32 [768, 768], replicated
- value_grad: float32 [768, 768], replicated
- output_grad: float32 [768, 768], replicated
- ffn_gain_grad: float32 [768], replicated
- gate_grad: float32 [768, 2048], replicated
- up_grad: float32 [768, 2048], replicated
- down_grad: float32 [2048, 768], replicated
- relative_grad: float32 [32, 12], replicated
- layout_grad: float32 [32, 12], replicated
The draws below stay inside these ranges and needn't reach their ends.
Inputs may be any that keep to these rules, and one draw needn't show every extreme that they name: `halo_index`: block [r, c, d] lists the tokens of region (r, c) that the neighbour in direction d reads (0: next row, 1: previous row, 2: next column, 3: previous column): between 48 and 96 distinct indices first, then -1; some block is full and some holds exactly 48 indices. `rel_bucket`: for a query of region (r, c), slots below 384 are its own region's tokens (never marked); then four blocks of 96 slots follow the order of the key window. The value 32 marks a slot that is no key: a missing region, a region of another page, or a -1 of the sender's block; pages cover both rows and 2 or 4 neighbouring columns.
All inputs are finite; a program needn't handle non-finite values.
Results may differ from the reference program's by a relative error of at most 0.015.
Values may be sent and summed in bfloat16 or wider, within the bound.
No kernel may reach another device: no remote copies, remote signals or barrier semaphores. Data moves between devices by JAX's collectives and lax.ppermute only.
A program may use at most 256 MiB of HBM per device.

```python
import jax
import jax.numpy as jnp
from jax import lax

D = 768
HEADS = 12
HEAD = 64
FF = 2048
BUCKETS = 32
LAYOUT_BUCKETS = 32
TOK_DEV = 384
HALO = 96
WIN = 768
GRID_ROWS = 2
GRID_COLS = 64
COL_TOKENS = 24576


def page_layout(key):
    key = jax.random.fold_in(key, 11)
    pairs = GRID_COLS // 2
    flips = jax.random.randint(key, (pairs,), 0, 2)

    def advance(previous, flip):
        start = jnp.where(previous == 1, flip, 1).astype(jnp.int32)
        return (start, start)
    _, starts = lax.scan(advance, jnp.int32(0), flips)
    pages = jnp.cumsum(starts) - 1
    return jnp.repeat(pages, 2)


def halo_counts(key):
    key = jax.random.fold_in(key, 12)
    counts = jax.random.randint(key, (GRID_ROWS, GRID_COLS, 4), HALO // 2, HALO + 1)
    flat = counts.reshape(-1)
    total = flat.shape[0]
    first = jax.random.randint(jax.random.fold_in(key, 1), (), 0, total)
    other = (first + 1 + jax.random.randint(jax.random.fold_in(key, 2), (), 0, total - 1)) % total
    flat = flat.at[first].set(HALO).at[other].set(HALO // 2)
    return flat.reshape(GRID_ROWS, GRID_COLS, 4)


def draw_halo_index(key, part):
    counts = halo_counts(key)
    key = jax.random.fold_in(key, 21)
    total = GRID_ROWS * GRID_COLS * 4
    orders = jax.vmap(lambda single: jax.random.permutation(single, TOK_DEV))(jax.random.split(key, total))
    flips = jax.random.randint(jax.random.fold_in(key, 3), (total,), 0, 2)
    chosen = jax.random.randint(jax.random.fold_in(key, 4), (), 0, total)
    flips = flips.at[chosen].set(1)[:, None]
    leading = orders[:, :1]
    slots = jnp.arange(TOK_DEV)[None, :]
    swapped = jnp.where(orders == TOK_DEV - 1, leading, orders)
    swapped = jnp.where(slots == 0, TOK_DEV - 1, swapped)
    orders = jnp.where(flips == 1, swapped, orders)[:, :HALO]
    filled = jnp.arange(HALO)[None, :] < counts.reshape(-1)[:, None]
    return jnp.where(filled, orders, -1).reshape(GRID_ROWS, GRID_COLS, 4, HALO).astype(jnp.int32)


def draw_rel_bucket(key, part):
    counts = halo_counts(key)
    pages = page_layout(key)
    key = jax.random.fold_in(key, 31)
    raw = jax.random.randint(key, (GRID_ROWS, GRID_COLS, TOK_DEV, WIN), 0, BUCKETS)
    row_zero = jnp.zeros((1, GRID_COLS), jnp.int32)
    col_zero = jnp.zeros((GRID_ROWS, 1), jnp.int32)
    lower = jnp.concatenate([row_zero, counts[:-1, :, 0]], axis=0)
    upper = jnp.concatenate([counts[1:, :, 1], row_zero], axis=0)
    same_left = jnp.concatenate([jnp.zeros((1,), bool), pages[1:] == pages[:-1]])
    same_right = jnp.concatenate([pages[:-1] == pages[1:], jnp.zeros((1,), bool)])
    left = jnp.where(same_left[None, :], jnp.concatenate([col_zero, counts[:, :-1, 2]], axis=1), 0)
    right = jnp.where(same_right[None, :], jnp.concatenate([counts[:, 1:, 3], col_zero], axis=1), 0)
    own = jnp.full((GRID_ROWS, GRID_COLS), TOK_DEV, jnp.int32)
    limits = jnp.stack([own, lower, upper, left, right], axis=-1)
    slots = jnp.arange(WIN)
    blocks = jnp.where(slots < TOK_DEV, 0, (slots - TOK_DEV) // HALO + 1)
    offsets = jnp.where(slots < TOK_DEV, 0, (slots - TOK_DEV) % HALO)
    valid = offsets[None, None, :] < limits[:, :, blocks]
    marked = jnp.where(valid[:, :, None, :], raw, BUCKETS)
    return marked.reshape(GRID_ROWS, GRID_COLS * TOK_DEV, WIN).astype(jnp.int32)


def plant(drawn, key, low, largest):
    index_at = [jax.random.randint(jax.random.fold_in(key, axis), (), 0, length) for axis, length in enumerate(drawn.shape)]
    longest = drawn.shape.index(max(drawn.shape))
    neighbour = index_at[:longest] + [(index_at[longest] + 1) % drawn.shape[longest]] + index_at[longest + 1:]
    return drawn.at[tuple(index_at)].set(low).at[tuple(neighbour)].set(largest)


def block_levels(own_key, extent, shards, low, top_value):
    def one(dim, parts):
        steps = jax.random.uniform(jax.random.fold_in(jax.random.fold_in(own_key, 6), dim), (parts,), jnp.float32, low / len(shards), top_value / len(shards))
        return jnp.repeat(jnp.exp(steps), extent[dim] // parts).reshape((-1,) + (1,) * (len(extent) - dim - 1))

    level = one(*shards[0])
    for cut in shards[1:]:
        level = level * one(*cut)
    return level


def scatter_about(own_key, dims, width, reach, cuts=(), kind=jnp.bfloat16):
    values = jax.random.normal(own_key, dims, jnp.float32) * width
    if len(cuts) > 0:
        values = block_levels(own_key, dims, cuts, -0.22, 0.18) * values
    return jnp.clip(values, min=-reach, max=reach).astype(kind)


def setup_inputs(seed: int = 0) -> dict:
    seeds = jax.random.split(jax.random.key(seed), 17)
    return {
        "tokens": scatter_about(seeds[0], (GRID_ROWS, COL_TOKENS, D), 1.0, 6.0, ((0, 2), (1, 64))),
        "attn_gain": jnp.clip(1.0 + 0.18 * jax.random.normal(seeds[1], (D,), jnp.float32), 0.099609375, 1.8984375).astype(jnp.bfloat16),
        "query_weight": scatter_about(seeds[2], (D, D), D ** -0.5, 0.21875),
        "key_weight": scatter_about(seeds[3], (D, D), D ** -0.5, 0.21875),
        "value_weight": scatter_about(seeds[4], (D, D), D ** -0.5, 0.21875),
        "output_weight": scatter_about(seeds[5], (D, D), (max(D // 128, 2)) ** -0.5, 2.5),
        "ffn_gain": jnp.clip(1.0 + 0.18 * jax.random.normal(seeds[6], (D,), jnp.float32), 0.099609375, 1.8984375).astype(jnp.bfloat16),
        "gate_weight": scatter_about(seeds[7], (D, FF), D ** -0.5, 0.21875),
        "up_weight": scatter_about(seeds[8], (D, FF), D ** -0.5, 0.21875),
        "down_weight": scatter_about(seeds[9], (FF, D), FF ** -0.5, 0.125),
        "relative_table": scatter_about(seeds[10], (BUCKETS, HEADS), 0.5, 3.0),
        "layout_table": scatter_about(seeds[11], (LAYOUT_BUCKETS, HEADS), 0.5, 3.0),
        "cotangent": scatter_about(seeds[12], (GRID_ROWS, COL_TOKENS, D), 1.0, 6.0, ((0, 2), (1, 64))),
        "rel_bucket": draw_rel_bucket(jax.random.fold_in(seeds[16], 71), 0),
        "layout_bucket": plant(jax.random.randint(seeds[14], (GRID_ROWS, COL_TOKENS, WIN), 0, LAYOUT_BUCKETS), jax.random.fold_in(seeds[14], 1), 0, LAYOUT_BUCKETS - 1).astype(jnp.int32),
        "halo_index": draw_halo_index(jax.random.fold_in(seeds[16], 71), 0),
    }


EPS = 1e-06
NEG = -1000000000.0
HIGH = lax.Precision.HIGHEST

@jax.custom_vjp
def low(v):
    return lax.optimization_barrier(v.astype(jnp.bfloat16)).astype(jnp.float32)

@jax.custom_vjp
def low_back(v):
    return v

def low_keep(v):
    return (low(v), None)

def low_pass(kept, grad):
    return (grad,)

def back_keep(v):
    return (v, None)

def back_low(kept, grad):
    return (low(grad),)
low.defvjp(low_keep, low_pass)
low_back.defvjp(back_keep, back_low)

def both_ways(value):
    return low(low_back(value))

def product(left, right):
    return jnp.dot(left, right, precision=HIGH, preferred_element_type=jnp.float32)

def rms_norm(value, gain):
    return value * lax.rsqrt(lax.optimization_barrier(jnp.mean(value * value, axis=-1, keepdims=True)) + EPS) * gain

def windows(grid, halo_index):
    picks = jnp.maximum(halo_index, 0)
    sent = jax.vmap(jax.vmap(lambda block, index: block[index]))(grid, picks)
    row_zero = jnp.zeros_like(sent[:1, :, 0])
    from_lower = jnp.concatenate([row_zero, sent[:-1, :, 0]], axis=0)
    from_upper = jnp.concatenate([sent[1:, :, 1], row_zero], axis=0)
    col_zero = jnp.zeros_like(sent[:, :1, 2])
    from_left = jnp.concatenate([col_zero, sent[:, :-1, 2]], axis=1)
    from_right = jnp.concatenate([sent[:, 1:, 3], col_zero], axis=1)
    return jnp.concatenate([grid, from_lower, from_upper, from_left, from_right], axis=2)

def region_attention(query, keys, values, relative, layout, padded_table, layout_table):
    rows = query.shape[0]
    query_heads = query.reshape(rows, HEADS, HEAD)
    key_heads = keys.reshape(keys.shape[0], HEADS, HEAD)
    value_heads = values.reshape(values.shape[0], HEADS, HEAD)
    raw = jnp.einsum('qhd,khd->hqk', query_heads, key_heads, precision=HIGH) * HEAD ** (-0.5)
    bias = jnp.transpose(padded_table[relative] + layout_table[layout], (2, 0, 1))
    logits = low_back(jnp.where((relative < BUCKETS)[None], raw + bias, NEG))
    probs = jax.nn.softmax(logits, axis=-1)
    attended = jnp.einsum('hqk,khd->qhd', low(probs), value_heads, precision=HIGH)
    return attended.reshape(rows, HEADS * HEAD)

def layer(resid, attn_gain, query_weight, key_weight, value_weight, output_weight, ffn_gain, gate_weight, up_weight, down_weight, relative_table, layout_table, rel_bucket, layout_bucket, halo_index):
    grid_rows = resid.shape[0]
    grid_cols = resid.shape[1] // TOK_DEV
    regions = grid_rows * grid_cols
    flat = resid.reshape(-1, D)
    normed_one = low(rms_norm(flat, attn_gain))
    query = both_ways(product(normed_one, query_weight))
    keys = both_ways(product(normed_one, key_weight))
    values = both_ways(product(normed_one, value_weight))
    key_win = windows(keys.reshape(grid_rows, grid_cols, TOK_DEV, D), halo_index).reshape(regions, WIN, D)
    value_win = windows(values.reshape(grid_rows, grid_cols, TOK_DEV, D), halo_index).reshape(regions, WIN, D)
    padded = jnp.concatenate([relative_table, jnp.zeros((1, HEADS), jnp.float32)], axis=0)

    def region(pieces):
        return region_attention(pieces[0], pieces[1], pieces[2], pieces[3], pieces[4], padded, layout_table)
    attended = lax.map(jax.checkpoint(region), (query.reshape(regions, TOK_DEV, D), key_win, value_win, rel_bucket.reshape(regions, TOK_DEV, WIN), layout_bucket.reshape(regions, TOK_DEV, WIN)))
    attended = both_ways(attended.reshape(-1, D))
    middle = flat + low_back(product(attended, output_weight))
    normed_two = low(rms_norm(middle, ffn_gain))
    gate = low_back(product(normed_two, gate_weight))
    up_part = low_back(product(normed_two, up_weight))
    mixed = low(jax.nn.gelu(gate, approximate=True) * up_part)
    result = middle + low_back(product(mixed, down_weight))
    return result.reshape(resid.shape)

def reference(tokens, attn_gain, query_weight, key_weight, value_weight, output_weight, ffn_gain, gate_weight, up_weight, down_weight, relative_table, layout_table, cotangent, rel_bucket, layout_bucket, halo_index):
    floats = [item.astype(jnp.float32) for item in (tokens, attn_gain, query_weight, key_weight, value_weight, output_weight, ffn_gain, gate_weight, up_weight, down_weight, relative_table, layout_table)]

    def forward(*weights):
        return layer(*weights, rel_bucket, layout_bucket, halo_index)
    result, pullback = jax.vjp(forward, *floats)
    grads = pullback(cotangent.astype(jnp.float32))
    return (result.astype(jnp.bfloat16), grads[0].astype(jnp.bfloat16), grads[1], grads[2], grads[3], grads[4], grads[5], grads[6], grads[7], grads[8], grads[9], grads[10], grads[11])
```

```python
import jax
import jax.numpy as jnp
from jax import lax
from jax.experimental import pallas as pl
from jax.experimental.pallas import tpu as pltpu
from jax.sharding import PartitionSpec as P

BF = jnp.bfloat16
F32 = jnp.float32
EPS = 1e-06
LOG2E = 1.4426950408889634
VMEM_BYTES = 56 * 2**20
REGION = 384
WIDTH = 768
WINDOW = 768
HEADS = 12
HALO = 96
FF = 2048


def params():
    return pltpu.CompilerParams(vmem_limit_bytes=VMEM_BYTES)


def cost(flops, moved, transcendentals=0):
    return pl.CostEstimate(flops=flops, bytes_accessed=moved, transcendentals=transcendentals)


def smem():
    return pl.BlockSpec(memory_space=pltpu.SMEM)


def whole(shape):
    return pl.BlockSpec(shape, lambda *_: (0,) * len(shape))


def mm(a, b):
    return jnp.dot(a, b, preferred_element_type=F32)


def mm_nt(a, b):
    return lax.dot_general(a, b, (((1,), (1,)), ((), ())), preferred_element_type=F32)


def mm_tn(a, b):
    return lax.dot_general(a, b, (((0,), (0,)), ((), ())), preferred_element_type=F32)


def struct(shape, dtype=BF):
    return jax.ShapeDtypeStruct(shape, dtype)


def norm_kernel(place, tokens, gain, index, normed, send_row, send_core, send_chip):
    value = tokens[...].astype(F32)
    inverse = lax.rsqrt(jnp.mean(value * value, axis=-1, keepdims=True) + EPS)
    low = (value * inverse * gain[...].astype(F32)).astype(BF)
    normed[...] = low
    row, odd = place[0], place[1]
    for out, block in ((send_row, row), (send_core, 2 + odd), (send_chip, 3 - odd)):
        picks = index[pl.ds(block, 1), :]
        chosen = lax.broadcasted_iota(jnp.int32, (REGION, HALO), 0) == picks
        out[...] = mm_tn(jnp.where(chosen, 1.0, 0.0).astype(BF), low).astype(BF)


def norm_call(place, tokens, gain, index):
    return pl.pallas_call(
        norm_kernel,
        out_shape=(struct((REGION, WIDTH)),) + (struct((HALO, WIDTH)),) * 3,
        in_specs=[smem()] + [pl.BlockSpec(memory_space=pltpu.VMEM)] * 3,
        out_specs=(pl.BlockSpec(memory_space=pltpu.VMEM),) * 4,
        compiler_params=params(),
        cost_estimate=cost(700_000_000, 2_000_000),
        name="norm_one",
    )(place, tokens, gain, index)


STEP = 2.0**-11
SHIFT = 9000


def bias_kernel(table, relative, layout, out):
    rows = relative.shape[0]

    def look(words, low, bit3, bit4):
        four = [jnp.take_along_axis(words[k], low, axis=0) for k in range(4)]
        return jnp.where(
            bit4, jnp.where(bit3, four[3], four[2]), jnp.where(bit3, four[1], four[0])
        )

    def step(number, carry):
        begin = pl.multiple_of(number * 8, 8)
        for tile in range(WINDOW // 128):
            lanes = slice(tile * 128, tile * 128 + 128)
            rel = relative[pl.ds(begin, 8), lanes]
            lay = layout[pl.ds(begin, 8), lanes]
            rel_low, lay_low = rel & 7, lay & 7
            rel3, rel4 = (rel & 8) != 0, (rel & 16) != 0
            lay3, lay4 = (lay & 8) != 0, (lay & 16) != 0
            masked = rel >= 32
            for pair in range(HEADS // 2):
                words = [table[pair * 8 + k] for k in range(8)]
                word = look(words[:4], rel_low, rel3, rel4) + look(words[4:], lay_low, lay3, lay4)
                high = (word >> 16).astype(F32) * STEP
                low = (word & 0xFFFF).astype(F32) * STEP - 2 * SHIFT * STEP
                out[2 * pair, pl.ds(begin, 8), lanes] = jnp.where(masked, -1.5e9, high)
                out[2 * pair + 1, pl.ds(begin, 8), lanes] = jnp.where(masked, -1.5e9, low)
        return carry

    lax.fori_loop(0, rows // 8, step, 0)


def bias_call(table, relative, layout):
    block = 128
    return pl.pallas_call(
        bias_kernel,
        grid=(REGION // block,),
        out_shape=struct((HEADS, REGION, WINDOW), F32),
        in_specs=[
            whole((48, 8, 128)),
            pl.BlockSpec((block, WINDOW), lambda i: (i, 0)),
            pl.BlockSpec((block, WINDOW), lambda i: (i, 0)),
        ],
        out_specs=pl.BlockSpec((HEADS, block, WINDOW), lambda i: (0, i, 0)),
        compiler_params=params(),
        cost_estimate=cost(100_000_000, 17_000_000),
        name="bias",
    )(table, relative, layout)


def packed_table(relative_table, layout_table):
    def words(table):
        fixed = jnp.round(table.astype(F32) * (LOG2E / STEP)).astype(jnp.int32)
        packed = fixed[:, 0::2] * 65536 + (fixed[:, 1::2] + SHIFT)
        return packed.T.reshape(HEADS // 2, 4, 8)

    both = jnp.concatenate([words(relative_table), words(layout_table)], axis=1)
    return jnp.broadcast_to(both.reshape(48, 8, 1), (48, 8, 128))


def attend_kernel(
    place, normed, from_row, from_core, from_chip, wq, wk, wv, bias,
    window, query, keys, values, probs, attended, scores,
):
    width = wq.shape[1]

    @pl.when(pl.program_id(0) == 0)
    def _():
        row, odd = place[0], place[1]
        window[:REGION] = normed[...]
        window[REGION : REGION + 2 * HALO] = jnp.zeros((2 * HALO, WIDTH), BF)
        window[pl.ds(pl.multiple_of(REGION + HALO - HALO * row, HALO), HALO)] = from_row[...]
        window[pl.ds(pl.multiple_of(REGION + 3 * HALO - HALO * odd, HALO), HALO)] = from_core[...]
        window[pl.ds(pl.multiple_of(REGION + 2 * HALO + HALO * odd, HALO), HALO)] = from_chip[...]

    rows = window[...]
    query[...] = mm(rows[:REGION], wq[...]).astype(BF)
    keys[...] = mm(rows, wk[...]).astype(BF)
    values[...] = mm(rows, wv[...]).astype(BF)
    lane = lax.broadcasted_iota(jnp.int32, (REGION, 128), 1)
    for pair in range(width // 128):
        lanes = slice(pair * 128, pair * 128 + 128)
        halves = []
        for half in range(2):
            head = 2 * pair + half
            mine = (lane < 64) if half == 0 else (lane >= 64)
            one = jnp.where(mine, query[:, lanes], jnp.zeros((), BF))
            slot = head % 2
            scores[slot] = mm_nt(one, keys[:, lanes])
            for begin in range(0, REGION, 32):
                part = slice(begin, begin + 32)
                logits = scores[slot, part] * (0.125 * LOG2E) + bias[head, part]
                highest = jnp.max(logits, axis=-1, keepdims=True)
                powered = jnp.exp2(logits - highest)
                total = jnp.sum(powered, axis=-1, keepdims=True)
                probs[head, part] = (powered * (1.0 / total)).astype(BF)
            halves.append(mm(probs[head], values[:, lanes]))
        attended[:, lanes] = jnp.where(lane < 64, halves[0], halves[1]).astype(BF)


def attend_call(place, normed, from_row, from_core, from_chip, wq, wk, wv, bias, group):
    count = HEADS // group
    width = group * 64
    cols = lambda rows: pl.BlockSpec((rows, width), lambda g: (0, g))
    return pl.pallas_call(
        attend_kernel,
        grid=(count,),
        out_shape=(
            struct((WINDOW, WIDTH)),
            struct((REGION, WIDTH)),
            struct((WINDOW, WIDTH)),
            struct((WINDOW, WIDTH)),
            struct((HEADS, REGION, WINDOW)),
            struct((REGION, WIDTH)),
        ),
        in_specs=[smem(), whole((REGION, WIDTH))]
        + [whole((HALO, WIDTH))] * 3
        + [cols(WIDTH)] * 3
        + [pl.BlockSpec((group, REGION, WINDOW), lambda g: (g, 0, 0))],
        out_specs=(
            whole((WINDOW, WIDTH)),
            cols(REGION),
            cols(WINDOW),
            cols(WINDOW),
            pl.BlockSpec((group, REGION, WINDOW), lambda g: (g, 0, 0)),
            cols(REGION),
        ),
        scratch_shapes=[pltpu.VMEM((2, REGION, WINDOW), F32)],
        compiler_params=params(),
        cost_estimate=cost(3_500_000_000, 30_000_000, 3_600_000),
        name="attend",
    )(place, normed, from_row, from_core, from_chip, wq, wk, wv, bias)


SHARDS = 128
HALF = 64
TILE = 512
PIECE = 16


def tile_of(step, ids):
    core = ids[0] >> 6
    return jnp.where(step < 2, 1 - core, core) * 2 + (step & 1)


def ffn_kernel(
    ids, tokens, attended, wo, gain, cotangent, wg, wu, wd,
    layer_out, d_middle, d_attended, out_grad, gain_grad,
    gate_send, gate_keep, up_send, up_keep, down_send, down_keep,
    middle, normed, normed_t, total_out, total_back,
):
    step = pl.program_id(0)

    def inverse_of(value):
        return lax.rsqrt(jnp.mean(value * value, axis=-1, keepdims=True) + EPS)

    @pl.when(step == 0)
    def _():
        value = tokens[...].astype(F32) + mm(attended[...], wo[...])
        middle[...] = value
        low = (value * inverse_of(value) * gain[...].astype(F32)).astype(BF)
        normed[...] = low
        normed_t[...] = low.T
        total_out[...] = value
        total_back[...] = jnp.zeros_like(total_back)

    low = normed[...]
    grad_out = cotangent[...]
    gate = mm(low, wg[...])
    up_part = mm(low, wu[...])
    cube = gate * gate * gate
    curve = jnp.tanh(0.7978845608 * (gate + 0.044715 * cube))
    half_up = 0.5 * (1.0 + curve)
    act = gate * half_up
    slope = half_up + 0.5 * gate * (1.0 - curve * curve) * (
        0.7978845608 + (3 * 0.7978845608 * 0.044715) * gate * gate
    )
    mixed = (act * up_part).astype(BF)
    d_mixed = mm_nt(grad_out, wd[...])
    d_gate = (d_mixed * up_part * slope).astype(BF)
    d_up = (d_mixed * act).astype(BF)
    total_out[...] += mm(mixed, wd[...])
    total_back[...] += mm_nt(d_gate, wg[...]) + mm_nt(d_up, wu[...])
    gate_grad = mm(normed_t[...], d_gate).astype(BF)
    up_grad = mm(normed_t[...], d_up).astype(BF)
    down_grad = mm_tn(mixed, grad_out).astype(BF)

    def put(gate_out, up_out, down_out):
        flips = [ids[k] & 31 for k in range(3)]
        for piece in range(32):
            col, row = piece // 16, piece % 16
            for third in range(3):
                rows = slice(row * 48 + third * 16, row * 48 + third * 16 + 16)
                cols = slice(col * 256, col * 256 + 256)
                lanes = slice(third * 256, third * 256 + 256)
                gate_out[piece ^ flips[0], :, lanes] = gate_grad[rows, cols]
                up_out[piece ^ flips[1], :, lanes] = up_grad[rows, cols]
            down_out[piece ^ flips[2]] = down_grad[piece * 16 : piece * 16 + 16]

    @pl.when(step < 2)
    def _():
        put(gate_send, up_send, down_send)

    @pl.when(step >= 2)
    def _():
        put(gate_keep, up_keep, down_keep)

    @pl.when(step == 3)
    def _():
        layer_out[...] = total_out[...].astype(BF)
        value = middle[...]
        inverse = inverse_of(value)
        back = total_back[...]
        gain_grad[...] = jnp.sum(back * value * inverse, axis=0, keepdims=True)
        scaled = back * gain[...].astype(F32)
        shared = jnp.mean(scaled * value, axis=-1, keepdims=True)
        whole_grad = (
            grad_out.astype(F32) + inverse * scaled - value * (inverse * inverse * inverse) * shared
        )
        d_middle[...] = whole_grad
        branch = whole_grad.astype(BF)
        out_grad[...] = mm_tn(attended[...], branch).astype(BF)
        d_attended[...] = mm_nt(branch, wo[...]).astype(BF)


def ffn_call(ids, tokens, attended, wo, gain, cotangent, wg, wu, wd):
    block = (32, PIECE, WIDTH)

    def sent(k):
        def index(g, ids):
            return (jnp.where(g < 2, g & 1, 1) ^ ((ids[k] >> 5) & 1), 0, 0)
        return pl.BlockSpec(block, index)

    def kept(k):
        def index(g, ids):
            return (jnp.where(g < 2, 0, g & 1) ^ ((ids[k] >> 5) & 1), 0, 0)
        return pl.BlockSpec(block, index)

    cols = pl.BlockSpec((WIDTH, TILE), lambda g, ids: (0, tile_of(g, ids)))
    half = struct((HALF, PIECE, WIDTH))
    return pl.pallas_call(
        ffn_kernel,
        grid_spec=pltpu.PrefetchScalarGridSpec(
            num_scalar_prefetch=1,
            grid=(FF // TILE,),
            in_specs=[
                whole((REGION, WIDTH)),
                whole((REGION, WIDTH)),
                whole((WIDTH, WIDTH)),
                whole((1, WIDTH)),
                whole((REGION, WIDTH)),
                cols,
                cols,
                pl.BlockSpec((TILE, WIDTH), lambda g, ids: (tile_of(g, ids), 0)),
            ],
            out_specs=[
                whole((REGION, WIDTH)),
                whole((REGION, WIDTH)),
                whole((REGION, WIDTH)),
                whole((WIDTH, WIDTH)),
                whole((1, WIDTH)),
                sent(0), kept(0), sent(1), kept(1), sent(2), kept(2),
            ],
            scratch_shapes=[
                pltpu.VMEM((REGION, WIDTH), F32),
                pltpu.VMEM((REGION, WIDTH), BF),
                pltpu.VMEM((WIDTH, REGION), BF),
                pltpu.VMEM((REGION, WIDTH), F32),
                pltpu.VMEM((REGION, WIDTH), F32),
            ],
        ),
        out_shape=[
            struct((REGION, WIDTH)),
            struct((REGION, WIDTH), F32),
            struct((REGION, WIDTH)),
            struct((WIDTH, WIDTH)),
            struct((1, WIDTH), F32),
            half, half, half, half, half, half,
        ],
        compiler_params=params(),
        cost_estimate=cost(12_300_000_000, 30_000_000, 800_000),
        name="feed_forward",
    )(ids, tokens, attended, wo, gain, cotangent, wg, wu, wd)


GROUP = 6
COLS = GROUP * 64


def back_kernel(
    ids, window, query, keys, values, probs, attended, d_attended, out_grad,
    d_query, d_keys_t, d_values_t, d_logits,
    send_a, keep_a, send_b, keep_b, send_c, keep_c,
    window_t, slopes,
):
    group = pl.program_id(0)

    @pl.when(group == 0)
    def _():
        window_t[...] = window[...].T

    query_t = query[...].T
    d_att_t = d_attended[...].T
    lane = lax.broadcasted_iota(jnp.int32, (REGION, 128), 1)
    for pair in range(GROUP // 2):
        lanes = slice(pair * 128, pair * 128 + 128)
        halves = []
        for half in range(2):
            head = 2 * pair + half
            mine = (lane < 64) if half == 0 else (lane >= 64)
            one = jnp.where(mine, d_attended[:, lanes], jnp.zeros((), BF))
            shared = jnp.sum(
                one.astype(F32) * attended[:, lanes].astype(F32), axis=-1, keepdims=True
            )
            slot = head % 2
            slopes[slot] = mm_nt(one, values[:, lanes])
            for begin in range(0, REGION, 32):
                part = slice(begin, begin + 32)
                grad = probs[head, part].astype(F32) * (slopes[slot, part] - shared[part])
                d_logits[head, part] = grad.astype(BF)
            halves.append(mm(d_logits[head], keys[:, lanes]))
            feats = slice(head * 64, head * 64 + 64)
            d_keys_t[feats] = (mm(query_t[feats], d_logits[head]) * 0.125).astype(BF)
            d_values_t[feats] = mm(d_att_t[feats], probs[head]).astype(BF)
        d_query[:, lanes] = (jnp.where(lane < 64, halves[0], halves[1]) * 0.125).astype(BF)
    grads = (
        mm(window_t[:, :REGION], d_query[...]).astype(BF),
        mm_nt(window_t[...], d_keys_t[...]).astype(BF),
        mm_nt(window_t[...], d_values_t[...]).astype(BF),
        out_grad[...],
    )
    core = ids[0] >> 6
    flips = [ids[k] & 63 for k in range(3)]

    def put(number, outs):
        for row in range(16):
            shard = ((2 * number + group) & 3) * 16 + row
            for third in range(3):
                begin = row * 48 + third * 16
                outs[third][shard ^ flips[third]] = grads[number][begin : begin + 16]

    for number in range(4):
        away = core != number // 2

        @pl.when(away)
        def _():
            put(number, (send_a, send_b, send_c))

        @pl.when(jnp.logical_not(away))
        def _():
            put(number, (keep_a, keep_b, keep_c))


def back_call(ids, window, query, keys, values, probs, attended, d_attended, out_grad):
    cols = lambda rows: pl.BlockSpec((rows, COLS), lambda g: (0, g))
    feats = pl.BlockSpec((COLS, WINDOW), lambda g: (g, 0))
    heads = pl.BlockSpec((GROUP, REGION, WINDOW), lambda g: (g, 0, 0))
    half = struct((HALF, PIECE, COLS))
    return pl.pallas_call(
        back_kernel,
        grid=(HEADS // GROUP,),
        in_specs=[
            smem(), whole((WINDOW, WIDTH)), cols(REGION), cols(WINDOW), cols(WINDOW), heads,
            cols(REGION), cols(REGION), cols(WIDTH),
        ],
        out_specs=[cols(REGION), feats, feats, heads] + [whole((HALF, PIECE, COLS))] * 6,
        out_shape=[
            struct((REGION, WIDTH)),
            struct((WIDTH, WINDOW)),
            struct((WIDTH, WINDOW)),
            struct((HEADS, REGION, WINDOW)),
        ]
        + [half] * 6,
        scratch_shapes=[pltpu.VMEM((WIDTH, WINDOW), BF), pltpu.VMEM((2, REGION, WINDOW), F32)],
        compiler_params=params(),
        cost_estimate=cost(6_000_000_000, 30_000_000),
        name="attend_back",
    )(ids, window, query, keys, values, probs, attended, d_attended, out_grad)


ROWS_A_STEP = 16


def table_kernel(d_logits, relative, layout, out, onehot, total):
    step = pl.program_id(0)

    @pl.when(step == 0)
    def _():
        total[...] = jnp.zeros_like(total)

    bucket = lax.broadcasted_iota(jnp.int32, (32, WINDOW), 0)
    for row in range(ROWS_A_STEP):
        for offset, source in ((0, relative), (32, layout)):
            hit = source[row : row + 1, :] == bucket
            begin = row * 64 + offset
            onehot[begin : begin + 32] = jnp.where(hit, 1.0, 0.0).astype(BF)
    left = d_logits[...].reshape(HEADS * ROWS_A_STEP, WINDOW)
    total[...] += mm_nt(left, onehot[...])

    @pl.when(step == pl.num_programs(0) - 1)
    def _():
        shape = total.shape
        left_row = lax.broadcasted_iota(jnp.int32, shape, 0) % ROWS_A_STEP
        right_row = lax.broadcasted_iota(jnp.int32, shape, 1) // 64
        kept = jnp.where(left_row == right_row, total[...], 0.0)
        by_head = jnp.sum(kept.reshape(HEADS, ROWS_A_STEP, shape[1]), axis=1)
        folded = by_head[:, 0:128]
        for tile in range(1, shape[1] // 128):
            folded = folded + by_head[:, tile * 128 : tile * 128 + 128]
        out[...] = folded[:, :64] + folded[:, 64:]


def table_call(d_logits, relative, layout):
    rows = ROWS_A_STEP
    return pl.pallas_call(
        table_kernel,
        grid=(REGION // rows,),
        in_specs=[
            pl.BlockSpec((HEADS, rows, WINDOW), lambda i: (0, i, 0)),
            pl.BlockSpec((rows, WINDOW), lambda i: (i, 0)),
            pl.BlockSpec((rows, WINDOW), lambda i: (i, 0)),
        ],
        out_specs=whole((HEADS, 64)),
        out_shape=struct((HEADS, 64), F32),
        scratch_shapes=[
            pltpu.VMEM((rows * 64, WINDOW), BF),
            pltpu.VMEM((HEADS * rows, rows * 64), F32),
        ],
        compiler_params=params(),
        cost_estimate=cost(7_000_000_000, 10_000_000),
        name="table_grads",
    )(d_logits, relative, layout)


def window_kernel(place, d_query, d_keys_t, d_values_t, wq, wk, wv, own, for_row, for_core, for_chip, rest):
    full = mm(wk[...], d_keys_t[...]) + mm(wv[...], d_values_t[...])
    own[...] = (full[:, :REGION] + mm_nt(wq[...], d_query[...])).T
    rest[...] = full[:, REGION:].T
    row, odd = place[0], place[1]
    for out, begin in (
        (for_row, HALO - HALO * row),
        (for_core, 3 * HALO - HALO * odd),
        (for_chip, 2 * HALO + HALO * odd),
    ):
        out[...] = rest[pl.ds(pl.multiple_of(begin, HALO), HALO)].astype(BF)


def window_call(place, d_query, d_keys_t, d_values_t, wq, wk, wv):
    return pl.pallas_call(
        window_kernel,
        in_specs=[smem()] + [pl.BlockSpec(memory_space=pltpu.VMEM)] * 6,
        out_specs=[pl.BlockSpec(memory_space=pltpu.VMEM)] * 4,
        out_shape=[struct((REGION, WIDTH), F32)] + [struct((HALO, WIDTH))] * 3,
        scratch_shapes=[pltpu.VMEM((WINDOW - REGION, WIDTH), F32)],
        compiler_params=params(),
        cost_estimate=cost(2_300_000_000, 10_000_000),
        name="window_back",
    )(place, d_query, d_keys_t, d_values_t, wq, wk, wv)


def input_kernel(
    place, tokens, gain, index, own, d_middle, from_row, from_core, from_chip, input_grad, gain_grad
):
    row, odd = place[0], place[1]
    back = own[...]
    for received, block in ((from_row, row), (from_core, 2 + odd), (from_chip, 3 - odd)):
        picks = index[pl.ds(block, 1), :]
        chosen = lax.broadcasted_iota(jnp.int32, (REGION, HALO), 0) == picks
        back = back + mm(jnp.where(chosen, 1.0, 0.0).astype(BF), received[...])
    value = tokens[...].astype(F32)
    inverse = lax.rsqrt(jnp.mean(value * value, axis=-1, keepdims=True) + EPS)
    gain_grad[...] = jnp.sum(back * value * inverse, axis=0, keepdims=True)
    scaled = back * gain[...].astype(F32)
    shared = jnp.mean(scaled * value, axis=-1, keepdims=True)
    input_grad[...] = (
        d_middle[...] + inverse * scaled - value * (inverse * inverse * inverse) * shared
    ).astype(BF)


def input_call(place, tokens, gain, index, own, d_middle, from_row, from_core, from_chip):
    return pl.pallas_call(
        input_kernel,
        in_specs=[smem()] + [pl.BlockSpec(memory_space=pltpu.VMEM)] * 8,
        out_specs=[pl.BlockSpec(memory_space=pltpu.VMEM)] * 2,
        out_shape=[struct((REGION, WIDTH)), struct((1, WIDTH), F32)],
        compiler_params=params(),
        cost_estimate=cost(500_000_000, 6_000_000),
        name="input_back",
    )(place, tokens, gain, index, own, d_middle, from_row, from_core, from_chip)


def ffn_out_kernel(ids, *refs):
    own, other, outs = refs[0:3], refs[3:6], refs[6:9]
    step = pl.program_id(0)

    def put(sources):
        flips = [ids[k] & 31 for k in range(3)]
        for piece in range(32):
            col, row = piece // 16, piece % 16
            for k in range(2):
                block = sources[k][piece ^ flips[k]].astype(F32)
                for third in range(3):
                    begin = row * 48 + third * 16
                    outs[k][begin : begin + 16, col * 256 : col * 256 + 256] = block[
                        :, third * 256 : third * 256 + 256
                    ]
            outs[2][piece * 16 : piece * 16 + 16] = sources[2][piece ^ flips[2]].astype(F32)

    @pl.when(step < 2)
    def _():
        put(own)

    @pl.when(step >= 2)
    def _():
        put(other)


def ffn_out_call(ids, own, other):
    block = (32, PIECE, WIDTH)

    def of_own(k):
        def index(g, ids):
            return (jnp.where(g < 2, g & 1, 1) ^ ((ids[k] >> 5) & 1), 0, 0)
        return pl.BlockSpec(block, index)

    def of_other(k):
        def index(g, ids):
            return (jnp.where(g < 2, 0, g & 1) ^ ((ids[k] >> 5) & 1), 0, 0)
        return pl.BlockSpec(block, index)

    def tile(g, ids):
        core = ids[0] >> 6
        return jnp.where(g < 2, core, 1 - core) * 2 + (g & 1)

    cols = pl.BlockSpec((WIDTH, TILE), lambda g, ids: (0, tile(g, ids)))
    return pl.pallas_call(
        ffn_out_kernel,
        grid_spec=pltpu.PrefetchScalarGridSpec(
            num_scalar_prefetch=1,
            grid=(FF // TILE,),
            in_specs=[of_own(k) for k in range(3)] + [of_other(k) for k in range(3)],
            out_specs=[cols, cols, pl.BlockSpec((TILE, WIDTH), lambda g, ids: (tile(g, ids), 0))],
        ),
        out_shape=[struct((WIDTH, FF), F32), struct((WIDTH, FF), F32), struct((FF, WIDTH), F32)],
        compiler_params=params(),
        cost_estimate=cost(10_000_000, 28_000_000),
        name="feed_forward_out",
    )(ids, *own, *other)


def att_out_kernel(ids, *refs):
    own, other, outs = refs[0:3], refs[3:6], refs[6:10]
    group = pl.program_id(0)
    core = ids[0] >> 6
    flips = [ids[k] & 63 for k in range(3)]

    def put(number, sources):
        for row in range(16):
            shard = ((2 * number + group) & 3) * 16 + row
            for third in range(3):
                begin = row * 48 + third * 16
                outs[number][begin : begin + 16] = sources[third][shard ^ flips[third]].astype(F32)

    for number in range(4):
        mine = core == number // 2

        @pl.when(mine)
        def _():
            put(number, own)

        @pl.when(jnp.logical_not(mine))
        def _():
            put(number, other)


def att_out_call(ids, own, other):
    return pl.pallas_call(
        att_out_kernel,
        grid=(2,),
        in_specs=[smem()] + [whole((HALF, PIECE, COLS))] * 6,
        out_specs=[pl.BlockSpec((WIDTH, COLS), lambda g: (0, g))] * 4,
        out_shape=[struct((WIDTH, WIDTH), F32)] * 4,
        compiler_params=params(),
        cost_estimate=cost(10_000_000, 14_000_000),
        name="attend_out",
    )(ids, *own, *other)


def body(
    tokens, attn_gain, query_weight, key_weight, value_weight, output_weight, ffn_gain, gate_weight,
    up_weight, down_weight, relative_table, layout_table, cotangent, rel_bucket, layout_bucket,
    halo_index,
):
    row = lax.axis_index("row")
    col = lax.axis_index("col")
    place = jnp.stack([row, col % 2]).astype(jnp.int32)
    ids = jnp.zeros((3,), jnp.int32)
    tokens, cotangent = tokens[0], cotangent[0]
    relative, layout = rel_bucket[0], layout_bucket[0]
    index = halo_index[0, 0]
    gain_one, gain_two = attn_gain[None], ffn_gain[None]
    columns = lax.axis_size("col")
    row_pairs = [(0, 1), (1, 0)]
    core_pairs = [(c, c ^ 1) for c in range(columns)]
    chip_pairs = [p for c in range(1, columns - 1, 2) for p in ((c, c + 1), (c + 1, c))]

    def exchange(for_row, for_core, for_chip):
        return (
            lax.ppermute(for_row, "row", row_pairs),
            lax.ppermute(for_core, "col", core_pairs),
            lax.ppermute(for_chip, "col", chip_pairs),
        )

    normed, *sends = norm_call(place, tokens, gain_one, index)
    received = exchange(*sends)
    bias = bias_call(packed_table(relative_table, layout_table), relative, layout)
    window, query, keys, values, probs, attended = attend_call(
        place, normed, *received, query_weight, key_weight, value_weight, bias, 4
    )
    layer_out, d_middle, d_attended, out_grad, gain_two_grad, *ffn_parts = ffn_call(
        ids, tokens, attended, output_weight, gain_two, cotangent, gate_weight, up_weight, down_weight
    )
    d_query, d_keys_t, d_values_t, d_logits, *att_parts = back_call(
        ids, window, query, keys, values, probs, attended, d_attended, out_grad
    )
    tables = table_call(d_logits, relative, layout)
    own, *returns = window_call(
        place, d_query, d_keys_t, d_values_t, query_weight, key_weight, value_weight
    )
    returned = exchange(*returns)
    input_grad, gain_one_grad = input_call(
        place, tokens, gain_one, index, own, d_middle, *returned
    )
    small = jnp.concatenate([gain_one_grad, gain_two_grad, tables.reshape(1, WIDTH)], axis=0)
    high = small.astype(BF)
    low = (small - high.astype(F32)).astype(BF)
    ffn_parts, att_parts, high, low = lax.psum((ffn_parts, att_parts, high, low), ("row", "col"))
    small = high.astype(F32) + low.astype(F32)
    gate_grad, up_grad, down_grad = ffn_out_call(ids, ffn_parts[1::2], ffn_parts[0::2])
    query_grad, key_grad, value_grad, output_grad = att_out_call(
        ids, att_parts[1::2], att_parts[0::2]
    )
    tables = small[2].reshape(HEADS, 64)
    return (
        layer_out[None], input_grad[None], small[0], query_grad, key_grad, value_grad, output_grad,
        small[1], gate_grad, up_grad, down_grad, tables[:, :32].T, tables[:, 32:].T,
    )


def solution(mesh):
    tokens = P("row", "col", None)
    whole_array = P()
    return jax.shard_map(
        body,
        mesh=mesh,
        in_specs=(tokens,) + (whole_array,) * 11 + (tokens,) * 3 + (P("row", "col", None, None),),
        out_specs=(tokens, tokens) + (whole_array,) * 11,
        check_vma=False,
    )
```

```python
import functools

import jax
import jax.numpy as jnp
from jax import lax
from jax.experimental import pallas as pl
from jax.experimental.pallas import tpu as pltpu
from jax.sharding import PartitionSpec as P

BF = jnp.bfloat16
F32 = jnp.float32
EPS = 1e-06
LOG2E = 1.4426950408889634
VMEM_BYTES = 56 * 2**20
REGION = 384
WIDTH = 768
WINDOW = 768
HEADS = 12
HALO = 96
FF = 2048


def params():
    return pltpu.CompilerParams(vmem_limit_bytes=VMEM_BYTES)


def cost(flops, moved, transcendentals=0):
    return pl.CostEstimate(flops=flops, bytes_accessed=moved, transcendentals=transcendentals)


def smem():
    return pl.BlockSpec(memory_space=pltpu.SMEM)


def whole(shape):
    return pl.BlockSpec(shape, lambda *_: (0,) * len(shape))


def mm(a, b):
    return jnp.dot(a, b, preferred_element_type=F32)


def mm_nt(a, b):
    return lax.dot_general(a, b, (((1,), (1,)), ((), ())), preferred_element_type=F32)


def mm_tn(a, b):
    return lax.dot_general(a, b, (((0,), (0,)), ((), ())), preferred_element_type=F32)


def struct(shape, dtype=BF):
    return jax.ShapeDtypeStruct(shape, dtype)


def norm_kernel(place, tokens, gain, index, normed, send_row, send_core, send_chip):
    value = tokens[...].astype(F32)
    inverse = lax.rsqrt(jnp.mean(value * value, axis=-1, keepdims=True) + EPS)
    low = (value * inverse * gain[...].astype(F32)).astype(BF)
    normed[...] = low
    row, odd = place[0], place[1]
    for out, block in ((send_row, row), (send_core, 2 + odd), (send_chip, 3 - odd)):
        picks = index[pl.ds(block, 1), :]
        chosen = lax.broadcasted_iota(jnp.int32, (REGION, HALO), 0) == picks
        out[...] = mm_tn(jnp.where(chosen, 1.0, 0.0).astype(BF), low).astype(BF)


def norm_call(place, tokens, gain, index):
    return pl.pallas_call(
        norm_kernel,
        out_shape=(struct((REGION, WIDTH)),) + (struct((HALO, WIDTH)),) * 3,
        in_specs=[smem()] + [pl.BlockSpec(memory_space=pltpu.VMEM)] * 3,
        out_specs=(pl.BlockSpec(memory_space=pltpu.VMEM),) * 4,
        compiler_params=params(),
        cost_estimate=cost(700_000_000, 2_000_000),
        name="norm_one",
    )(place, tokens, gain, index)


STEP = 2.0**-11
SHIFT = 9000


def bias_kernel(table, relative, layout, out):
    rows = relative.shape[0]

    def look(words, low, bit3, bit4):
        four = [jnp.take_along_axis(words[k], low, axis=0) for k in range(4)]
        return jnp.where(
            bit4, jnp.where(bit3, four[3], four[2]), jnp.where(bit3, four[1], four[0])
        )

    def step(number, carry):
        begin = pl.multiple_of(number * 8, 8)
        for tile in range(WINDOW // 128):
            lanes = slice(tile * 128, tile * 128 + 128)
            rel = relative[pl.ds(begin, 8), lanes]
            lay = layout[pl.ds(begin, 8), lanes]
            rel_low, lay_low = rel & 7, lay & 7
            rel3, rel4 = (rel & 8) != 0, (rel & 16) != 0
            lay3, lay4 = (lay & 8) != 0, (lay & 16) != 0
            masked = rel >= 32
            for pair in range(HEADS // 2):
                words = [table[pair * 8 + k] for k in range(8)]
                word = look(words[:4], rel_low, rel3, rel4) + look(words[4:], lay_low, lay3, lay4)
                high = (word >> 16).astype(F32) * STEP
                low = (word & 0xFFFF).astype(F32) * STEP - 2 * SHIFT * STEP
                out[2 * pair, pl.ds(begin, 8), lanes] = jnp.where(masked, -1.5e9, high)
                out[2 * pair + 1, pl.ds(begin, 8), lanes] = jnp.where(masked, -1.5e9, low)
        return carry

    lax.fori_loop(0, rows // 8, step, 0)


def bias_call(table, relative, layout):
    block = 128
    return pl.pallas_call(
        bias_kernel,
        grid=(REGION // block,),
        out_shape=struct((HEADS, REGION, WINDOW), F32),
        in_specs=[
            whole((48, 8, 128)),
            pl.BlockSpec((block, WINDOW), lambda i: (i, 0)),
            pl.BlockSpec((block, WINDOW), lambda i: (i, 0)),
        ],
        out_specs=pl.BlockSpec((HEADS, block, WINDOW), lambda i: (0, i, 0)),
        compiler_params=params(),
        cost_estimate=cost(100_000_000, 17_000_000),
        name="bias",
    )(table, relative, layout)


def packed_table(relative_table, layout_table):
    def words(table):
        fixed = jnp.round(table.astype(F32) * (LOG2E / STEP)).astype(jnp.int32)
        packed = fixed[:, 0::2] * 65536 + (fixed[:, 1::2] + SHIFT)
        return packed.T.reshape(HEADS // 2, 4, 8)

    both = jnp.concatenate([words(relative_table), words(layout_table)], axis=1)
    return jnp.broadcast_to(both.reshape(48, 8, 1), (48, 8, 128))


def attend_kernel(
    place, normed, from_row, from_core, from_chip, wq, wk, wv, bias,
    window, query, keys, values, probs, attended, scores,
):
    width = wq.shape[1]

    @pl.when(pl.program_id(0) == 0)
    def _():
        row, odd = place[0], place[1]
        window[:REGION] = normed[...]
        window[REGION : REGION + 2 * HALO] = jnp.zeros((2 * HALO, WIDTH), BF)
        window[pl.ds(pl.multiple_of(REGION + HALO - HALO * row, HALO), HALO)] = from_row[...]
        window[pl.ds(pl.multiple_of(REGION + 3 * HALO - HALO * odd, HALO), HALO)] = from_core[...]
        window[pl.ds(pl.multiple_of(REGION + 2 * HALO + HALO * odd, HALO), HALO)] = from_chip[...]

    rows = window[...]
    query[...] = mm(rows[:REGION], wq[...]).astype(BF)
    keys[...] = mm(rows, wk[...]).astype(BF)
    values[...] = mm(rows, wv[...]).astype(BF)
    lane = lax.broadcasted_iota(jnp.int32, (REGION, 128), 1)
    for pair in range(width // 128):
        lanes = slice(pair * 128, pair * 128 + 128)
        halves = []
        for half in range(2):
            head = 2 * pair + half
            mine = (lane < 64) if half == 0 else (lane >= 64)
            one = jnp.where(mine, query[:, lanes], jnp.zeros((), BF))
            slot = head % 2
            scores[slot] = mm_nt(one, keys[:, lanes])
            for begin in range(0, REGION, 32):
                part = slice(begin, begin + 32)
                logits = scores[slot, part] * (0.125 * LOG2E) + bias[head, part]
                highest = jnp.max(logits, axis=-1, keepdims=True)
                powered = jnp.exp2(logits - highest)
                total = jnp.sum(powered, axis=-1, keepdims=True)
                probs[head, part] = (powered * (1.0 / total)).astype(BF)
            halves.append(mm(probs[head], values[:, lanes]))
        attended[:, lanes] = jnp.where(lane < 64, halves[0], halves[1]).astype(BF)


def attend_call(place, normed, from_row, from_core, from_chip, wq, wk, wv, bias, group):
    count = HEADS // group
    width = group * 64
    cols = lambda rows: pl.BlockSpec((rows, width), lambda g: (0, g))
    return pl.pallas_call(
        attend_kernel,
        grid=(count,),
        out_shape=(
            struct((WINDOW, WIDTH)),
            struct((REGION, WIDTH)),
            struct((WINDOW, WIDTH)),
            struct((WINDOW, WIDTH)),
            struct((HEADS, REGION, WINDOW)),
            struct((REGION, WIDTH)),
        ),
        in_specs=[smem(), whole((REGION, WIDTH))]
        + [whole((HALO, WIDTH))] * 3
        + [cols(WIDTH)] * 3
        + [pl.BlockSpec((group, REGION, WINDOW), lambda g: (g, 0, 0))],
        out_specs=(
            whole((WINDOW, WIDTH)),
            cols(REGION),
            cols(WINDOW),
            cols(WINDOW),
            pl.BlockSpec((group, REGION, WINDOW), lambda g: (g, 0, 0)),
            cols(REGION),
        ),
        scratch_shapes=[pltpu.VMEM((2, REGION, WINDOW), F32)],
        compiler_params=params(),
        cost_estimate=cost(3_500_000_000, 30_000_000, 3_600_000),
        name="attend",
    )(place, normed, from_row, from_core, from_chip, wq, wk, wv, bias)


SHARDS = 128
HALF = 64
TILE = 512
PIECE = 16
MERGED = 1152


def inverse_of(value):
    return lax.rsqrt(jnp.mean(value * value, axis=-1, keepdims=True) + EPS)


def ffn_kernel(
    ids, tokens, attended, wo, gain, cotangent, wg, wu, wd,
    layer_out, d_middle, d_attended, d_branch, gain_grad, normed,
    mixed_send, mixed_keep, gate_send, gate_keep, up_send, up_keep,
    middle, total_out, total_back,
):
    step = pl.program_id(0)

    @pl.when(step == 0)
    def _():
        value = tokens[...].astype(F32) + mm(attended[...], wo[...])
        middle[...] = value
        normed[...] = (value * inverse_of(value) * gain[...].astype(F32)).astype(BF)
        total_out[...] = value
        total_back[...] = jnp.zeros_like(total_back)

    low = normed[...]
    gate = mm(low, wg[...])
    up_part = mm(low, wu[...])
    d_mixed = mm_nt(cotangent[...], wd[...])
    curve = jnp.tanh(gate * (0.7978845608 + (0.7978845608 * 0.044715) * (gate * gate)))
    half_up = 0.5 * (1.0 + curve)
    act = gate * half_up
    slope = half_up + 0.5 * gate * (1.0 - curve * curve) * (
        0.7978845608 + (3 * 0.7978845608 * 0.044715) * gate * gate
    )
    mixed = (act * up_part).astype(BF)
    d_gate = (d_mixed * up_part * slope).astype(BF)
    d_up = (d_mixed * act).astype(BF)
    total_out[...] += mm(mixed, wd[...])
    total_back[...] += mm_nt(d_gate, wg[...]) + mm_nt(d_up, wu[...])

    @pl.when(step < 2)
    def _():
        mixed_send[...] = mixed
        gate_send[...] = d_gate
        up_send[...] = d_up

    @pl.when(step >= 2)
    def _():
        mixed_keep[...] = mixed
        gate_keep[...] = d_gate
        up_keep[...] = d_up

    @pl.when(step == 3)
    def _():
        layer_out[...] = total_out[...].astype(BF)
        value = middle[...]
        inverse = inverse_of(value)
        back = total_back[...]
        gain_grad[...] = jnp.sum(back * value * inverse, axis=0, keepdims=True)
        scaled = back * gain[...].astype(F32)
        shared = jnp.mean(scaled * value, axis=-1, keepdims=True)
        whole_grad = (
            cotangent[...].astype(F32)
            + inverse * scaled
            - value * (inverse * inverse * inverse) * shared
        )
        d_middle[...] = whole_grad
        branch = whole_grad.astype(BF)
        d_branch[...] = branch
        d_attended[...] = mm_nt(branch, wo[...]).astype(BF)


def ffn_call(ids, tokens, attended, wo, gain, cotangent, wg, wu, wd):
    def tile(g, ids):
        return jnp.where(g < 2, 1 - ids[0], ids[0]) * 2 + (g & 1)

    cols = pl.BlockSpec((WIDTH, TILE), lambda g, ids: (0, tile(g, ids)))
    sent = pl.BlockSpec((REGION, TILE), lambda g, ids: (0, jnp.minimum(g, 1)))
    kept = pl.BlockSpec((REGION, TILE), lambda g, ids: (0, jnp.maximum(g - 2, 0)))
    full = whole((REGION, WIDTH))
    return pl.pallas_call(
        ffn_kernel,
        grid_spec=pltpu.PrefetchScalarGridSpec(
            num_scalar_prefetch=1,
            grid=(FF // TILE,),
            in_specs=[
                full, full, whole((WIDTH, WIDTH)), whole((1, WIDTH)), full, cols, cols,
                pl.BlockSpec((TILE, WIDTH), lambda g, ids: (tile(g, ids), 0)),
            ],
            out_specs=[full, full, full, full, whole((1, WIDTH)), full]
            + [sent, kept, sent, kept, sent, kept],
            scratch_shapes=[pltpu.VMEM((REGION, WIDTH), F32)] * 3,
        ),
        out_shape=[
            struct((REGION, WIDTH)),
            struct((REGION, WIDTH), F32),
            struct((REGION, WIDTH)),
            struct((REGION, WIDTH)),
            struct((1, WIDTH), F32),
            struct((REGION, WIDTH)),
        ]
        + [struct((REGION, FF // 2))] * 6,
        compiler_params=params(),
        cost_estimate=cost(8_000_000_000, 20_000_000, 800_000),
        name="feed_forward",
    )(ids, tokens, attended, wo, gain, cotangent, wg, wu, wd)


def grads_kernel(
    ids, normed, normed_other, cotangent, cotangent_other,
    mixed, mixed_other, d_gate, d_gate_other, d_up, d_up_other, *refs
):
    att, att_other = refs[0:3], refs[3:6]
    sends, keeps = refs[6:9], refs[9:12]
    normed_t, grad_out, right = refs[12:]
    step = pl.program_id(0)

    @pl.when(step == 0)
    def _():
        normed_t[:, :REGION] = normed[...].T
        normed_t[:, REGION:] = normed_other[...].T
        grad_out[:REGION] = cotangent[...]
        grad_out[REGION:] = cotangent_other[...]
        for k in range(3):
            for place in range(32):
                out = keeps[k] if place < 16 else sends[k]
                for group in range(2):
                    both = att[k][place, group].astype(F32) + att_other[k][place, group].astype(F32)
                    out[(place % 16) * 2 + group, :, WIDTH:] = both.astype(BF)

    for number, (mine, theirs) in enumerate(
        ((d_gate, d_gate_other), (d_up, d_up_other), (mixed, mixed_other))
    ):
        right[number, :REGION] = mine[...]
        right[number, REGION:] = theirs[...]
    gate_grad = mm(normed_t[...], right[0]).astype(BF)
    up_grad = mm(normed_t[...], right[1]).astype(BF)
    down_grad = mm_tn(right[2], grad_out[...]).astype(BF)

    def put_cols(out, grad, flip):
        for piece in range(32):
            col, row = piece // 16, piece % 16
            for third in range(3):
                begin = row * 48 + third * 16
                out[piece ^ flip, :, third * 256 : third * 256 + 256] = grad[
                    begin : begin + 16, col * 256 : col * 256 + 256
                ]

    def put_rows(out, grad, flip):
        for piece in range(32):
            out[piece ^ flip, :, :WIDTH] = grad[piece * 16 : piece * 16 + 16]

    for k, (put, grad) in enumerate(
        ((put_cols, gate_grad), (put_cols, up_grad), (put_rows, down_grad))
    ):
        place = ids[1 + k]
        away = ((place >> 5) & 1) != step

        @pl.when(away)
        def _():
            put(sends[k], grad, place & 31)

        @pl.when(jnp.logical_not(away))
        def _():
            put(keeps[k], grad, place & 31)


def grads_call(ids, normed, normed_other, cotangent, cotangent_other, pairs, att, att_other):
    full = whole((REGION, WIDTH))
    cols = pl.BlockSpec((REGION, TILE), lambda g, ids: (0, g))
    merged = (32, PIECE, MERGED)
    return pl.pallas_call(
        grads_kernel,
        grid_spec=pltpu.PrefetchScalarGridSpec(
            num_scalar_prefetch=1,
            grid=(2,),
            in_specs=[full] * 4 + [cols] * 6 + [whole((32, 2, PIECE, COLS))] * 6,
            out_specs=[whole(merged)] * 6,
            scratch_shapes=[
                pltpu.VMEM((WIDTH, 2 * REGION), BF),
                pltpu.VMEM((2 * REGION, WIDTH), BF),
                pltpu.VMEM((3, 2 * REGION, TILE), BF),
            ],
        ),
        out_shape=[struct(merged)] * 6,
        compiler_params=params(),
        cost_estimate=cost(3_700_000_000, 16_000_000),
        name="feed_forward_grads",
    )(ids, normed, normed_other, cotangent, cotangent_other, *pairs, *att, *att_other)


GROUP = 6
COLS = GROUP * 64


def back_kernel(
    ids, window, query, keys, values, probs, attended, d_attended, attended_all, d_branch, *refs
):
    d_query, d_keys_t, d_values_t, d_logits = refs[:4]
    sends, keeps = refs[4:7], refs[7:10]
    window_t, slopes, attended_t = refs[10:]

    @pl.when(pl.program_id(0) == 0)
    def _():
        window_t[...] = window[...].T
        attended_t[...] = attended_all[...].T

    query_t = query[...].T
    d_att_t = d_attended[...].T
    lane = lax.broadcasted_iota(jnp.int32, (REGION, 128), 1)
    for pair in range(GROUP // 2):
        lanes = slice(pair * 128, pair * 128 + 128)
        halves = []
        for half in range(2):
            head = 2 * pair + half
            mine = (lane < 64) if half == 0 else (lane >= 64)
            one = jnp.where(mine, d_attended[:, lanes], jnp.zeros((), BF))
            shared = jnp.sum(
                one.astype(F32) * attended[:, lanes].astype(F32), axis=-1, keepdims=True
            )
            slot = head % 2
            slopes[slot] = mm_nt(one, values[:, lanes])
            for begin in range(0, REGION, 32):
                part = slice(begin, begin + 32)
                grad = probs[head, part].astype(F32) * (slopes[slot, part] - shared[part])
                d_logits[head, part] = grad.astype(BF)
            halves.append(mm(d_logits[head], keys[:, lanes]))
            feats = slice(head * 64, head * 64 + 64)
            d_keys_t[feats] = (mm(query_t[feats], d_logits[head]) * 0.125).astype(BF)
            d_values_t[feats] = mm(d_att_t[feats], probs[head]).astype(BF)
        d_query[:, lanes] = (jnp.where(lane < 64, halves[0], halves[1]) * 0.125).astype(BF)
    grads = (
        mm(window_t[:, :REGION], d_query[...]).astype(BF),
        mm_nt(window_t[...], d_keys_t[...]).astype(BF),
        mm_nt(window_t[...], d_values_t[...]).astype(BF),
        mm(attended_t[...], d_branch[...]).astype(BF),
    )

    def put(numbers, outs, first):
        for third in range(3):
            flip = (ids[first + third] >> 1) & 31
            for number in numbers:
                for row in range(16):
                    shard = (number & 1) * 16 + row
                    begin = row * 48 + third * 16
                    outs[third][shard ^ flip, 0] = grads[number][begin : begin + 16]

    first = ids[0] == 0

    @pl.when(first)
    def _():
        put((0, 1), keeps, 1)
        put((2, 3), sends, 4)

    @pl.when(jnp.logical_not(first))
    def _():
        put((0, 1), sends, 4)
        put((2, 3), keeps, 1)


def back_call(ids, window, query, keys, values, probs, attended, d_attended, d_branch):
    cols = lambda rows: pl.BlockSpec((rows, COLS), lambda g: (0, g))
    feats = pl.BlockSpec((COLS, WINDOW), lambda g: (g, 0))
    heads = pl.BlockSpec((GROUP, REGION, WINDOW), lambda g: (g, 0, 0))
    return pl.pallas_call(
        back_kernel,
        grid=(2,),
        in_specs=[
            smem(), whole((WINDOW, WIDTH)), cols(REGION), cols(WINDOW), cols(WINDOW), heads,
            cols(REGION), cols(REGION), whole((REGION, WIDTH)), cols(REGION),
        ],
        out_specs=[cols(REGION), feats, feats, heads]
        + [pl.BlockSpec((32, 1, PIECE, COLS), lambda g: (0, g, 0, 0))] * 6,
        out_shape=[
            struct((REGION, WIDTH)),
            struct((WIDTH, WINDOW)),
            struct((WIDTH, WINDOW)),
            struct((HEADS, REGION, WINDOW)),
        ]
        + [struct((32, 2, PIECE, COLS))] * 6,
        scratch_shapes=[
            pltpu.VMEM((WIDTH, WINDOW), BF),
            pltpu.VMEM((2, REGION, WINDOW), F32),
            pltpu.VMEM((WIDTH, REGION), BF),
        ],
        compiler_params=params(),
        cost_estimate=cost(6_000_000_000, 30_000_000),
        name="attend_back",
    )(ids, window, query, keys, values, probs, attended, d_attended, attended, d_branch)


ROWS = 16
BLOCKS = 4


def table_kernel(d_logits, relative, layout, out, onehot, total):
    step = pl.program_id(0)

    @pl.when(step == 0)
    def _():
        total[...] = jnp.zeros_like(total)

    bucket = lax.broadcasted_iota(jnp.int32, (32, WINDOW), 0)
    added = []
    for block in range(BLOCKS):
        for row in range(ROWS):
            for offset, source in ((0, relative), (32, layout)):
                at = block * ROWS + row
                hit = source[at : at + 1, :] == bucket
                begin = row * 64 + offset
                onehot[block, begin : begin + 32] = jnp.where(hit, 1.0, 0.0).astype(BF)
        rows = slice(block * ROWS, block * ROWS + ROWS)
        left = d_logits[:, rows, :].reshape(HEADS * ROWS, WINDOW)
        added.append(mm_nt(left, onehot[block]))
    total[...] += (added[0] + added[1]) + (added[2] + added[3])

    @pl.when(step == pl.num_programs(0) - 1)
    def _():
        shape = total.shape
        left_row = lax.broadcasted_iota(jnp.int32, shape, 0) % ROWS
        right_row = lax.broadcasted_iota(jnp.int32, shape, 1) // 64
        kept = jnp.where(left_row == right_row, total[...], 0.0)
        by_head = jnp.sum(kept.reshape(HEADS, ROWS, shape[1]), axis=1)
        folded = by_head[:, 0:128]
        for tile in range(1, shape[1] // 128):
            folded = folded + by_head[:, tile * 128 : tile * 128 + 128]
        out[...] = folded[:, :64] + folded[:, 64:]


def table_call(third, d_logits, relative, layout):
    rows = ROWS * BLOCKS
    steps = REGION // 3 // rows
    heads = pl.BlockSpec((HEADS, rows, WINDOW), lambda i: (0, third * steps + i, 0))
    buckets = pl.BlockSpec((rows, WINDOW), lambda i: (third * steps + i, 0))
    return pl.pallas_call(
        table_kernel,
        grid=(steps,),
        in_specs=[heads, buckets, buckets],
        out_specs=whole((HEADS, 64)),
        out_shape=struct((HEADS, 64), F32),
        scratch_shapes=[
            pltpu.VMEM((BLOCKS, ROWS * 64, WINDOW), BF),
            pltpu.VMEM((HEADS * ROWS, ROWS * 64), F32),
        ],
        compiler_params=params(),
        cost_estimate=cost(2_500_000_000, 4_000_000),
        name="table_grads",
    )(d_logits, relative, layout)


def small_kernel(one, two, three, gain_grad, out):
    out[...] = jnp.zeros_like(out)

    def put(value, rows, lanes):
        high = value.astype(BF)
        out[0, rows, lanes] = high
        out[1, rows, lanes] = (value - high.astype(F32)).astype(BF)

    tables = jnp.concatenate([one[...] + two[...] + three[...], jnp.zeros((4, 64), F32)])
    put(jnp.concatenate([tables, jnp.zeros((16, 64), F32)], axis=1), slice(0, 16), slice(0, 128))
    row = lax.broadcasted_iota(jnp.int32, (16, WIDTH), 0)
    put(jnp.where(row == 12, gain_grad[...], 0.0), slice(0, 16), slice(128, 128 + WIDTH))


def small_call(one, two, three, gain_grad):
    return pl.pallas_call(
        small_kernel,
        in_specs=[pl.BlockSpec(memory_space=pltpu.VMEM)] * 4,
        out_specs=pl.BlockSpec(memory_space=pltpu.VMEM),
        out_shape=struct((2, PIECE, MERGED)),
        compiler_params=params(),
        name="small_sums",
    )(one, two, three, gain_grad)


def window_kernel(place, d_query, d_keys_t, d_values_t, wq, wk, wv, own, for_row, for_core, for_chip, rest):
    full = mm(wk[...], d_keys_t[...]) + mm(wv[...], d_values_t[...])
    own[...] = (full[:, :REGION] + mm_nt(wq[...], d_query[...])).T
    rest[...] = full[:, REGION:].T
    row, odd = place[0], place[1]
    for out, begin in (
        (for_row, HALO - HALO * row),
        (for_core, 3 * HALO - HALO * odd),
        (for_chip, 2 * HALO + HALO * odd),
    ):
        out[...] = rest[pl.ds(pl.multiple_of(begin, HALO), HALO)].astype(BF)


def window_call(place, d_query, d_keys_t, d_values_t, wq, wk, wv):
    return pl.pallas_call(
        window_kernel,
        in_specs=[smem()] + [pl.BlockSpec(memory_space=pltpu.VMEM)] * 6,
        out_specs=[pl.BlockSpec(memory_space=pltpu.VMEM)] * 4,
        out_shape=[struct((REGION, WIDTH), F32)] + [struct((HALO, WIDTH))] * 3,
        scratch_shapes=[pltpu.VMEM((WINDOW - REGION, WIDTH), F32)],
        compiler_params=params(),
        cost_estimate=cost(2_300_000_000, 10_000_000),
        name="window_back",
    )(place, d_query, d_keys_t, d_values_t, wq, wk, wv)


def input_kernel(
    place, tokens, gain, index, own, d_middle, from_row, from_core, from_chip, input_grad
):
    row, odd = place[0], place[1]
    back = own[...]
    for received, block in ((from_row, row), (from_core, 2 + odd), (from_chip, 3 - odd)):
        picks = index[pl.ds(block, 1), :]
        chosen = lax.broadcasted_iota(jnp.int32, (REGION, HALO), 0) == picks
        back = back + mm(jnp.where(chosen, 1.0, 0.0).astype(BF), received[...])
    value = tokens[...].astype(F32)
    inverse = lax.rsqrt(jnp.mean(value * value, axis=-1, keepdims=True) + EPS)
    scaled = back * gain[...].astype(F32)
    shared = jnp.mean(scaled * value, axis=-1, keepdims=True)
    input_grad[...] = (
        d_middle[...] + inverse * scaled - value * (inverse * inverse * inverse) * shared
    ).astype(BF)


def input_call(place, tokens, gain, index, own, d_middle, from_row, from_core, from_chip):
    return pl.pallas_call(
        input_kernel,
        in_specs=[smem()] + [pl.BlockSpec(memory_space=pltpu.VMEM)] * 8,
        out_specs=pl.BlockSpec(memory_space=pltpu.VMEM),
        out_shape=struct((REGION, WIDTH)),
        compiler_params=params(),
        cost_estimate=cost(500_000_000, 6_000_000),
        name="input_back",
    )(place, tokens, gain, index, own, d_middle, from_row, from_core, from_chip)


def put_ffn(ids, sources, side, gate, up, down):
    flips = [ids[1 + 3 * side + k] & 31 for k in range(3)]
    for piece in range(32):
        col, row = piece // 16, piece % 16
        for k, out in ((0, gate), (1, up)):
            block = sources[k][piece ^ flips[k]].astype(F32)
            for third in range(3):
                begin = row * 48 + third * 16
                out[begin : begin + 16, col * 256 : col * 256 + 256] = block[
                    :, third * 256 : third * 256 + 256
                ]
        down[piece * 16 : piece * 16 + 16] = sources[2][piece ^ flips[2]].astype(F32)


def ffn_specs(far):
    def tile(side, k, ids):
        half = jnp.where(side == 0, ids[0], 1 - ids[0])
        return half * 2 + (((ids[1 + 3 * side + k] >> 5) & 1) ^ far)

    return [
        pl.BlockSpec((WIDTH, TILE), lambda g, ids: (0, tile(jnp.minimum(g, 1), 0, ids))),
        pl.BlockSpec((WIDTH, TILE), lambda g, ids: (0, tile(jnp.minimum(g, 1), 1, ids))),
        pl.BlockSpec((TILE, WIDTH), lambda g, ids: (tile(jnp.minimum(g, 1), 2, ids), 0)),
    ]


FFN_OUT = [struct((WIDTH, FF), F32), struct((WIDTH, FF), F32), struct((FF, WIDTH), F32)]


def near_kernel(ids, *refs):
    own, other, outs = refs[0:3], refs[3:6], refs[6:9]
    side = pl.program_id(0)

    @pl.when(side == 0)
    def _():
        put_ffn(ids, own, side, *outs)

    @pl.when(side == 1)
    def _():
        put_ffn(ids, other, side, *outs)


def near_call(ids, own, other):
    part = pl.BlockSpec((32, PIECE, WIDTH), lambda g, ids: (0, 0, 0))
    return pl.pallas_call(
        near_kernel,
        grid_spec=pltpu.PrefetchScalarGridSpec(
            num_scalar_prefetch=1, grid=(2,), in_specs=[part] * 6, out_specs=ffn_specs(0)
        ),
        out_shape=FFN_OUT,
        compiler_params=params(),
        cost_estimate=cost(10_000_000, 14_000_000),
        name="outputs_near",
    )(ids, *own, *other)


def far_kernel(ids, wq, wk, wv, gain, *refs):
    parts = [refs[4 * k : 4 * k + 4] for k in range(3)]
    gate, up, down, query, key, value, output, gain_grad = refs[15:23]
    ffn, att, total, ffn_sem, att_sem = refs[23:]
    step = pl.program_id(0)

    def far_copy(side, k):
        return pltpu.make_async_copy(
            parts[k][2 * side + 1].at[:, :, :WIDTH], ffn.at[side, k], ffn_sem.at[side]
        )

    def att_copies():
        return [
            pltpu.make_async_copy(parts[k][c].at[:, :, WIDTH:], att.at[k, c], att_sem)
            for k in range(3)
            for c in range(4)
        ]

    @pl.when(step == 0)
    def _():
        for side in range(2):
            for k in range(3):
                far_copy(side, k).start()
        for copy in att_copies():
            copy.start()

    for side in range(2):

        @pl.when(step == side)
        def _():
            for k in range(3):
                far_copy(side, k).wait()
            put_ffn(ids, [ffn.at[side, k] for k in range(3)], side, gate, up, down)

    @pl.when(step == 2)
    def _():
        for copy in att_copies():
            copy.wait()

    @pl.when(step >= 2)
    def _():
        group = step - 2
        for number, out in enumerate((query, key, value, output)):
            side = jnp.where(ids[0] == number // 2, 0, 1)
            for third in range(3):
                flip = ids[1 + 3 * side + third] >> 1
                for row in range(16):
                    place = (((number & 1) * 16 + row) ^ flip) & 31
                    begin = row * 48 + third * 16
                    out[begin : begin + 16] = att[
                        third, 2 * side + (place >> 4), (place & 15) * 2 + group
                    ].astype(F32)
        product = query[...] * wq[...].astype(F32) + key[...] * wk[...].astype(F32)
        product = product + value[...] * wv[...].astype(F32)
        sums = lax.dot_general(
            jnp.ones((8, COLS), F32), product, (((1,), (1,)), ((), ())),
            precision=lax.Precision.HIGHEST, preferred_element_type=F32,
        )

        @pl.when(step == 2)
        def _():
            total[...] = sums

        @pl.when(step == 3)
        def _():
            gain_grad[...] = (total[0:1] + sums[0:1]) / gain[...].astype(F32)


def far_call(ids, wq, wk, wv, gain, parts, nears):
    part = pl.BlockSpec((WIDTH, COLS), lambda g, ids: (0, jnp.maximum(g - 2, 0)))
    anywhere = pl.BlockSpec(memory_space=pl.ANY)
    return pl.pallas_call(
        far_kernel,
        grid_spec=pltpu.PrefetchScalarGridSpec(
            num_scalar_prefetch=1,
            grid=(4,),
            in_specs=[part] * 3 + [whole((1, WIDTH))] + [anywhere] * 15,
            out_specs=ffn_specs(1) + [part] * 4 + [whole((1, WIDTH))],
            scratch_shapes=[
                pltpu.VMEM((2, 3, 32, PIECE, WIDTH), BF),
                pltpu.VMEM((3, 4, 32, PIECE, COLS), BF),
                pltpu.VMEM((8, WIDTH), F32),
                pltpu.SemaphoreType.DMA((2,)),
                pltpu.SemaphoreType.DMA,
            ],
        ),
        out_shape=FFN_OUT + [struct((WIDTH, WIDTH), F32)] * 4 + [struct((1, WIDTH), F32)],
        input_output_aliases={17: 0, 18: 1, 19: 2},
        compiler_params=params(),
        cost_estimate=cost(10_000_000, 30_000_000),
        name="outputs_far",
    )(ids, wq, wk, wv, gain, *parts[0], *parts[1], *parts[2], *nears)


AXES = ("row", "col")
OTHER_PAIRS = {0: 3, 3: 0, 1: 2, 2: 1}


def ring_pairs(axis, bit):
    pairs = []
    for chip in range(64):
        for core in range(2):
            spot = [chip // 16, chip // 4 % 4, chip % 4]
            first = (bit + core) % 2 == 0
            spot[axis] = spot[axis] ^ 1 if first else OTHER_PAIRS[spot[axis]]
            partner = (spot[0] * 4 + spot[1]) * 4 + spot[2]
            pairs.append((2 * chip + core, 2 * partner + core))
    return pairs


CORE_PAIRS = [(d, d ^ 1) for d in range(SHARDS)]


def shard_ids(row, col):
    spots = (2 * row + (col >> 5), (col >> 3) & 3, (col >> 1) & 3)
    near = [((v + 1) >> 1) & 1 for v in spots]
    far = [v >> 1 for v in spots]
    core = col & 1
    ids = [core]
    for side in (core, 1 - core):
        first = [jnp.where(side == 1, f, n) for n, f in zip(near, far)]
        second = [jnp.where(side == 1, n, f) for n, f in zip(near, far)]
        for chunk in range(3):
            turned = [first[(chunk + turn) % 3] for turn in range(3)]
            ids.append(turned[0] * 32 + turned[1] * 16 + turned[2] * 8 + second[chunk] * 4)
    return jnp.stack(ids).astype(jnp.int32)


def swap(value, pairs):
    return lax.ppermute(value, AXES, pairs)


def added(mine, received):
    return (mine.astype(F32) + received.astype(F32)).astype(BF)


def after(first, *values):
    held = lax.optimization_barrier((first, values))[1]
    return held[0] if len(values) == 1 else held


def words_sum(one, two):
    value = (one[0].astype(F32) + one[1].astype(F32)) + (two[0].astype(F32) + two[1].astype(F32))
    high = value.astype(BF)
    return jnp.stack([high, (value - high.astype(F32)).astype(BF)])


def body(
    tokens, attn_gain, query_weight, key_weight, value_weight, output_weight, ffn_gain, gate_weight,
    up_weight, down_weight, relative_table, layout_table, cotangent, rel_bucket, layout_bucket,
    halo_index,
):
    row = lax.axis_index("row")
    col = lax.axis_index("col")
    place = jnp.stack([row, col % 2]).astype(jnp.int32)
    ids = shard_ids(row, col)
    tokens, cotangent = tokens[0], cotangent[0]
    relative, layout = rel_bucket[0], layout_bucket[0]
    index = halo_index[0, 0]
    gain_one, gain_two = attn_gain[None], ffn_gain[None]
    columns = lax.axis_size("col")
    row_pairs = [(0, 1), (1, 0)]
    core_pairs = [(c, c ^ 1) for c in range(columns)]
    chip_pairs = [p for c in range(1, columns - 1, 2) for p in ((c, c + 1), (c + 1, c))]

    def exchange(for_row, for_core, for_chip):
        return (
            lax.ppermute(for_row, "row", row_pairs),
            lax.ppermute(for_core, "col", core_pairs),
            lax.ppermute(for_chip, "col", chip_pairs),
        )

    def ring(axis, bit):
        return ring_pairs(axis, bit)

    normed, *sends = norm_call(place, tokens, gain_one, index)
    received = exchange(*sends)
    bias = bias_call(packed_table(relative_table, layout_table), relative, layout)
    cotangent_other = swap(cotangent, CORE_PAIRS)
    window, query, keys, values, probs, attended = attend_call(
        place, normed, *received, query_weight, key_weight, value_weight, bias, 4
    )
    (
        layer_out, d_middle, d_attended, d_branch, gain_two_grad, normed_two, *halves
    ) = ffn_call(
        ids, tokens, attended, output_weight, gain_two, cotangent, gate_weight, up_weight, down_weight
    )
    mixed_send, mixed, gate_send, d_gate, up_send, d_up = halves
    normed_two_other, mixed_other, d_gate_other, d_up_other = [
        swap(v, CORE_PAIRS) for v in (normed_two, mixed_send, gate_send, up_send)
    ]
    d_query, d_keys_t, d_values_t, d_logits, *att = back_call(
        ids, window, query, keys, values, probs, attended, d_attended, d_branch
    )
    att_other = [swap(v, CORE_PAIRS) for v in att[:3]]
    normed_two = after(d_query, normed_two)
    merged = grads_call(
        ids, normed_two, normed_two_other, cotangent, cotangent_other,
        (mixed, mixed_other, d_gate, d_gate_other, d_up, d_up_other), att[3:], att_other,
    )
    sent, kept = list(merged[:3]), list(merged[3:])

    last = sent[2]
    got = [swap(sent[k], ring(k, 0)) for k in range(3)]
    tables = []
    for third in range(2):
        tables.append(table_call(third, d_logits, after(last, relative), layout))
        last = tables[-1]

    def halve(turn, last):
        half = kept[0].shape[0] // 2
        for k in range(3):
            new = after(last, got[k])
            sent = added(kept[k][half:], new[half:])
            kept[k] = added(kept[k][:half], new[:half])
            pairs = ring((k + turn) % 3, 0) if turn < 3 else ring(k, 1)
            got[k] = swap(sent, pairs)
            last = kept[k]
        return last

    last = halve(1, last)
    tables.append(table_call(2, d_logits, after(last, relative), layout))
    last = halve(2, tables[-1])
    small = small_call(*tables, after(last, gain_two_grad))
    last = halve(3, small)
    for turn in (1, 2):
        for k in range(3):
            new = after(last, got[k])
            if k == 0 and turn == 2:
                small = words_sum(small, new[-2:])
                new = new[:-2]
            kept[k] = added(kept[k], new)
            last = kept[k]
            out = jnp.concatenate([kept[k], small]) if k == 0 else kept[k]
            got[k] = swap(out, ring((k + turn) % 3, 1))
    for k in range(3):
        new = after(last, got[k])
        if k == 0:
            small = words_sum(small, new[-2:])
            new = new[:-2]
        kept[k] = added(kept[k], new)
        last = kept[k]
        out = jnp.concatenate([kept[k], small]) if k == 0 else kept[k]
        got[k] = swap(out, ring(k, 1))
    for turn in (2, 1, 0):
        for k in range(3):
            new = after(last, got[k])
            if k == 0:
                small = words_sum(small, new[-2:])
                new = new[:-2]
                out = jnp.concatenate([kept[k], new, small])
                kept[k] = out[:-2]
            else:
                out = kept[k] = jnp.concatenate([kept[k], new])
            last = out
            got[k] = swap(out, ring((k + turn) % 3, 0))
        if turn == 1:
            own, *returns = window_call(
                place, d_query, d_keys_t, d_values_t, query_weight, key_weight,
                after(last, value_weight),
            )
            last = own
    near_other = [swap(kept[k], CORE_PAIRS) for k in range(3)]
    returned = exchange(*returns)
    nears = near_call(ids, kept, near_other)
    input_grad = input_call(
        place, after(nears[0], tokens), gain_one, index, own, d_middle, *returned
    )
    last = input_grad
    far, far_other = [], []
    for k in range(3):
        new = after(last, got[k])
        if k == 0:
            small = words_sum(small, new[-2:])
            new = new[:-2]
            got_small = swap(small, CORE_PAIRS)
        far.append(new)
        far_other.append(swap(new, CORE_PAIRS))
    small = words_sum(small, got_small)
    small = small[0].astype(F32) + small[1].astype(F32)
    parts = [(kept[k], far[k], near_other[k], far_other[k]) for k in range(3)]
    gate_grad, up_grad, down_grad, query_grad, key_grad, value_grad, output_grad, gain_one_grad = (
        far_call(ids, query_weight, key_weight, value_weight, gain_one, parts, nears)
    )
    return (
        layer_out[None], input_grad[None], gain_one_grad[0], query_grad, key_grad, value_grad,
        output_grad, small[12, 128 : 128 + WIDTH], gate_grad, up_grad, down_grad,
        small[:HEADS, :32].T, small[:HEADS, 32:64].T,
    )


def solution(mesh):
    tokens = P("row", "col", None)
    whole_array = P()
    return jax.shard_map(
        body,
        mesh=mesh,
        in_specs=(tokens,) + (whole_array,) * 11 + (tokens,) * 3 + (P("row", "col", None, None),),
        out_specs=(tokens, tokens) + (whole_array,) * 11,
        check_vma=False,
    )
```

```python
import functools

import jax
import jax.numpy as jnp
from jax import lax
from jax.experimental import pallas as pl
from jax.experimental.pallas import tpu as pltpu
from jax.sharding import PartitionSpec as P

BF = jnp.bfloat16
F32 = jnp.float32
EPS = 1e-06
LOG2E = 1.4426950408889634
REGION = 384
WIDTH = 768
WINDOW = 768
HEADS = 12
HALO = 96
FF = 2048


def params(mib):
    return pltpu.CompilerParams(vmem_limit_bytes=mib * 2**20)


def cost(flops, moved, transcendentals=0):
    return pl.CostEstimate(flops=flops, bytes_accessed=moved, transcendentals=transcendentals)


def smem():
    return pl.BlockSpec(memory_space=pltpu.SMEM)


def whole(shape):
    return pl.BlockSpec(shape, lambda *_: (0,) * len(shape))


def mm(a, b):
    return jnp.dot(a, b, preferred_element_type=F32)


def mm_nt(a, b):
    return lax.dot_general(a, b, (((1,), (1,)), ((), ())), preferred_element_type=F32)


def mm_tn(a, b):
    return lax.dot_general(a, b, (((0,), (0,)), ((), ())), preferred_element_type=F32)


def struct(shape, dtype=BF):
    return jax.ShapeDtypeStruct(shape, dtype)


def norm_kernel(tokens, gain, index, normed, send_row, send_core, send_chip, ids):
    value = tokens[...].astype(F32)
    inverse = lax.rsqrt(jnp.mean(value * value, axis=-1, keepdims=True) + EPS)
    low = (value * inverse * gain[...].reshape(1, WIDTH).astype(F32)).astype(BF)
    normed[...] = low
    row, col = lax.axis_index("row"), lax.axis_index("col")
    core = col & 1
    for out, block in ((send_row, row), (send_core, 2 + core), (send_chip, 3 - core)):
        picks = index[pl.ds(block, 1), :]
        chosen = lax.broadcasted_iota(jnp.int32, (REGION, HALO), 0) == picks
        out[...] = mm_tn(jnp.where(chosen, 1.0, 0.0).astype(BF), low).astype(BF)
    spots = (2 * row + (col >> 5), (col >> 3) & 3, (col >> 1) & 3)
    near = [((v + 1) >> 1) & 1 for v in spots]
    far = [v >> 1 for v in spots]
    ids[0] = core
    ids[7] = row
    for other in range(2):
        side = core ^ other
        first = [jnp.where(side == 1, f, n) for n, f in zip(near, far)]
        second = [jnp.where(side == 1, n, f) for n, f in zip(near, far)]
        for chunk in range(3):
            turned = [first[(chunk + turn) % 3] for turn in range(3)]
            ids[1 + 3 * other + chunk] = (
                turned[0] * 32 + turned[1] * 16 + turned[2] * 8 + second[0] * 4 + second[1] * 2
            )


def norm_call(tokens, gain, index):
    vmem = pl.BlockSpec(memory_space=pltpu.VMEM)
    return pl.pallas_call(
        norm_kernel,
        out_shape=(struct((REGION, WIDTH)),) + (struct((HALO, WIDTH)),) * 3 + (struct((8,), jnp.int32),),
        in_specs=[vmem] * 3,
        out_specs=(vmem,) * 4 + (smem(),),
        compiler_params=params(56),
        cost_estimate=cost(700_000_000, 2_000_000),
        name="norm_one",
    )(tokens, gain, index)


STEP = 2.0**-11
SHIFT = 9000


def bias_kernel(relative_table, layout_table, relative, layout, out, table):
    rows = relative.shape[0]

    @pl.when(pl.program_id(0) == 0)
    def _():
        for number, source in enumerate((relative_table, layout_table)):
            values = jnp.round(source[...].astype(F32) * (LOG2E / STEP))
            fixed = jnp.concatenate([values, jnp.zeros((4, 32), F32)]).T.astype(jnp.int32)
            for pair in range(HEADS // 2):
                high = jnp.broadcast_to(fixed[:, 2 * pair : 2 * pair + 1], (32, 128))
                low = jnp.broadcast_to(fixed[:, 2 * pair + 1 : 2 * pair + 2], (32, 128))
                table[pair, number] = high * 65536 + (low + SHIFT)

    def look(words, low, bit3, bit4):
        four = [jnp.take_along_axis(words[8 * k : 8 * k + 8], low, axis=0) for k in range(4)]
        return jnp.where(
            bit4, jnp.where(bit3, four[3], four[2]), jnp.where(bit3, four[1], four[0])
        )

    def step(number, carry):
        begin = pl.multiple_of(number * 8, 8)
        for tile in range(WINDOW // 128):
            lanes = slice(tile * 128, tile * 128 + 128)
            rel = relative[pl.ds(begin, 8), lanes]
            lay = layout[pl.ds(begin, 8), lanes]
            rel_low, lay_low = rel & 7, lay & 7
            rel3, rel4 = (rel & 8) != 0, (rel & 16) != 0
            lay3, lay4 = (lay & 8) != 0, (lay & 16) != 0
            masked = rel >= 32
            for pair in range(HEADS // 2):
                word = look(table[pair, 0], rel_low, rel3, rel4)
                word = word + look(table[pair, 1], lay_low, lay3, lay4)
                high = (word >> 16).astype(F32) * STEP
                low = (word & 0xFFFF).astype(F32) * STEP - 2 * SHIFT * STEP
                out[2 * pair, pl.ds(begin, 8), lanes] = jnp.where(masked, -1.5e9, high)
                out[2 * pair + 1, pl.ds(begin, 8), lanes] = jnp.where(masked, -1.5e9, low)
        return carry

    lax.fori_loop(0, rows // 8, step, 0)


def bias_call(relative_table, layout_table, relative, layout):
    block = 128
    buckets = pl.BlockSpec((block, WINDOW), lambda i: (i, 0))
    return pl.pallas_call(
        bias_kernel,
        grid=(REGION // block,),
        out_shape=struct((HEADS, REGION, WINDOW), F32),
        in_specs=[whole((HEADS, 32)), whole((HEADS, 32)), buckets, buckets],
        out_specs=pl.BlockSpec((HEADS, block, WINDOW), lambda i: (0, i, 0)),
        scratch_shapes=[pltpu.VMEM((HEADS // 2, 2, 32, 128), jnp.int32)],
        compiler_params=params(56),
        cost_estimate=cost(100_000_000, 17_000_000),
        name="bias",
    )(relative_table.T, layout_table.T, relative, layout)


def attend_kernel(
    place, normed, from_row, from_core, from_chip, wq, wk, wv, bias,
    window, query, keys, values, probs, attended, scores,
):
    width = wq.shape[1]

    @pl.when(pl.program_id(0) == 0)
    def _():
        row, odd = place[7], place[0]
        window[:REGION] = normed[...]
        window[REGION : REGION + 2 * HALO] = jnp.zeros((2 * HALO, WIDTH), BF)
        window[pl.ds(pl.multiple_of(REGION + HALO - HALO * row, HALO), HALO)] = from_row[...]
        window[pl.ds(pl.multiple_of(REGION + 3 * HALO - HALO * odd, HALO), HALO)] = from_core[...]
        window[pl.ds(pl.multiple_of(REGION + 2 * HALO + HALO * odd, HALO), HALO)] = from_chip[...]

    rows = window[...]
    query[...] = mm(rows[:REGION], wq[...]).astype(BF)
    keys[...] = mm(rows, wk[...]).astype(BF)
    values[...] = mm(rows, wv[...]).astype(BF)
    lane = lax.broadcasted_iota(jnp.int32, (REGION, 128), 1)
    for pair in range(width // 128):
        lanes = slice(pair * 128, pair * 128 + 128)
        halves = []
        for half in range(2):
            head = 2 * pair + half
            mine = (lane < 64) if half == 0 else (lane >= 64)
            one = jnp.where(mine, query[:, lanes], jnp.zeros((), BF))
            slot = head % 2
            scores[slot] = mm_nt(one, keys[:, lanes])
            for begin in range(0, REGION, 32):
                part = slice(begin, begin + 32)
                logits = scores[slot, part] * (0.125 * LOG2E) + bias[head, part]
                highest = jnp.max(logits, axis=-1, keepdims=True)
                powered = jnp.exp2(logits - highest)
                total = jnp.sum(powered, axis=-1, keepdims=True)
                probs[head, part] = (powered * (1.0 / total)).astype(BF)
            halves.append(mm(probs[head], values[:, lanes]))
        attended[:, lanes] = jnp.where(lane < 64, halves[0], halves[1]).astype(BF)


def attend_call(place, normed, from_row, from_core, from_chip, wq, wk, wv, bias, group):
    count = HEADS // group
    width = group * 64
    cols = lambda rows: pl.BlockSpec((rows, width), lambda g: (0, g))
    return pl.pallas_call(
        attend_kernel,
        grid=(count,),
        out_shape=(
            struct((WINDOW, WIDTH)),
            struct((REGION, WIDTH)),
            struct((WINDOW, WIDTH)),
            struct((WINDOW, WIDTH)),
            struct((HEADS, REGION, WINDOW)),
            struct((REGION, WIDTH)),
        ),
        in_specs=[smem(), whole((REGION, WIDTH))]
        + [whole((HALO, WIDTH))] * 3
        + [cols(WIDTH)] * 3
        + [pl.BlockSpec((group, REGION, WINDOW), lambda g: (g, 0, 0))],
        out_specs=(
            whole((WINDOW, WIDTH)),
            cols(REGION),
            cols(WINDOW),
            cols(WINDOW),
            pl.BlockSpec((group, REGION, WINDOW), lambda g: (g, 0, 0)),
            cols(REGION),
        ),
        scratch_shapes=[pltpu.VMEM((2, REGION, WINDOW), F32)],
        compiler_params=params(56),
        cost_estimate=cost(3_500_000_000, 30_000_000, 3_600_000),
        name="attend",
    )(place, normed, from_row, from_core, from_chip, wq, wk, wv, bias)


SHARDS = 128
HALF = 64
TILE = 512
PIECE = 16
MERGED = 1152


def inverse_of(value):
    return lax.rsqrt(jnp.mean(value * value, axis=-1, keepdims=True) + EPS)


def ffn_kernel(
    ids, tokens, attended, wo, gain, cotangent, wg, wu, wd,
    layer_out, d_middle, d_attended, d_branch, gain_grad, normed,
    mixed_send, mixed_keep, gate_send, gate_keep, up_send, up_keep,
    middle, total_out, total_back,
):
    step = pl.program_id(0)

    @pl.when(step == 0)
    def _():
        value = tokens[...].astype(F32) + mm(attended[...], wo[...])
        middle[...] = value
        normed[...] = (value * inverse_of(value) * gain[...].reshape(1, WIDTH).astype(F32)).astype(BF)
        total_out[...] = value
        total_back[...] = jnp.zeros_like(total_back)

    low = normed[...]
    gate = mm(low, wg[...])
    up_part = mm(low, wu[...])
    d_mixed = mm_nt(cotangent[...], wd[...])
    curve = jnp.tanh(gate * (0.7978845608 + (0.7978845608 * 0.044715) * (gate * gate)))
    half_up = 0.5 * (1.0 + curve)
    act = gate * half_up
    slope = half_up + 0.5 * gate * (1.0 - curve * curve) * (
        0.7978845608 + (3 * 0.7978845608 * 0.044715) * gate * gate
    )
    mixed = (act * up_part).astype(BF)
    d_gate = (d_mixed * up_part * slope).astype(BF)
    d_up = (d_mixed * act).astype(BF)
    total_out[...] += mm(mixed, wd[...])
    total_back[...] += mm_nt(d_gate, wg[...]) + mm_nt(d_up, wu[...])

    @pl.when(step < 2)
    def _():
        mixed_send[...] = mixed
        gate_send[...] = d_gate
        up_send[...] = d_up

    @pl.when(step >= 2)
    def _():
        mixed_keep[...] = mixed
        gate_keep[...] = d_gate
        up_keep[...] = d_up

    @pl.when(step == 3)
    def _():
        layer_out[...] = total_out[...].astype(BF)
        value = middle[...]
        inverse = inverse_of(value)
        back = total_back[...]
        gain_grad[...] = jnp.sum(back * value * inverse, axis=0, keepdims=True)
        scaled = back * gain[...].reshape(1, WIDTH).astype(F32)
        shared = jnp.mean(scaled * value, axis=-1, keepdims=True)
        whole_grad = (
            cotangent[...].astype(F32)
            + inverse * scaled
            - value * (inverse * inverse * inverse) * shared
        )
        d_middle[...] = whole_grad
        branch = whole_grad.astype(BF)
        d_branch[...] = branch
        d_attended[...] = mm_nt(branch, wo[...]).astype(BF)


def ffn_call(ids, tokens, attended, wo, gain, cotangent, wg, wu, wd):
    def tile(g, ids):
        return jnp.where(g < 2, 1 - ids[0], ids[0]) * 2 + (g & 1)

    cols = pl.BlockSpec((WIDTH, TILE), lambda g, ids: (0, tile(g, ids)))
    sent = pl.BlockSpec((REGION, TILE), lambda g, ids: (0, jnp.minimum(g, 1)))
    kept = pl.BlockSpec((REGION, TILE), lambda g, ids: (0, jnp.maximum(g - 2, 0)))
    full = whole((REGION, WIDTH))
    return pl.pallas_call(
        ffn_kernel,
        grid_spec=pltpu.PrefetchScalarGridSpec(
            num_scalar_prefetch=1,
            grid=(FF // TILE,),
            in_specs=[
                full, full, whole((WIDTH, WIDTH)), whole((WIDTH,)), full, cols, cols,
                pl.BlockSpec((TILE, WIDTH), lambda g, ids: (tile(g, ids), 0)),
            ],
            out_specs=[full, full, full, full, whole((1, WIDTH)), full]
            + [sent, kept, sent, kept, sent, kept],
            scratch_shapes=[pltpu.VMEM((REGION, WIDTH), F32)] * 3,
        ),
        out_shape=[
            struct((REGION, WIDTH)),
            struct((REGION, WIDTH), F32),
            struct((REGION, WIDTH)),
            struct((REGION, WIDTH)),
            struct((1, WIDTH), F32),
            struct((REGION, WIDTH)),
        ]
        + [struct((REGION, FF // 2))] * 6,
        compiler_params=params(56),
        cost_estimate=cost(8_000_000_000, 20_000_000, 800_000),
        name="feed_forward",
    )(ids, tokens, attended, wo, gain, cotangent, wg, wu, wd)


def grads_kernel(ids, *refs):
    normeds, cots = refs[0:2], refs[2:4]
    hidden = (refs[4:6], refs[6:8], refs[8:10])
    att, att_other, outs = refs[10:13], refs[13:16], refs[16:22]
    normed, grad_out, right, atts, pieces, normed_t, in_sem, out_sem = refs[22:]

    def pair_in(sources, target, number):
        return [
            pltpu.make_async_copy(
                sources[k], target.at[k * REGION : k * REGION + REGION], in_sem.at[number]
            )
            for k in range(2)
        ]

    copies = [pair_in(normeds, normed, 0)]
    copies += [pair_in(hidden[k], right.at[k], 1 + k) for k in range(3)]
    copies += [pair_in(cots, grad_out, 4)]
    copies += [
        [
            pltpu.make_async_copy(source[k], atts.at[side, k], in_sem.at[5 + k])
            for side, source in enumerate((att, att_other))
        ]
        for k in range(3)
    ]
    for number in (0, 1, 5, 2, 6, 4, 3, 7):
        for copy in copies[number]:
            copy.start()

    def wait(number):
        for copy in copies[number]:
            copy.wait()

    def out_copy(k, side):
        return pltpu.make_async_copy(pieces.at[k, side], outs[3 * side + k], out_sem.at[2 * k + side])

    wait(0)
    normed_t[...] = normed[...].T
    for k in range(3):
        wait(1 + k)
        if k == 2:
            wait(4)
        place = ids[1 + k]
        top, flip = (place >> 5) & 1, place & 31
        for tile in range(2):
            cols = slice(tile * TILE, tile * TILE + TILE)
            if k < 2:
                grad = mm(normed_t[...], right[k, :, cols]).astype(BF)
            else:
                grad = mm_tn(right[k, :, cols], grad_out[...]).astype(BF)
            side = top ^ (1 - tile)
            for piece in range(32):
                col, row = piece // 16, piece % 16
                if k == 2:
                    pieces[k, side, piece ^ flip, :, :WIDTH] = grad[piece * 16 : piece * 16 + 16]
                    continue
                for third in range(3):
                    begin = row * 48 + third * 16
                    lanes = slice(third * 256, third * 256 + 256)
                    pieces[k, side, piece ^ flip, :, lanes] = grad[
                        begin : begin + 16, col * 256 : col * 256 + 256
                    ]
        wait(5 + k)
        for spot in range(32):
            for group in range(2):
                both = atts[0, k, spot, group].astype(F32) + atts[1, k, spot, group].astype(F32)
                pieces[k, 1 - spot // 16, (spot % 16) * 2 + group, :, WIDTH:] = both.astype(BF)
        for side in range(2):
            out_copy(k, side).start()
    for k in range(3):
        for side in range(2):
            out_copy(k, side).wait()


def grads_call(ids, normed, normed_other, cotangent, cotangent_other, pairs, att, att_other):
    merged = (32, PIECE, MERGED)
    anywhere = pl.BlockSpec(memory_space=pl.ANY)
    return pl.pallas_call(
        grads_kernel,
        in_specs=[smem()] + [anywhere] * 16,
        out_specs=[anywhere] * 6,
        scratch_shapes=[
            pltpu.VMEM((2 * REGION, WIDTH), BF),
            pltpu.VMEM((2 * REGION, WIDTH), BF),
            pltpu.VMEM((3, 2 * REGION, FF // 2), BF),
            pltpu.VMEM((2, 3, 32, 2, PIECE, COLS), BF),
            pltpu.VMEM((3, 2, 32, PIECE, MERGED), BF),
            pltpu.VMEM((WIDTH, 2 * REGION), BF),
            pltpu.SemaphoreType.DMA((8,)),
            pltpu.SemaphoreType.DMA((6,)),
        ],
        out_shape=[struct(merged)] * 6,
        compiler_params=params(56),
        cost_estimate=cost(3_700_000_000, 16_000_000),
        name="feed_forward_grads",
    )(ids, normed, normed_other, cotangent, cotangent_other, *pairs, *att, *att_other)


GROUP = 6
COLS = GROUP * 64


def back_kernel(
    ids, window, query, keys, values, probs, attended, d_attended, attended_all, d_branch, *refs
):
    d_query, d_keys_t, d_values_t, d_logits = refs[:4]
    sends, keeps = refs[4:7], refs[7:10]
    window_t, slopes, attended_t = refs[10:]

    @pl.when(pl.program_id(0) == 0)
    def _():
        window_t[...] = window[...].T
        attended_t[...] = attended_all[...].T

    query_t = query[...].T
    d_att_t = d_attended[...].T
    lane = lax.broadcasted_iota(jnp.int32, (REGION, 128), 1)
    for pair in range(GROUP // 2):
        lanes = slice(pair * 128, pair * 128 + 128)
        halves = []
        for half in range(2):
            head = 2 * pair + half
            mine = (lane < 64) if half == 0 else (lane >= 64)
            one = jnp.where(mine, d_attended[:, lanes], jnp.zeros((), BF))
            shared = jnp.sum(
                one.astype(F32) * attended[:, lanes].astype(F32), axis=-1, keepdims=True
            )
            slot = head % 2
            slopes[slot] = mm_nt(one, values[:, lanes])
            for begin in range(0, REGION, 32):
                part = slice(begin, begin + 32)
                grad = probs[head, part].astype(F32) * (slopes[slot, part] - shared[part])
                d_logits[head, part] = grad.astype(BF)
            halves.append(mm(d_logits[head], keys[:, lanes]))
            feats = slice(head * 64, head * 64 + 64)
            d_keys_t[feats] = (mm(query_t[feats], d_logits[head]) * 0.125).astype(BF)
            d_values_t[feats] = mm(d_att_t[feats], probs[head]).astype(BF)
        d_query[:, lanes] = (jnp.where(lane < 64, halves[0], halves[1]) * 0.125).astype(BF)
    grads = (
        mm(window_t[:, :REGION], d_query[...]).astype(BF),
        mm_nt(window_t[...], d_keys_t[...]).astype(BF),
        mm_nt(window_t[...], d_values_t[...]).astype(BF),
        mm(attended_t[...], d_branch[...]).astype(BF),
    )

    def put(numbers, outs, first):
        for third in range(3):
            flip = (ids[first + third] >> 1) & 31
            for number in numbers:
                for row in range(16):
                    shard = (number & 1) * 16 + row
                    begin = third * 256 + row * 16
                    outs[third][shard ^ flip, 0] = grads[number][begin : begin + 16]

    first = ids[0] == 0

    @pl.when(first)
    def _():
        put((0, 1), keeps, 1)
        put((2, 3), sends, 4)

    @pl.when(jnp.logical_not(first))
    def _():
        put((0, 1), sends, 4)
        put((2, 3), keeps, 1)


def back_call(ids, window, query, keys, values, probs, attended, d_attended, d_branch):
    cols = lambda rows: pl.BlockSpec((rows, COLS), lambda g: (0, g))
    feats = pl.BlockSpec((COLS, WINDOW), lambda g: (g, 0))
    heads = pl.BlockSpec((GROUP, REGION, WINDOW), lambda g: (g, 0, 0))
    return pl.pallas_call(
        back_kernel,
        grid=(2,),
        in_specs=[
            smem(), whole((WINDOW, WIDTH)), cols(REGION), cols(WINDOW), cols(WINDOW), heads,
            cols(REGION), cols(REGION), whole((REGION, WIDTH)), cols(REGION),
        ],
        out_specs=[cols(REGION), feats, feats, heads]
        + [pl.BlockSpec((32, 1, PIECE, COLS), lambda g: (0, g, 0, 0))] * 6,
        out_shape=[
            struct((REGION, WIDTH)),
            struct((WIDTH, WINDOW)),
            struct((WIDTH, WINDOW)),
            struct((HEADS, REGION, WINDOW)),
        ]
        + [struct((32, 2, PIECE, COLS))] * 6,
        scratch_shapes=[
            pltpu.VMEM((WIDTH, WINDOW), BF),
            pltpu.VMEM((2, REGION, WINDOW), F32),
            pltpu.VMEM((WIDTH, REGION), BF),
        ],
        compiler_params=params(56),
        cost_estimate=cost(6_000_000_000, 30_000_000),
        name="attend_back",
    )(ids, window, query, keys, values, probs, attended, d_attended, attended, d_branch)


ROWS = 16
BLOCKS = 4


def table_kernel(d_logits, relative, layout, out, onehot, total):
    step = pl.program_id(0)

    @pl.when(step == 0)
    def _():
        total[...] = jnp.zeros_like(total)

    bucket = lax.broadcasted_iota(jnp.int32, (32, WINDOW), 0)
    added = []
    for block in range(BLOCKS):
        for row in range(ROWS):
            for offset, source in ((0, relative), (32, layout)):
                at = block * ROWS + row
                hit = source[at : at + 1, :] == bucket
                begin = row * 64 + offset
                onehot[block, begin : begin + 32] = jnp.where(hit, 1.0, 0.0).astype(BF)
        rows = slice(block * ROWS, block * ROWS + ROWS)
        left = d_logits[:, rows, :].reshape(HEADS * ROWS, WINDOW)
        added.append(mm_nt(left, onehot[block]))
    total[...] += (added[0] + added[1]) + (added[2] + added[3])

    @pl.when(step == pl.num_programs(0) - 1)
    def _():
        shape = total.shape
        left_row = lax.broadcasted_iota(jnp.int32, shape, 0) % ROWS
        right_row = lax.broadcasted_iota(jnp.int32, shape, 1) // 64
        kept = jnp.where(left_row == right_row, total[...], 0.0)
        by_head = jnp.sum(kept.reshape(HEADS, ROWS, shape[1]), axis=1)
        folded = by_head[:, 0:128]
        for tile in range(1, shape[1] // 128):
            folded = folded + by_head[:, tile * 128 : tile * 128 + 128]
        out[...] = folded[:, :64] + folded[:, 64:]


def table_call(third, d_logits, relative, layout):
    rows = ROWS * BLOCKS
    steps = REGION // 3 // rows
    heads = pl.BlockSpec((HEADS, rows, WINDOW), lambda i: (0, third * steps + i, 0))
    buckets = pl.BlockSpec((rows, WINDOW), lambda i: (third * steps + i, 0))
    return pl.pallas_call(
        table_kernel,
        grid=(steps,),
        in_specs=[heads, buckets, buckets],
        out_specs=whole((HEADS, 64)),
        out_shape=struct((HEADS, 64), F32),
        scratch_shapes=[
            pltpu.VMEM((BLOCKS, ROWS * 64, WINDOW), BF),
            pltpu.VMEM((HEADS * ROWS, ROWS * 64), F32),
        ],
        compiler_params=params(20),
        cost_estimate=cost(2_500_000_000, 4_000_000),
        name="table_grads",
    )(d_logits, relative, layout)


def small_kernel(one, two, three, gain_grad, out):
    out[...] = jnp.zeros_like(out)

    def put(value, rows, lanes):
        high = value.astype(BF)
        out[0, rows, lanes] = high
        out[1, rows, lanes] = (value - high.astype(F32)).astype(BF)

    tables = jnp.concatenate([one[...] + two[...] + three[...], jnp.zeros((4, 64), F32)])
    put(jnp.concatenate([tables, jnp.zeros((16, 64), F32)], axis=1), slice(0, 16), slice(0, 128))
    row = lax.broadcasted_iota(jnp.int32, (16, WIDTH), 0)
    put(jnp.where(row == 12, gain_grad[...], 0.0), slice(0, 16), slice(128, 128 + WIDTH))


def small_call(one, two, three, gain_grad):
    return pl.pallas_call(
        small_kernel,
        in_specs=[pl.BlockSpec(memory_space=pltpu.VMEM)] * 4,
        out_specs=pl.BlockSpec(memory_space=pltpu.VMEM),
        out_shape=struct((2, PIECE, MERGED)),
        compiler_params=params(8),
        name="small_sums",
    )(one, two, three, gain_grad)


def window_kernel(place, d_query, d_keys_t, d_values_t, wq, wk, wv, own, for_row, for_core, for_chip, rest):
    full = mm(wk[...], d_keys_t[...]) + mm(wv[...], d_values_t[...])
    own[...] = (full[:, :REGION] + mm_nt(wq[...], d_query[...])).T
    rest[...] = full[:, REGION:].T
    row, odd = place[7], place[0]
    for out, begin in (
        (for_row, HALO - HALO * row),
        (for_core, 3 * HALO - HALO * odd),
        (for_chip, 2 * HALO + HALO * odd),
    ):
        out[...] = rest[pl.ds(pl.multiple_of(begin, HALO), HALO)].astype(BF)


def window_call(place, d_query, d_keys_t, d_values_t, wq, wk, wv):
    return pl.pallas_call(
        window_kernel,
        in_specs=[smem()] + [pl.BlockSpec(memory_space=pltpu.VMEM)] * 6,
        out_specs=[pl.BlockSpec(memory_space=pltpu.VMEM)] * 4,
        out_shape=[struct((REGION, WIDTH), F32)] + [struct((HALO, WIDTH))] * 3,
        scratch_shapes=[pltpu.VMEM((WINDOW - REGION, WIDTH), F32)],
        compiler_params=params(24),
        cost_estimate=cost(2_300_000_000, 10_000_000),
        name="window_back",
    )(place, d_query, d_keys_t, d_values_t, wq, wk, wv)


def input_kernel(
    place, tokens, gain, index, own, d_middle, from_row, from_core, from_chip, input_grad
):
    row, odd = place[7], place[0]
    back = own[...]
    for received, block in ((from_row, row), (from_core, 2 + odd), (from_chip, 3 - odd)):
        picks = index[pl.ds(block, 1), :]
        chosen = lax.broadcasted_iota(jnp.int32, (REGION, HALO), 0) == picks
        back = back + mm(jnp.where(chosen, 1.0, 0.0).astype(BF), received[...])
    value = tokens[...].astype(F32)
    inverse = lax.rsqrt(jnp.mean(value * value, axis=-1, keepdims=True) + EPS)
    scaled = back * gain[...].reshape(1, WIDTH).astype(F32)
    shared = jnp.mean(scaled * value, axis=-1, keepdims=True)
    input_grad[...] = (
        d_middle[...] + inverse * scaled - value * (inverse * inverse * inverse) * shared
    ).astype(BF)


def input_call(place, tokens, gain, index, own, d_middle, from_row, from_core, from_chip):
    return pl.pallas_call(
        input_kernel,
        in_specs=[smem()] + [pl.BlockSpec(memory_space=pltpu.VMEM)] * 8,
        out_specs=pl.BlockSpec(memory_space=pltpu.VMEM),
        out_shape=struct((REGION, WIDTH)),
        compiler_params=params(16),
        cost_estimate=cost(500_000_000, 6_000_000),
        name="input_back",
    )(place, tokens, gain, index, own, d_middle, from_row, from_core, from_chip)


def halves_kernel(ids, *refs, far):
    weights, gain, before, parts = refs[0:3], refs[3], refs[4], refs[5:11]
    skip = 18 if far else 11
    outs, gain_out = refs[skip : skip + 7], refs[skip + 7]
    weight, wide, tall, att, total, weight_sem, ffn_sem, att_sem = refs[skip + 8 :]

    def place_of(side, k):
        half = ids[0] ^ side
        return 2 * half + (((ids[1 + 3 * side + k] >> 5) & 1) ^ far)

    def weight_copy(side, k, number):
        rows = pl.ds(256 * k, 256)
        unit = 3 * side + k
        return pltpu.make_async_copy(
            weights[number].at[rows], weight.at[unit], weight_sem.at[unit]
        )

    def ffn_copy(side, k):
        begin = pl.multiple_of(place_of(side, k) * TILE, TILE)
        window = pl.ds(begin, TILE)
        if k == 2:
            return pltpu.make_async_copy(tall.at[side], outs[2].at[window], ffn_sem.at[3 * side + 2])
        return pltpu.make_async_copy(
            wide.at[side, k], outs[k].at[:, window], ffn_sem.at[3 * side + k]
        )

    def att_copy(side, k, number):
        rows = pl.ds(256 * k, 256)
        unit = 3 * side + k
        return pltpu.make_async_copy(att.at[unit], outs[3 + number].at[rows], att_sem.at[unit])

    def each_number(side, k, count, act):
        for number in range(count):

            @pl.when(place_of(side, k) == number)
            def _():
                act(number)

    units = [(side, k) for side in range(2) for k in range(3)]
    for side, k in units:
        each_number(side, k, 3, lambda number: weight_copy(side, k, number).start())
    total[...] = jnp.zeros_like(total)
    for side, k in units:
        unit = 3 * side + k
        flip = ids[1 + 3 * side + k] & 31
        for piece in range(32):
            block = parts[unit][piece ^ flip, :, :WIDTH].astype(F32)
            if k == 2:
                tall[side, piece * 16 : piece * 16 + 16] = block
                continue
            col, row = piece // 16, piece % 16
            for third in range(3):
                begin = row * 48 + third * 16
                wide[side, k, begin : begin + 16, col * 256 : col * 256 + 256] = block[
                    :, third * 256 : third * 256 + 256
                ]
        ffn_copy(side, k).start()
        flip = flip >> 1
        for row in range(16):
            for group in range(2):
                att[unit, row * 16 : row * 16 + 16, group * COLS : group * COLS + COLS] = parts[unit][
                    (row ^ flip) * 2 + group, :, WIDTH:
                ].astype(F32)
        each_number(side, k, 4, lambda number: att_copy(side, k, number).start())

        def add_gain(number):
            weight_copy(side, k, number).wait()
            product = att[unit] * weight[unit].astype(F32)
            total[:, 256 * k : 256 * k + 256] += lax.dot_general(
                jnp.ones((8, WIDTH), F32), product, (((1,), (1,)), ((), ())),
                precision=lax.Precision.HIGHEST, preferred_element_type=F32,
            )

        each_number(side, k, 3, add_gain)
    if far:
        sums = total[0:1] + before[...]
        gain_out[...] = (sums / gain[...].reshape(1, WIDTH).astype(F32)).reshape(WIDTH)
    else:
        gain_out[...] = total[0:1]
    for side, k in units:
        ffn_copy(side, k).wait()
        att_copy(side, k, 0).wait()


def halves_call(far, ids, weights, gain, before, own, other, nears=()):
    anywhere = pl.BlockSpec(memory_space=pl.ANY)
    vmem = pl.BlockSpec(memory_space=pltpu.VMEM)
    return pl.pallas_call(
        functools.partial(halves_kernel, far=far),
        in_specs=[smem()] + [anywhere] * 3 + [vmem] * 8 + [anywhere] * len(nears),
        out_specs=[anywhere] * 7 + [vmem],
        scratch_shapes=[
            pltpu.VMEM((6, 256, WIDTH), BF),
            pltpu.VMEM((2, 2, WIDTH, TILE), F32),
            pltpu.VMEM((2, TILE, WIDTH), F32),
            pltpu.VMEM((6, 256, WIDTH), F32),
            pltpu.VMEM((8, WIDTH), F32),
            pltpu.SemaphoreType.DMA((6,)),
            pltpu.SemaphoreType.DMA((6,)),
            pltpu.SemaphoreType.DMA((6,)),
        ],
        out_shape=[struct((WIDTH, FF), F32), struct((WIDTH, FF), F32), struct((FF, WIDTH), F32)]
        + [struct((WIDTH, WIDTH), F32)] * 4
        + [struct((WIDTH,) if far else (1, WIDTH), F32)],
        input_output_aliases={12 + k: k for k in range(len(nears))},
        compiler_params=params(28),
        cost_estimate=cost(10_000_000, 24_000_000),
        name="outputs_far" if far else "outputs_near",
    )(ids, *weights, gain, before, *own, *other, *nears)


AXES = ("row", "col")
OTHER_PAIRS = {0: 3, 3: 0, 1: 2, 2: 1}


def ring_pairs(axes, bit):
    pairs = []
    for chip in range(64):
        for core in range(2):
            spot = [chip // 16, chip // 4 % 4, chip % 4]
            first = (bit + core) % 2 == 0
            for axis in axes:
                spot[axis] = spot[axis] ^ 1 if first else OTHER_PAIRS[spot[axis]]
            partner = (spot[0] * 4 + spot[1]) * 4 + spot[2]
            pairs.append((2 * chip + core, 2 * partner + core))
    return pairs


CORE_PAIRS = [(d, d ^ 1) for d in range(SHARDS)]


def swap(value, pairs):
    return lax.ppermute(value, AXES, pairs)


def added(mine, received):
    return (mine.astype(F32) + received.astype(F32)).astype(BF)


def after(first, *values):
    held = lax.optimization_barrier((first, values))[1]
    return held[0] if len(values) == 1 else held


def words_sum(one, two):
    value = (one[0].astype(F32) + one[1].astype(F32)) + (two[0].astype(F32) + two[1].astype(F32))
    high = value.astype(BF)
    return jnp.stack([high, (value - high.astype(F32)).astype(BF)])


def body(
    tokens, attn_gain, query_weight, key_weight, value_weight, output_weight, ffn_gain, gate_weight,
    up_weight, down_weight, relative_table, layout_table, cotangent, rel_bucket, layout_bucket,
    halo_index,
):
    tokens, cotangent = tokens[0], cotangent[0]
    relative, layout = rel_bucket[0], layout_bucket[0]
    index = halo_index[0, 0]
    columns = lax.axis_size("col")
    row_pairs = [(0, 1), (1, 0)]
    core_pairs = [(c, c ^ 1) for c in range(columns)]
    chip_pairs = [p for c in range(1, columns - 1, 2) for p in ((c, c + 1), (c + 1, c))]

    exchange_row = lambda v: lax.ppermute(v, "row", row_pairs)
    exchange_core = lambda v: lax.ppermute(v, "col", core_pairs)
    exchange_chip = lambda v: lax.ppermute(v, "col", chip_pairs)

    def ring(axis, bit):
        return ring_pairs((axis,), bit)

    normed, *sends, ids = norm_call(tokens, attn_gain, index)
    received = (exchange_row(sends[0]), exchange_core(sends[1]), exchange_chip(sends[2]))
    bias = bias_call(relative_table, layout_table, relative, layout)
    cotangent_other = swap(cotangent, CORE_PAIRS)
    window, query, keys, values, probs, attended = attend_call(
        ids, normed, *received, query_weight, key_weight, value_weight, bias, 4
    )
    (
        layer_out, d_middle, d_attended, d_branch, gain_two_grad, normed_two, *halves
    ) = ffn_call(
        ids, tokens, attended, output_weight, ffn_gain, cotangent, gate_weight, up_weight, down_weight
    )
    mixed_send, mixed, gate_send, d_gate, up_send, d_up = halves
    normed_two_other, mixed_other, d_gate_other, d_up_other = [
        swap(v, CORE_PAIRS) for v in (normed_two, mixed_send, gate_send, up_send)
    ]
    d_query, d_keys_t, d_values_t, d_logits, *att = back_call(
        ids, window, query, keys, values, probs, attended, d_attended, d_branch
    )
    att_other = [swap(v, CORE_PAIRS) for v in att[:3]]
    normed_two = after(d_query, normed_two)
    merged = grads_call(
        ids, normed_two, normed_two_other, cotangent, cotangent_other,
        (d_gate, d_gate_other, d_up, d_up_other, mixed, mixed_other), att[3:], att_other,
    )
    sent, kept = list(merged[:3]), list(merged[3:])

    last = tuple(sent)
    got = [swap(sent[k], ring(k, 0)) for k in range(3)]
    tables = []
    for third in range(2):
        tables.append(table_call(third, d_logits, after(last, relative), layout))
        last = tables[-1]

    def halve(turn, got):
        half = kept[0].shape[0] // 2
        sent = [added(kept[k][half:], got[k][half:]) for k in range(3)]
        for k in range(3):
            kept[k] = added(kept[k][:half], got[k][:half])
        return tuple(sent), [swap(sent[k], ring((k + turn) % 3, 0)) for k in range(3)]

    own, *returns = window_call(
        ids, d_query, d_keys_t, d_values_t, query_weight, key_weight, after(last, value_weight)
    )
    last, got = halve(1, after(own, *got))
    from_row, from_chip = exchange_row(returns[0]), exchange_chip(returns[2])
    tables.append(table_call(2, d_logits, after(last, relative), layout))
    *got, from_row, from_chip = after(tables[-1], *got, from_row, from_chip)
    last, got = halve(2, got)
    from_core = exchange_core(after(last, returns[1]))
    small = small_call(*tables, after(last, gain_two_grad))
    got = after(small, *got)
    quarters = [
        jnp.stack([added(kept[k][2 * q : 2 * q + 2], got[k][2 * q : 2 * q + 2]) for k in range(3)])
        .reshape(6, PIECE, MERGED)
        for q in range(4)
    ]
    partners = {1: ring_pairs((1,), 1), 2: ring_pairs((0,), 1), 3: ring_pairs((0, 1), 1)}
    quarters[1] = jnp.concatenate([quarters[1], small])
    got = {q: swap(quarters[q], partners[q]) for q in (3, 2, 1)}
    mine = (
        (quarters[0].astype(F32) + got[1][:6].astype(F32))
        + (got[2].astype(F32) + got[3].astype(F32))
    ).astype(BF)
    small = words_sum(small, got[1][6:])
    got = swap(jnp.concatenate([mine, small]), ring(2, 1))
    mine = added(mine, got[:6])
    small = words_sum(small, got[6:])
    with_small = jnp.concatenate([mine, small])
    got = {q: swap(with_small if q == 2 else mine, partners[q]) for q in (3, 2, 1)}
    small = words_sum(small, got[2][6:])
    four = [v[:6].reshape(3, 2, PIECE, MERGED) for v in (mine, got[1], got[2], got[3])]
    near = [jnp.concatenate([v[k] for v in four]) for k in range(3)]
    for turn in (2, 1, 0):
        near[0] = jnp.concatenate([near[0], small])
        last = tuple(near)
        got = [swap(near[k], ring((k + turn) % 3, 0)) for k in range(3)]
        if turn == 0:
            break
        if turn == 1:
            input_grad = input_call(
                ids, after(last, tokens), attn_gain, index, own, d_middle,
                from_row, from_core, from_chip,
            )
            last = input_grad
        got = after(last, *got)
        small = words_sum(small, got[0][-2:])
        near = [jnp.concatenate([near[k][: got[1].shape[0]], got[k][: got[1].shape[0]]]) for k in range(3)]
    near_other = [swap(near[k], CORE_PAIRS) for k in range(3)]
    weights = (query_weight, key_weight, value_weight)
    empty = gain_two_grad
    *nears, gain_part = halves_call(0, ids, weights, attn_gain, empty, near, near_other)
    far, far_other, last = [], [], gain_part
    for k in range(3):
        far.append(after(last, got[k]))
        if k == 0:
            small = words_sum(small, far[0][-2:])
            got_small = swap(small, CORE_PAIRS)
        far_other.append(swap(far[k], CORE_PAIRS))
        last = far[k]
    small = words_sum(small, got_small)
    small = small[0].astype(F32) + small[1].astype(F32)
    gate_grad, up_grad, down_grad, query_grad, key_grad, value_grad, output_grad, gain_one_grad = (
        halves_call(1, ids, weights, attn_gain, gain_part, far, far_other, nears)
    )
    return (
        layer_out[None], input_grad[None], gain_one_grad, query_grad, key_grad, value_grad,
        output_grad, small[12, 128 : 128 + WIDTH], gate_grad, up_grad, down_grad,
        small[:HEADS, :32].T, small[:HEADS, 32:64].T,
    )


def solution(mesh):
    tokens = P("row", "col", None)
    whole_array = P()
    return jax.shard_map(
        body,
        mesh=mesh,
        in_specs=(tokens,) + (whole_array,) * 11 + (tokens,) * 3 + (P("row", "col", None, None),),
        out_specs=(tokens, tokens) + (whole_array,) * 11,
        check_vma=False,
    )
```

```python
import functools

import jax
import jax.numpy as jnp
from jax import lax
from jax.experimental import pallas as pl
from jax.experimental.pallas import tpu as pltpu
from jax.sharding import PartitionSpec as P

BF = jnp.bfloat16
F32 = jnp.float32
EPS = 1e-06
LOG2E = 1.4426950408889634
REGION = 384
WIDTH = 768
WINDOW = 768
HEADS = 12
HALO = 96
FF = 2048


def params(mib):
    return pltpu.CompilerParams(vmem_limit_bytes=mib * 2**20)


def cost(flops, moved, transcendentals=0):
    return pl.CostEstimate(flops=flops, bytes_accessed=moved, transcendentals=transcendentals)


def smem():
    return pl.BlockSpec(memory_space=pltpu.SMEM)


def whole(shape):
    return pl.BlockSpec(shape, lambda *_: (0,) * len(shape))


def mm(a, b):
    return jnp.dot(a, b, preferred_element_type=F32)


def mm_nt(a, b):
    return lax.dot_general(a, b, (((1,), (1,)), ((), ())), preferred_element_type=F32)


def mm_tn(a, b):
    return lax.dot_general(a, b, (((0,), (0,)), ((), ())), preferred_element_type=F32)


def struct(shape, dtype=BF):
    return jax.ShapeDtypeStruct(shape, dtype)


def near_by(shape, dtype=BF):
    return pltpu.VMEM(shape, dtype)


def main(shape, dtype=BF):
    return pltpu.HBM(shape, dtype)


def here(value):
    return pltpu.with_memory_space_constraint(value, pltpu.HBM)


def norm_kernel(tokens, gain, index, normed, send_row, send_core, send_chip, ids):
    value = tokens[...].astype(F32)
    inverse = lax.rsqrt(jnp.mean(value * value, axis=-1, keepdims=True) + EPS)
    low = (value * inverse * gain[...].reshape(1, WIDTH).astype(F32)).astype(BF)
    normed[...] = low
    row, col = lax.axis_index("row"), lax.axis_index("col")
    core = col & 1
    for out, block in ((send_row, row), (send_core, 2 + core), (send_chip, 3 - core)):
        picks = index[pl.ds(block, 1), :]
        chosen = lax.broadcasted_iota(jnp.int32, (REGION, HALO), 0) == picks
        out[...] = mm_tn(jnp.where(chosen, 1.0, 0.0).astype(BF), low).astype(BF)
    spots = (2 * row + (col >> 5), (col >> 3) & 3, (col >> 1) & 3)
    near = [((v + 1) >> 1) & 1 for v in spots]
    far = [v >> 1 for v in spots]
    ids[0] = core
    ids[7] = row
    for other in range(2):
        side = core ^ other
        first = [jnp.where(side == 1, f, n) for n, f in zip(near, far)]
        second = [jnp.where(side == 1, n, f) for n, f in zip(near, far)]
        for chunk in range(3):
            turned = [first[(chunk + turn) % 3] for turn in range(3)]
            ids[1 + 3 * other + chunk] = (
                turned[0] * 32 + turned[1] * 16 + turned[2] * 8 + second[0] * 4 + second[1] * 2
            )


def norm_call(tokens, gain, index):
    vmem = pl.BlockSpec(memory_space=pltpu.VMEM)
    return pl.pallas_call(
        norm_kernel,
        out_shape=(struct((REGION, WIDTH)),) + (struct((HALO, WIDTH)),) * 3 + (struct((8,), jnp.int32),),
        in_specs=[vmem] * 3,
        out_specs=(vmem,) * 4 + (smem(),),
        compiler_params=params(56),
        cost_estimate=cost(700_000_000, 2_000_000),
        name="norm_one",
    )(tokens, gain, index)


STEP = 2.0**-11
SHIFT = 9000
MASKED = -(2**31)
ROW_BLOCK = 32


def bias_kernel(relative_table, layout_table, relative, layout, out, table):
    rows = relative.shape[0]

    @pl.when(pl.program_id(0) == 0)
    def _():
        for number, source in enumerate((relative_table, layout_table)):
            values = jnp.round(source[...].astype(F32) * (LOG2E / STEP))
            fixed = jnp.concatenate([values, jnp.zeros((4, 32), F32)]).T.astype(jnp.int32)
            for pair in range(HEADS // 2):
                high = jnp.broadcast_to(fixed[:, 2 * pair : 2 * pair + 1], (32, 128))
                low = jnp.broadcast_to(fixed[:, 2 * pair + 1 : 2 * pair + 2], (32, 128))
                table[pair, number] = high * 65536 + (low + SHIFT)

    def look(words, low, bit3, bit4):
        four = [jnp.take_along_axis(words[8 * k : 8 * k + 8], low, axis=0) for k in range(4)]
        return jnp.where(
            bit4, jnp.where(bit3, four[3], four[2]), jnp.where(bit3, four[1], four[0])
        )

    def step(number, carry):
        begin = pl.multiple_of(number * 8, 8)
        for tile in range(WINDOW // 128):
            lanes = slice(tile * 128, tile * 128 + 128)
            rel = relative[pl.ds(begin, 8), lanes]
            lay = layout[pl.ds(begin, 8), lanes]
            rel_low, lay_low = rel & 7, lay & 7
            rel3, rel4 = (rel & 8) != 0, (rel & 16) != 0
            lay3, lay4 = (lay & 8) != 0, (lay & 16) != 0
            masked = rel >= 32
            for pair in range(HEADS // 2):
                word = look(table[pair, 0], rel_low, rel3, rel4)
                word = word + look(table[pair, 1], lay_low, lay3, lay4)
                out[pair, pl.ds(begin, 8), lanes] = jnp.where(masked, MASKED, word)
        return carry

    lax.fori_loop(0, rows // 8, step, 0)


def bias_call(relative_table, layout_table, relative, layout):
    block = 128
    buckets = pl.BlockSpec((block, WINDOW), lambda i: (i, 0))
    return pl.pallas_call(
        bias_kernel,
        grid=(REGION // block,),
        out_shape=struct((HEADS // 2, REGION, WINDOW), jnp.int32),
        in_specs=[whole((HEADS, 32)), whole((HEADS, 32)), buckets, buckets],
        out_specs=pl.BlockSpec((HEADS // 2, block, WINDOW), lambda i: (0, i, 0)),
        scratch_shapes=[pltpu.VMEM((HEADS // 2, 2, 32, 128), jnp.int32)],
        compiler_params=params(24),
        cost_estimate=cost(100_000_000, 17_000_000),
        name="bias",
    )(relative_table.T, layout_table.T, relative, layout)


def attend_kernel(
    place, normed, from_row, from_core, from_chip, wq, wk, wv, bias,
    window, query, keys, values, probs, attended, scores,
):
    width = wq.shape[1]

    @pl.when(pl.program_id(0) == 0)
    def _():
        row, odd = place[7], place[0]
        window[:REGION] = normed[...]
        window[REGION : REGION + 2 * HALO] = jnp.zeros((2 * HALO, WIDTH), BF)
        window[pl.ds(pl.multiple_of(REGION + HALO - HALO * row, HALO), HALO)] = from_row[...]
        window[pl.ds(pl.multiple_of(REGION + 3 * HALO - HALO * odd, HALO), HALO)] = from_core[...]
        window[pl.ds(pl.multiple_of(REGION + 2 * HALO + HALO * odd, HALO), HALO)] = from_chip[...]

    rows = window[...]
    query[...] = mm(rows[:REGION], wq[...]).astype(BF)
    keys[...] = mm(rows, wk[...]).astype(BF)
    lane = lax.broadcasted_iota(jnp.int32, (REGION, 128), 1)
    pairs = width // 128

    def score(pair):
        lanes = slice(pair * 128, pair * 128 + 128)
        for half in range(2):
            mine = (lane < 64) if half == 0 else (lane >= 64)
            one = jnp.where(mine, query[:, lanes], jnp.zeros((), BF))
            scores[2 * (pair % 2) + half] = mm_nt(one, keys[:, lanes])

    def soften(pair, half, begin):
        part = slice(begin, begin + ROW_BLOCK)
        word = bias[pair, part]
        fixed = (word >> 16) if half == 0 else (word & 0xFFFF)
        logits = scores[2 * (pair % 2) + half, part] * (0.125 * LOG2E) + fixed.astype(F32) * STEP
        logits = jnp.where(word == MASKED, -1.5e9, logits)
        highest = jnp.max(logits, axis=-1, keepdims=True)
        powered = jnp.exp2(logits - highest)
        total = jnp.sum(powered, axis=-1, keepdims=True)
        probs[2 * pair + half, part] = (powered * (1.0 / total)).astype(BF)

    score(0)
    values[...] = mm(rows, wv[...]).astype(BF)
    for pair in range(pairs):
        if pair + 1 < pairs:
            score(pair + 1)
        for begin in range(0, REGION, ROW_BLOCK):
            for half in range(2):
                soften(pair, half, begin)
        lanes = slice(pair * 128, pair * 128 + 128)
        halves = [mm(probs[2 * pair + half], values[:, lanes]) for half in range(2)]
        attended[:, lanes] = jnp.where(lane < 64, halves[0], halves[1]).astype(BF)


def attend_call(place, normed, from_row, from_core, from_chip, wq, wk, wv, bias, group):
    count = HEADS // group
    width = group * 64
    cols = lambda rows: pl.BlockSpec((rows, width), lambda g: (0, g))
    return pl.pallas_call(
        attend_kernel,
        grid=(count,),
        out_shape=(
            main((WINDOW, WIDTH)),
            main((REGION, WIDTH)),
            main((WINDOW, WIDTH)),
            main((WINDOW, WIDTH)),
            main((HEADS, REGION, WINDOW)),
            near_by((REGION, WIDTH)),
        ),
        in_specs=[smem(), whole((REGION, WIDTH))]
        + [whole((HALO, WIDTH))] * 3
        + [cols(WIDTH)] * 3
        + [pl.BlockSpec((group // 2, REGION, WINDOW), lambda g: (g, 0, 0))],
        out_specs=(
            whole((WINDOW, WIDTH)),
            cols(REGION),
            cols(WINDOW),
            cols(WINDOW),
            pl.BlockSpec((group, REGION, WINDOW), lambda g: (g, 0, 0)),
            cols(REGION),
        ),
        scratch_shapes=[pltpu.VMEM((4, REGION, WINDOW), F32)],
        compiler_params=params(40),
        cost_estimate=cost(3_500_000_000, 30_000_000, 3_600_000),
        name="attend",
    )(place, normed, from_row, from_core, from_chip, wq, wk, wv, bias)


SHARDS = 128
HALF = 64
TILE = 512
PIECE = 16
MERGED = 1152


def inverse_of(value):
    return lax.rsqrt(jnp.mean(value * value, axis=-1, keepdims=True) + EPS)


def ffn_kernel(
    ids, tokens, attended, wo, gain, cotangent, wg, wu, wd,
    layer_out, d_middle, d_attended, d_branch, gain_grad, normed,
    mixed_send, mixed_keep, gate_send, gate_keep, up_send, up_keep,
    middle, total_out, total_back,
):
    step = pl.program_id(0)

    @pl.when(step == 0)
    def _():
        value = tokens[...].astype(F32) + mm(attended[...], wo[...])
        middle[...] = value
        normed[...] = (value * inverse_of(value) * gain[...].reshape(1, WIDTH).astype(F32)).astype(BF)
        total_out[...] = value
        total_back[...] = jnp.zeros_like(total_back)

    low = normed[...]
    gate = mm(low, wg[...])
    up_part = mm(low, wu[...])
    d_mixed = mm_nt(cotangent[...], wd[...])
    curve = jnp.tanh(gate * (0.7978845608 + (0.7978845608 * 0.044715) * (gate * gate)))
    half_up = 0.5 * (1.0 + curve)
    act = gate * half_up
    slope = half_up + 0.5 * gate * (1.0 - curve * curve) * (
        0.7978845608 + (3 * 0.7978845608 * 0.044715) * gate * gate
    )
    mixed = (act * up_part).astype(BF)
    d_gate = (d_mixed * up_part * slope).astype(BF)
    d_up = (d_mixed * act).astype(BF)
    total_out[...] += mm(mixed, wd[...])
    total_back[...] += mm_nt(d_gate, wg[...]) + mm_nt(d_up, wu[...])

    @pl.when(step < 2)
    def _():
        mixed_send[...] = mixed
        gate_send[...] = d_gate
        up_send[...] = d_up

    @pl.when(step >= 2)
    def _():
        mixed_keep[...] = mixed
        gate_keep[...] = d_gate
        up_keep[...] = d_up

    @pl.when(step == 3)
    def _():
        layer_out[...] = total_out[...].astype(BF)
        value = middle[...]
        inverse = inverse_of(value)
        back = total_back[...]
        gain_grad[...] = jnp.sum(back * value * inverse, axis=0, keepdims=True)
        scaled = back * gain[...].reshape(1, WIDTH).astype(F32)
        shared = jnp.mean(scaled * value, axis=-1, keepdims=True)
        whole_grad = (
            cotangent[...].astype(F32)
            + inverse * scaled
            - value * (inverse * inverse * inverse) * shared
        )
        d_middle[...] = whole_grad
        branch = whole_grad.astype(BF)
        d_branch[...] = branch
        d_attended[...] = mm_nt(branch, wo[...]).astype(BF)


def ffn_call(ids, tokens, attended, wo, gain, cotangent, wg, wu, wd):
    def tile(g, ids):
        return jnp.where(g < 2, 1 - ids[0], ids[0]) * 2 + (g & 1)

    cols = pl.BlockSpec((WIDTH, TILE), lambda g, ids: (0, tile(g, ids)))
    sent = pl.BlockSpec((REGION, TILE), lambda g, ids: (0, jnp.minimum(g, 1)))
    kept = pl.BlockSpec((REGION, TILE), lambda g, ids: (0, jnp.maximum(g - 2, 0)))
    full = whole((REGION, WIDTH))
    return pl.pallas_call(
        ffn_kernel,
        grid_spec=pltpu.PrefetchScalarGridSpec(
            num_scalar_prefetch=1,
            grid=(FF // TILE,),
            in_specs=[
                full, full, whole((WIDTH, WIDTH)), whole((WIDTH,)), full, cols, cols,
                pl.BlockSpec((TILE, WIDTH), lambda g, ids: (tile(g, ids), 0)),
            ],
            out_specs=[full, full, full, full, whole((1, WIDTH)), full]
            + [sent, kept, sent, kept, sent, kept],
            scratch_shapes=[pltpu.VMEM((REGION, WIDTH), F32)] * 3,
        ),
        out_shape=[
            main((REGION, WIDTH)),
            main((REGION, WIDTH), F32),
            near_by((REGION, WIDTH)),
            near_by((REGION, WIDTH)),
            main((1, WIDTH), F32),
            main((REGION, WIDTH)),
        ]
        + [main((REGION, FF // 2))] * 6,
        compiler_params=params(36),
        cost_estimate=cost(8_000_000_000, 20_000_000, 800_000),
        name="feed_forward",
    )(ids, tokens, attended, wo, gain, cotangent, wg, here(wu), here(wd))


def grads_kernel(ids, *refs):
    normeds, cots = refs[0:2], refs[2:4]
    hidden = (refs[4:6], refs[6:8], refs[8:10])
    att, att_other, outs = refs[10:13], refs[13:16], refs[16:22]
    normed, grad_out, right, normed_t, kept, in_sem = refs[22:]

    def pair_in(sources, target, number):
        return [
            pltpu.make_async_copy(
                sources[k], target.at[k * REGION : k * REGION + REGION], in_sem.at[number]
            )
            for k in range(2)
        ]

    copies = [pair_in(normeds, normed, 0)]
    copies += [pair_in(hidden[k], right.at[k], 1 + k) for k in range(3)]
    copies += [pair_in(cots, grad_out, 4)]
    copies += [[pltpu.make_async_copy(att[k], kept.at[k], in_sem.at[5]) for k in range(3)]]
    for number in (0, 1, 5, 2, 4, 3):
        for copy in copies[number]:
            copy.start()

    def wait(number):
        for copy in copies[number]:
            copy.wait()

    def put(out, k, grad, flip):
        for piece in range(32):
            col, row = piece // 16, piece % 16
            if k == 2:
                out[piece ^ flip, :, :WIDTH] = grad[piece * 16 : piece * 16 + 16]
                continue
            for third in range(3):
                begin = row * 48 + third * 16
                out[piece ^ flip, :, third * 256 : third * 256 + 256] = grad[
                    begin : begin + 16, col * 256 : col * 256 + 256
                ]

    wait(0)
    normed_t[...] = normed[...].T
    for k in range(3):
        wait(1 + k)
        if k == 2:
            wait(4)
        place = ids[1 + k]
        top, flip = (place >> 5) & 1, place & 31
        for tile in range(2):
            cols = slice(tile * TILE, tile * TILE + TILE)
            if k < 2:
                grad = mm(normed_t[...], right[k, :, cols]).astype(BF)
            else:
                grad = mm_tn(right[k, :, cols], grad_out[...]).astype(BF)
            away = top != tile

            @pl.when(away)
            def _():
                put(outs[k], k, grad, flip)

            @pl.when(jnp.logical_not(away))
            def _():
                put(outs[3 + k], k, grad, flip)

        if k == 0:
            wait(5)
        for spot in range(32):
            out = outs[3 * (1 - spot // 16) + k]
            for group in range(2):
                both = kept[k, spot, group].astype(F32) + att_other[k][spot, group].astype(F32)
                out[(spot % 16) * 2 + group, :, WIDTH:] = both.astype(BF)


def grads_call(ids, normed, normed_other, cotangent, cotangent_other, pairs, att, att_other):
    merged = (32, PIECE, MERGED)
    anywhere = pl.BlockSpec(memory_space=pl.ANY)
    vmem = pl.BlockSpec(memory_space=pltpu.VMEM)
    pairs = [here(v) if k % 2 == 0 else v for k, v in enumerate(pairs)]
    return pl.pallas_call(
        grads_kernel,
        in_specs=[smem()] + [anywhere] * 13 + [vmem] * 3,
        out_specs=[vmem] * 6,
        scratch_shapes=[
            pltpu.VMEM((2 * REGION, WIDTH), BF),
            pltpu.VMEM((2 * REGION, WIDTH), BF),
            pltpu.VMEM((3, 2 * REGION, FF // 2), BF),
            pltpu.VMEM((WIDTH, 2 * REGION), BF),
            pltpu.VMEM((3, 32, 2, PIECE, COLS), BF),
            pltpu.SemaphoreType.DMA((6,)),
        ],
        out_shape=[near_by(merged)] * 6,
        compiler_params=params(20),
        cost_estimate=cost(3_700_000_000, 16_000_000),
        name="feed_forward_grads",
    )(
        ids, here(normed), normed_other, here(cotangent), cotangent_other, *pairs, *map(here, att),
        *att_other,
    )


GROUP = 6
COLS = GROUP * 64


def back_kernel(
    ids, window, query, keys, values, probs, attended, d_attended, attended_all, d_branch, *refs
):
    d_query, d_keys_t, d_values_t, d_logits = refs[:4]
    sends, keeps = refs[4:7], refs[7:10]
    window_t, slopes, attended_t = refs[10:]

    @pl.when(pl.program_id(0) == 0)
    def _():
        window_t[...] = window[...].T
        attended_t[...] = attended_all[...].T

    query_t = query[...].T
    d_att_t = d_attended[...].T
    lane = lax.broadcasted_iota(jnp.int32, (REGION, 128), 1)
    for pair in range(GROUP // 2):
        lanes = slice(pair * 128, pair * 128 + 128)
        halves = []
        for half in range(2):
            head = 2 * pair + half
            mine = (lane < 64) if half == 0 else (lane >= 64)
            one = jnp.where(mine, d_attended[:, lanes], jnp.zeros((), BF))
            shared = jnp.sum(
                one.astype(F32) * attended[:, lanes].astype(F32), axis=-1, keepdims=True
            )
            slot = head % 2
            slopes[slot] = mm_nt(one, values[:, lanes])
            for begin in range(0, REGION, 32):
                part = slice(begin, begin + 32)
                grad = probs[head, part].astype(F32) * (slopes[slot, part] - shared[part])
                d_logits[head, part] = grad.astype(BF)
            halves.append(mm(d_logits[head], keys[:, lanes]))
            feats = slice(head * 64, head * 64 + 64)
            d_keys_t[feats] = (mm(query_t[feats], d_logits[head]) * 0.125).astype(BF)
            d_values_t[feats] = mm(d_att_t[feats], probs[head]).astype(BF)
        d_query[:, lanes] = (jnp.where(lane < 64, halves[0], halves[1]) * 0.125).astype(BF)
    grads = (
        mm(window_t[:, :REGION], d_query[...]).astype(BF),
        mm_nt(window_t[...], d_keys_t[...]).astype(BF),
        mm_nt(window_t[...], d_values_t[...]).astype(BF),
        mm(attended_t[...], d_branch[...]).astype(BF),
    )

    def put(numbers, outs, first):
        for third in range(3):
            flip = (ids[first + third] >> 1) & 31
            for number in numbers:
                for row in range(16):
                    shard = (number & 1) * 16 + row
                    begin = third * 256 + row * 16
                    outs[third][shard ^ flip, 0] = grads[number][begin : begin + 16]

    first = ids[0] == 0

    @pl.when(first)
    def _():
        put((0, 1), keeps, 1)
        put((2, 3), sends, 4)

    @pl.when(jnp.logical_not(first))
    def _():
        put((0, 1), sends, 4)
        put((2, 3), keeps, 1)


def back_call(ids, window, query, keys, values, probs, attended, d_attended, d_branch):
    cols = lambda rows: pl.BlockSpec((rows, COLS), lambda g: (0, g))
    feats = pl.BlockSpec((COLS, WINDOW), lambda g: (g, 0))
    heads = pl.BlockSpec((GROUP, REGION, WINDOW), lambda g: (g, 0, 0))
    return pl.pallas_call(
        back_kernel,
        grid=(2,),
        in_specs=[
            smem(), whole((WINDOW, WIDTH)), cols(REGION), cols(WINDOW), cols(WINDOW), heads,
            cols(REGION), cols(REGION), whole((REGION, WIDTH)), cols(REGION),
        ],
        out_specs=[cols(REGION), feats, feats, heads]
        + [pl.BlockSpec((32, 1, PIECE, COLS), lambda g: (0, g, 0, 0))] * 6,
        out_shape=[
            main((REGION, WIDTH)),
            main((WIDTH, WINDOW)),
            main((WIDTH, WINDOW)),
            main((HEADS, REGION, WINDOW)),
        ]
        + [main((32, 2, PIECE, COLS))] * 6,
        scratch_shapes=[
            pltpu.VMEM((WIDTH, WINDOW), BF),
            pltpu.VMEM((2, REGION, WINDOW), F32),
            pltpu.VMEM((WIDTH, REGION), BF),
        ],
        compiler_params=params(44),
        cost_estimate=cost(6_000_000_000, 30_000_000),
        name="attend_back",
    )(
        ids, here(window), here(query), here(keys), here(values), here(probs), attended, d_attended,
        attended, d_branch,
    )


ROWS = 16
BLOCKS = 4


def table_kernel(d_logits, relative, layout, out, onehot, total):
    step = pl.program_id(0)

    @pl.when(step == 0)
    def _():
        total[...] = jnp.zeros_like(total)

    bucket = lax.broadcasted_iota(jnp.int32, (32, WINDOW), 0)
    added = []
    for block in range(BLOCKS):
        for row in range(ROWS):
            for offset, source in ((0, relative), (32, layout)):
                at = block * ROWS + row
                hit = source[at : at + 1, :] == bucket
                begin = row * 64 + offset
                onehot[block, begin : begin + 32] = jnp.where(hit, 1.0, 0.0).astype(BF)
        rows = slice(block * ROWS, block * ROWS + ROWS)
        left = d_logits[:, rows, :].reshape(HEADS * ROWS, WINDOW)
        added.append(mm_nt(left, onehot[block]))
    total[...] += (added[0] + added[1]) + (added[2] + added[3])

    @pl.when(step == pl.num_programs(0) - 1)
    def _():
        shape = total.shape
        left_row = lax.broadcasted_iota(jnp.int32, shape, 0) % ROWS
        right_row = lax.broadcasted_iota(jnp.int32, shape, 1) // 64
        kept = jnp.where(left_row == right_row, total[...], 0.0)
        by_head = jnp.sum(kept.reshape(HEADS, ROWS, shape[1]), axis=1)
        folded = by_head[:, 0:128]
        for tile in range(1, shape[1] // 128):
            folded = folded + by_head[:, tile * 128 : tile * 128 + 128]
        out[...] = folded[:, :64] + folded[:, 64:]


def table_call(third, d_logits, relative, layout):
    rows = ROWS * BLOCKS
    steps = REGION // 3 // rows
    heads = pl.BlockSpec((HEADS, rows, WINDOW), lambda i: (0, third * steps + i, 0))
    buckets = pl.BlockSpec((rows, WINDOW), lambda i: (third * steps + i, 0))
    return pl.pallas_call(
        table_kernel,
        grid=(steps,),
        in_specs=[heads, buckets, buckets],
        out_specs=whole((HEADS, 64)),
        out_shape=struct((HEADS, 64), F32),
        scratch_shapes=[
            pltpu.VMEM((BLOCKS, ROWS * 64, WINDOW), BF),
            pltpu.VMEM((HEADS * ROWS, ROWS * 64), F32),
        ],
        compiler_params=params(20),
        cost_estimate=cost(2_500_000_000, 4_000_000),
        name="table_grads",
    )(d_logits, relative, layout)


def small_kernel(one, two, three, gain_grad, out):
    out[...] = jnp.zeros_like(out)

    def put(value, rows, lanes):
        high = value.astype(BF)
        out[0, rows, lanes] = high
        out[1, rows, lanes] = (value - high.astype(F32)).astype(BF)

    tables = jnp.concatenate([one[...] + two[...] + three[...], jnp.zeros((4, 64), F32)])
    put(jnp.concatenate([tables, jnp.zeros((16, 64), F32)], axis=1), slice(0, 16), slice(0, 128))
    row = lax.broadcasted_iota(jnp.int32, (16, WIDTH), 0)
    put(jnp.where(row == 12, gain_grad[...], 0.0), slice(0, 16), slice(128, 128 + WIDTH))


def small_call(one, two, three, gain_grad):
    return pl.pallas_call(
        small_kernel,
        in_specs=[pl.BlockSpec(memory_space=pltpu.VMEM)] * 4,
        out_specs=pl.BlockSpec(memory_space=pltpu.VMEM),
        out_shape=struct((2, PIECE, MERGED)),
        compiler_params=params(8),
        name="small_sums",
    )(one, two, three, gain_grad)


def window_kernel(place, d_query, d_keys_t, d_values_t, wq, wk, wv, own, for_row, for_core, for_chip, rest):
    full = mm(wk[...], d_keys_t[...]) + mm(wv[...], d_values_t[...])
    own[...] = (full[:, :REGION] + mm_nt(wq[...], d_query[...])).T
    rest[...] = full[:, REGION:].T
    row, odd = place[7], place[0]
    for out, begin in (
        (for_row, HALO - HALO * row),
        (for_core, 3 * HALO - HALO * odd),
        (for_chip, 2 * HALO + HALO * odd),
    ):
        out[...] = rest[pl.ds(pl.multiple_of(begin, HALO), HALO)].astype(BF)


def window_call(place, d_query, d_keys_t, d_values_t, wq, wk, wv):
    return pl.pallas_call(
        window_kernel,
        in_specs=[smem()] + [pl.BlockSpec(memory_space=pltpu.VMEM)] * 6,
        out_specs=[pl.BlockSpec(memory_space=pltpu.VMEM)] * 4,
        out_shape=[struct((REGION, WIDTH), F32)] + [struct((HALO, WIDTH))] * 3,
        scratch_shapes=[pltpu.VMEM((WINDOW - REGION, WIDTH), F32)],
        compiler_params=params(24),
        cost_estimate=cost(2_300_000_000, 10_000_000),
        name="window_back",
    )(place, d_query, d_keys_t, d_values_t, wq, wk, wv)


def input_kernel(
    place, tokens, gain, index, own, d_middle, from_row, from_core, from_chip, input_grad
):
    row, odd = place[7], place[0]
    back = own[...]
    for received, block in ((from_row, row), (from_core, 2 + odd), (from_chip, 3 - odd)):
        picks = index[pl.ds(block, 1), :]
        chosen = lax.broadcasted_iota(jnp.int32, (REGION, HALO), 0) == picks
        back = back + mm(jnp.where(chosen, 1.0, 0.0).astype(BF), received[...])
    value = tokens[...].astype(F32)
    inverse = lax.rsqrt(jnp.mean(value * value, axis=-1, keepdims=True) + EPS)
    scaled = back * gain[...].reshape(1, WIDTH).astype(F32)
    shared = jnp.mean(scaled * value, axis=-1, keepdims=True)
    input_grad[...] = (
        d_middle[...] + inverse * scaled - value * (inverse * inverse * inverse) * shared
    ).astype(BF)


def input_call(place, tokens, gain, index, own, d_middle, from_row, from_core, from_chip):
    return pl.pallas_call(
        input_kernel,
        in_specs=[smem()] + [pl.BlockSpec(memory_space=pltpu.VMEM)] * 8,
        out_specs=pl.BlockSpec(memory_space=pltpu.VMEM),
        out_shape=struct((REGION, WIDTH)),
        compiler_params=params(16),
        cost_estimate=cost(500_000_000, 6_000_000),
        name="input_back",
    )(place, tokens, gain, index, own, d_middle, from_row, from_core, from_chip)


def halves_kernel(ids, *refs, stage):
    sides = (range(2), range(1), range(1, 2))[stage]
    far = 1 if stage else 0
    units = [(side, k) for side in sides for k in range(3)]
    weights, gain, before, words = refs[0:3], refs[3], refs[4], refs[5:7]
    parts = dict(zip([3 * side + k for side, k in units], refs[7:]))
    skip = 7 + len(units) + (7 if stage else 0)
    outs, gain_out = refs[skip : skip + 7], refs[skip + 7]
    if stage == 2:
        ffn_gain, rel, lay = refs[skip + 8 : skip + 11]
        skip += 3
    weight, wide, tall, att, total, weight_sem, ffn_sem, att_sem = refs[skip + 8 :]

    def place_of(side, k):
        half = ids[0] ^ side
        return 2 * half + (((ids[1 + 3 * side + k] >> 5) & 1) ^ far)

    def weight_copy(side, k, number):
        rows = pl.ds(256 * k, 256)
        unit = 3 * side + k
        return pltpu.make_async_copy(
            weights[number].at[rows], weight.at[unit], weight_sem.at[unit]
        )

    def ffn_copy(side, k):
        begin = pl.multiple_of(place_of(side, k) * TILE, TILE)
        window = pl.ds(begin, TILE)
        if k == 2:
            return pltpu.make_async_copy(tall.at[side], outs[2].at[window], ffn_sem.at[3 * side + 2])
        return pltpu.make_async_copy(
            wide.at[side, k], outs[k].at[:, window], ffn_sem.at[3 * side + k]
        )

    def att_copy(side, k, number):
        rows = pl.ds(256 * k, 256)
        unit = 3 * side + k
        return pltpu.make_async_copy(att.at[unit], outs[3 + number].at[rows], att_sem.at[unit])

    def each_number(side, k, count, act):
        for number in range(count):

            @pl.when(place_of(side, k) == number)
            def _():
                act(number)

    for side, k in units:
        each_number(side, k, 3, lambda number: weight_copy(side, k, number).start())
    total[...] = jnp.zeros_like(total)
    for side, k in units:
        unit = 3 * side + k
        flip = ids[1 + 3 * side + k] & 31
        for piece in range(32):
            block = parts[unit][piece ^ flip, :, :WIDTH].astype(F32)
            if k == 2:
                tall[side, piece * 16 : piece * 16 + 16] = block
                continue
            col, row = piece // 16, piece % 16
            for third in range(3):
                begin = row * 48 + third * 16
                wide[side, k, begin : begin + 16, col * 256 : col * 256 + 256] = block[
                    :, third * 256 : third * 256 + 256
                ]
        ffn_copy(side, k).start()
        flip = flip >> 1
        for row in range(16):
            for group in range(2):
                att[unit, row * 16 : row * 16 + 16, group * COLS : group * COLS + COLS] = parts[unit][
                    (row ^ flip) * 2 + group, :, WIDTH:
                ].astype(F32)
        each_number(side, k, 4, lambda number: att_copy(side, k, number).start())

        def add_gain(number):
            weight_copy(side, k, number).wait()
            product = att[unit] * weight[unit].astype(F32)
            total[:, 256 * k : 256 * k + 256] += lax.dot_general(
                jnp.ones((8, WIDTH), F32), product, (((1,), (1,)), ((), ())),
                precision=lax.Precision.HIGHEST, preferred_element_type=F32,
            )

        each_number(side, k, 3, add_gain)
    if stage == 2:
        sums = total[0:1] + before[...]
        gain_out[...] = (sums / gain[...].reshape(1, WIDTH).astype(F32)).reshape(WIDTH)
        both = [word[0].astype(F32) + word[1].astype(F32) for word in words]
        small = both[0] + both[1]
        ffn_gain[...] = small[12:13, 128 : 128 + WIDTH].reshape(WIDTH)
        rel[...] = small[:HEADS, 0:32]
        lay[...] = small[:HEADS, 32:64]
    else:
        gain_out[...] = total[0:1] + (before[...] if stage else 0.0)
    for side, k in units:
        ffn_copy(side, k).wait()
        att_copy(side, k, 0).wait()


def halves_call(stage, ids, weights, gain, before, words, parts, firsts=()):
    anywhere = pl.BlockSpec(memory_space=pl.ANY)
    vmem = pl.BlockSpec(memory_space=pltpu.VMEM)
    ends = [struct((WIDTH,), F32), struct((HEADS, 32), F32), struct((HEADS, 32), F32)]
    last = stage == 2
    return pl.pallas_call(
        functools.partial(halves_kernel, stage=stage),
        in_specs=[smem()] + [anywhere] * 3 + [vmem] * (4 + len(parts)) + [anywhere] * len(firsts),
        out_specs=[anywhere] * 7 + [vmem] * (4 if last else 1),
        scratch_shapes=[
            pltpu.VMEM((6, 256, WIDTH), BF),
            pltpu.VMEM((2, 2, WIDTH, TILE), F32),
            pltpu.VMEM((2, TILE, WIDTH), F32),
            pltpu.VMEM((6, 256, WIDTH), F32),
            pltpu.VMEM((8, WIDTH), F32),
            pltpu.SemaphoreType.DMA((6,)),
            pltpu.SemaphoreType.DMA((6,)),
            pltpu.SemaphoreType.DMA((6,)),
        ],
        out_shape=[struct((WIDTH, FF), F32), struct((WIDTH, FF), F32), struct((FF, WIDTH), F32)]
        + [struct((WIDTH, WIDTH), F32)] * 4
        + [struct((WIDTH,) if last else (1, WIDTH), F32)]
        + (ends if last else []),
        input_output_aliases={8 + len(parts) + k: k for k in range(len(firsts))},
        compiler_params=params(28),
        cost_estimate=cost(10_000_000, 24_000_000),
        name=("outputs_near", "outputs_far_own", "outputs_far_other")[stage],
    )(ids, *weights, gain, before, *words, *parts, *firsts)


AXES = ("row", "col")
OTHER_PAIRS = {0: 3, 3: 0, 1: 2, 2: 1}


def ring_pairs(axes, bit):
    pairs = []
    for chip in range(64):
        for core in range(2):
            spot = [chip // 16, chip // 4 % 4, chip % 4]
            first = (bit + core) % 2 == 0
            for axis in axes:
                spot[axis] = spot[axis] ^ 1 if first else OTHER_PAIRS[spot[axis]]
            partner = (spot[0] * 4 + spot[1]) * 4 + spot[2]
            pairs.append((2 * chip + core, 2 * partner + core))
    return pairs


CORE_PAIRS = [(d, d ^ 1) for d in range(SHARDS)]


def swap(value, pairs):
    return lax.ppermute(value, AXES, pairs)


def added(mine, received):
    return (mine.astype(F32) + received.astype(F32)).astype(BF)


def after(first, *values):
    held = lax.optimization_barrier((first, values))[1]
    return held[0] if len(values) == 1 else held


def words_sum(one, two):
    value = (one[0].astype(F32) + one[1].astype(F32)) + (two[0].astype(F32) + two[1].astype(F32))
    high = value.astype(BF)
    return jnp.stack([high, (value - high.astype(F32)).astype(BF)])


def body(
    tokens, attn_gain, query_weight, key_weight, value_weight, output_weight, ffn_gain, gate_weight,
    up_weight, down_weight, relative_table, layout_table, cotangent, rel_bucket, layout_bucket,
    halo_index,
):
    tokens, cotangent = tokens[0], cotangent[0]
    relative, layout = rel_bucket[0], layout_bucket[0]
    index = halo_index[0, 0]
    columns = lax.axis_size("col")
    row_pairs = [(0, 1), (1, 0)]
    core_pairs = [(c, c ^ 1) for c in range(columns)]
    chip_pairs = [p for c in range(1, columns - 1, 2) for p in ((c, c + 1), (c + 1, c))]

    exchange_row = lambda v: lax.ppermute(v, "row", row_pairs)
    exchange_core = lambda v: lax.ppermute(v, "col", core_pairs)
    exchange_chip = lambda v: lax.ppermute(v, "col", chip_pairs)

    def ring(axis, bit):
        return ring_pairs((axis,), bit)

    normed, *sends, ids = norm_call(tokens, attn_gain, index)
    received = (exchange_row(sends[0]), exchange_core(sends[1]), exchange_chip(sends[2]))
    bias = bias_call(relative_table, layout_table, relative, layout)
    cotangent_other = swap(cotangent, CORE_PAIRS)
    window, query, keys, values, probs, attended = attend_call(
        ids, normed, *received, query_weight, key_weight, value_weight, bias, 4
    )
    (
        layer_out, d_middle, d_attended, d_branch, gain_two_grad, normed_two, *halves
    ) = ffn_call(
        ids, tokens, attended, output_weight, ffn_gain, cotangent, gate_weight, up_weight, down_weight
    )
    mixed_send, mixed, gate_send, d_gate, up_send, d_up = halves
    normed_two_other, mixed_other, d_gate_other, d_up_other = [
        swap(v, CORE_PAIRS) for v in (normed_two, mixed_send, gate_send, up_send)
    ]
    d_query, d_keys_t, d_values_t, d_logits, *att = back_call(
        ids, window, query, keys, values, probs, attended, d_attended, d_branch
    )
    att_other = [swap(v, CORE_PAIRS) for v in att[:3]]
    normed_two = after(d_query, normed_two)
    merged = grads_call(
        ids, normed_two, normed_two_other, cotangent, cotangent_other,
        (d_gate, d_gate_other, d_up, d_up_other, mixed, mixed_other), att[3:], att_other,
    )
    sent, kept = list(merged[:3]), list(merged[3:])

    last = tuple(sent)
    got = [swap(sent[k], ring(k, 0)) for k in range(3)]
    tables = []
    for third in range(2):
        tables.append(table_call(third, d_logits, after(last, relative), layout))
        last = tables[-1]

    def halve(turn, got):
        half = kept[0].shape[0] // 2
        sent = [added(kept[k][half:], got[k][half:]) for k in range(3)]
        for k in range(3):
            kept[k] = added(kept[k][:half], got[k][:half])
        return tuple(sent), [swap(sent[k], ring((k + turn) % 3, 0)) for k in range(3)]

    own, *returns = window_call(
        ids, d_query, d_keys_t, d_values_t, query_weight, key_weight, after(last, value_weight)
    )
    last, got = halve(1, after(own, *got))
    from_row, from_chip = exchange_row(returns[0]), exchange_chip(returns[2])
    tables.append(table_call(2, d_logits, after(last, relative), layout))
    *got, from_row, from_chip = after(tables[-1], *got, from_row, from_chip)
    last, got = halve(2, got)
    from_core = exchange_core(after(last, returns[1]))
    small = small_call(*tables, after(last, gain_two_grad))
    got = after(small, *got)
    quarters = [
        jnp.stack([added(kept[k][2 * q : 2 * q + 2], got[k][2 * q : 2 * q + 2]) for k in range(3)])
        .reshape(6, PIECE, MERGED)
        for q in range(4)
    ]
    partners = {1: ring_pairs((1,), 1), 2: ring_pairs((0,), 1), 3: ring_pairs((0, 1), 1)}
    quarters[1] = jnp.concatenate([quarters[1], small])
    got = {q: swap(quarters[q], partners[q]) for q in (3, 2, 1)}
    mine = (
        (quarters[0].astype(F32) + got[1][:6].astype(F32))
        + (got[2].astype(F32) + got[3].astype(F32))
    ).astype(BF)
    small = words_sum(small, got[1][6:])
    got = swap(jnp.concatenate([mine, small]), ring(2, 1))
    mine = added(mine, got[:6])
    small = words_sum(small, got[6:])
    with_small = jnp.concatenate([mine, small])
    got = {q: swap(with_small if q == 2 else mine, partners[q]) for q in (3, 2, 1)}
    small = words_sum(small, got[2][6:])
    four = [v[:6].reshape(3, 2, PIECE, MERGED) for v in (mine, got[1], got[2], got[3])]
    near = [jnp.concatenate([v[k] for v in four]) for k in range(3)]
    for turn in (2, 1, 0):
        near[0] = jnp.concatenate([near[0], small])
        last = tuple(near)
        got = [swap(near[k], ring((k + turn) % 3, 0)) for k in range(3)]
        if turn == 0:
            break
        if turn == 1:
            input_grad = input_call(
                ids, after(last, tokens), attn_gain, index, own, d_middle,
                from_row, from_core, from_chip,
            )
            last = input_grad
        got = after(last, *got)
        small = words_sum(small, got[0][-2:])
        near = [jnp.concatenate([near[k][: got[1].shape[0]], got[k][: got[1].shape[0]]]) for k in range(3)]
    near_other = [swap(near[k], CORE_PAIRS) for k in range(3)]
    weights = (query_weight, key_weight, value_weight)
    common = (ids, weights, attn_gain)
    *outs, gain_part = halves_call(
        0, *common, gain_two_grad, (small, small), (*near, *near_other)
    )
    far, far_other, last = [], [], gain_part
    for k in range(3):
        far.append(after(last, got[k]))
        if k == 0:
            small = words_sum(small, far[0][-2:])
            small_other = swap(small, CORE_PAIRS)
        far_other.append(swap(far[k], CORE_PAIRS))
        last = far[k]
    words = (small, small)
    *outs, gain_part = halves_call(1, *common, gain_part, words, far, outs)
    words = (small, small_other)
    *outs, gain_one, gain_two, relative_grad, layout_grad = halves_call(
        2, *common, gain_part, words, after(gain_part, *far_other), outs
    )
    gate_grad, up_grad, down_grad, query_grad, key_grad, value_grad, output_grad = outs
    return (
        layer_out[None], input_grad[None], gain_one, query_grad, key_grad, value_grad,
        output_grad, gain_two, gate_grad, up_grad, down_grad, relative_grad.T, layout_grad.T,
    )


def solution(mesh):
    tokens = P("row", "col", None)
    whole_array = P()
    return jax.shard_map(
        body,
        mesh=mesh,
        in_specs=(tokens,) + (whole_array,) * 11 + (tokens,) * 3 + (P("row", "col", None, None),),
        out_specs=(tokens, tokens) + (whole_array,) * 11,
        check_vma=False,
    )
```

```python
import functools

import jax
import jax.numpy as jnp
from jax import lax
from jax.experimental import pallas as pl
from jax.experimental.pallas import tpu as pltpu
from jax.sharding import PartitionSpec as P

BF = jnp.bfloat16
F32 = jnp.float32
EPS = 1e-06
LOG2E = 1.4426950408889634
REGION = 384
WIDTH = 768
WINDOW = 768
HEADS = 12
HALO = 96
FF = 2048


def params(mib):
    return pltpu.CompilerParams(vmem_limit_bytes=mib * 2**20)


def cost(flops, moved, transcendentals=0):
    return pl.CostEstimate(flops=flops, bytes_accessed=moved, transcendentals=transcendentals)


def smem():
    return pl.BlockSpec(memory_space=pltpu.SMEM)


def whole(shape):
    return pl.BlockSpec(shape, lambda *_: (0,) * len(shape))


def mm(a, b):
    return jnp.dot(a, b, preferred_element_type=F32)


def mm_nt(a, b):
    return lax.dot_general(a, b, (((1,), (1,)), ((), ())), preferred_element_type=F32)


def mm_tn(a, b):
    return lax.dot_general(a, b, (((0,), (0,)), ((), ())), preferred_element_type=F32)


def struct(shape, dtype=BF):
    return jax.ShapeDtypeStruct(shape, dtype)


def near_by(shape, dtype=BF):
    return pltpu.VMEM(shape, dtype)


def main(shape, dtype=BF):
    return pltpu.HBM(shape, dtype)


def here(value):
    return pltpu.with_memory_space_constraint(value, pltpu.HBM)


def norm_kernel(tokens, gain, index, normed, send_row, send_core, send_chip, ids):
    value = tokens[...].astype(F32)
    inverse = lax.rsqrt(jnp.mean(value * value, axis=-1, keepdims=True) + EPS)
    low = (value * inverse * gain[...].reshape(1, WIDTH).astype(F32)).astype(BF)
    normed[...] = low
    row, col = lax.axis_index("row"), lax.axis_index("col")
    core = col & 1
    for out, block in ((send_row, row), (send_core, 2 + core), (send_chip, 3 - core)):
        picks = index[pl.ds(block, 1), :]
        chosen = lax.broadcasted_iota(jnp.int32, (REGION, HALO), 0) == picks
        out[...] = mm_tn(jnp.where(chosen, 1.0, 0.0).astype(BF), low).astype(BF)
    spots = (2 * row + (col >> 5), (col >> 3) & 3, (col >> 1) & 3)
    near = [((v + 1) >> 1) & 1 for v in spots]
    far = [v >> 1 for v in spots]
    ids[0] = core
    ids[7] = row
    for other in range(2):
        side = core ^ other
        first = [jnp.where(side == 1, f, n) for n, f in zip(near, far)]
        second = [jnp.where(side == 1, n, f) for n, f in zip(near, far)]
        for chunk in range(3):
            turned = [first[(chunk + turn) % 3] for turn in range(3)]
            ids[1 + 3 * other + chunk] = (
                turned[0] * 32 + turned[1] * 16 + turned[2] * 8 + second[0] * 4 + second[1] * 2
            )


def norm_call(tokens, gain, index):
    vmem = pl.BlockSpec(memory_space=pltpu.VMEM)
    return pl.pallas_call(
        norm_kernel,
        out_shape=(struct((REGION, WIDTH)),) + (struct((HALO, WIDTH)),) * 3 + (struct((8,), jnp.int32),),
        in_specs=[vmem] * 3,
        out_specs=(vmem,) * 4 + (smem(),),
        compiler_params=params(56),
        cost_estimate=cost(700_000_000, 2_000_000),
        name="norm_one",
    )(tokens, gain, index)


STEP = 2.0**-11
SHIFT = 9000
MASKED = -(2**31)
ROW_BLOCK = 32


def bias_kernel(relative_table, layout_table, relative, layout, out, table):
    rows = relative.shape[0]

    @pl.when(pl.program_id(0) == 0)
    def _():
        for number, source in enumerate((relative_table, layout_table)):
            values = jnp.round(source[...].astype(F32) * (LOG2E / STEP))
            fixed = jnp.concatenate([values, jnp.zeros((4, 32), F32)]).T.astype(jnp.int32)
            for pair in range(HEADS // 2):
                high = jnp.broadcast_to(fixed[:, 2 * pair : 2 * pair + 1], (32, 128))
                low = jnp.broadcast_to(fixed[:, 2 * pair + 1 : 2 * pair + 2], (32, 128))
                table[pair, number] = high * 65536 + (low + SHIFT)

    def look(words, low, bit3, bit4):
        four = [jnp.take_along_axis(words[8 * k : 8 * k + 8], low, axis=0) for k in range(4)]
        return jnp.where(
            bit4, jnp.where(bit3, four[3], four[2]), jnp.where(bit3, four[1], four[0])
        )

    def step(number, carry):
        begin = pl.multiple_of(number * 8, 8)
        for tile in range(WINDOW // 128):
            lanes = slice(tile * 128, tile * 128 + 128)
            rel = relative[pl.ds(begin, 8), lanes]
            lay = layout[pl.ds(begin, 8), lanes]
            rel_low, lay_low = rel & 7, lay & 7
            rel3, rel4 = (rel & 8) != 0, (rel & 16) != 0
            lay3, lay4 = (lay & 8) != 0, (lay & 16) != 0
            masked = rel >= 32
            for pair in range(HEADS // 2):
                word = look(table[pair, 0], rel_low, rel3, rel4)
                word = word + look(table[pair, 1], lay_low, lay3, lay4)
                out[pair, pl.ds(begin, 8), lanes] = jnp.where(masked, MASKED, word)
        return carry

    lax.fori_loop(0, rows // 8, step, 0)


def bias_call(relative_table, layout_table, relative, layout):
    block = 128
    buckets = pl.BlockSpec((block, WINDOW), lambda i: (i, 0))
    return pl.pallas_call(
        bias_kernel,
        grid=(REGION // block,),
        out_shape=struct((HEADS // 2, REGION, WINDOW), jnp.int32),
        in_specs=[whole((HEADS, 32)), whole((HEADS, 32)), buckets, buckets],
        out_specs=pl.BlockSpec((HEADS // 2, block, WINDOW), lambda i: (0, i, 0)),
        scratch_shapes=[pltpu.VMEM((HEADS // 2, 2, 32, 128), jnp.int32)],
        compiler_params=params(24),
        cost_estimate=cost(100_000_000, 17_000_000),
        name="bias",
    )(relative_table.T, layout_table.T, relative, layout)


def attend_kernel(
    place, normed, from_row, from_core, from_chip, wq, wk, wv, bias,
    window, query, keys, values, probs, attended, scores,
):
    width = wq.shape[1]

    @pl.when(pl.program_id(0) == 0)
    def _():
        row, odd = place[7], place[0]
        window[:REGION] = normed[...]
        window[REGION : REGION + 2 * HALO] = jnp.zeros((2 * HALO, WIDTH), BF)
        window[pl.ds(pl.multiple_of(REGION + HALO - HALO * row, HALO), HALO)] = from_row[...]
        window[pl.ds(pl.multiple_of(REGION + 3 * HALO - HALO * odd, HALO), HALO)] = from_core[...]
        window[pl.ds(pl.multiple_of(REGION + 2 * HALO + HALO * odd, HALO), HALO)] = from_chip[...]

    rows = window[...]
    query[...] = mm(rows[:REGION], wq[...]).astype(BF)
    keys[...] = mm(rows, wk[...]).astype(BF)
    lane = lax.broadcasted_iota(jnp.int32, (REGION, 128), 1)
    pairs = width // 128

    def score(pair):
        lanes = slice(pair * 128, pair * 128 + 128)
        for half in range(2):
            mine = (lane < 64) if half == 0 else (lane >= 64)
            one = jnp.where(mine, query[:, lanes], jnp.zeros((), BF))
            scores[2 * (pair % 2) + half] = mm_nt(one, keys[:, lanes])

    def soften(pair, half, begin):
        part = slice(begin, begin + ROW_BLOCK)
        word = bias[pair, part]
        fixed = (word >> 16) if half == 0 else (word & 0xFFFF)
        logits = scores[2 * (pair % 2) + half, part] * (0.125 * LOG2E) + fixed.astype(F32) * STEP
        logits = jnp.where(word == MASKED, -1.5e9, logits)
        highest = jnp.max(logits, axis=-1, keepdims=True)
        powered = jnp.exp2(logits - highest)
        total = jnp.sum(powered, axis=-1, keepdims=True)
        probs[2 * pair + half, part] = (powered * (1.0 / total)).astype(BF)

    score(0)
    values[...] = mm(rows, wv[...]).astype(BF)
    for pair in range(pairs):
        if pair + 1 < pairs:
            score(pair + 1)
        for begin in range(0, REGION, ROW_BLOCK):
            for half in range(2):
                soften(pair, half, begin)
        lanes = slice(pair * 128, pair * 128 + 128)
        halves = [mm(probs[2 * pair + half], values[:, lanes]) for half in range(2)]
        attended[:, lanes] = jnp.where(lane < 64, halves[0], halves[1]).astype(BF)


def attend_call(place, normed, from_row, from_core, from_chip, wq, wk, wv, bias, group):
    count = HEADS // group
    width = group * 64
    cols = lambda rows: pl.BlockSpec((rows, width), lambda g: (0, g))
    return pl.pallas_call(
        attend_kernel,
        grid=(count,),
        out_shape=(
            main((WINDOW, WIDTH)),
            main((REGION, WIDTH)),
            main((WINDOW, WIDTH)),
            main((WINDOW, WIDTH)),
            main((HEADS, REGION, WINDOW)),
            near_by((REGION, WIDTH)),
        ),
        in_specs=[smem(), whole((REGION, WIDTH))]
        + [whole((HALO, WIDTH))] * 3
        + [cols(WIDTH)] * 3
        + [pl.BlockSpec((group // 2, REGION, WINDOW), lambda g: (g, 0, 0))],
        out_specs=(
            whole((WINDOW, WIDTH)),
            cols(REGION),
            cols(WINDOW),
            cols(WINDOW),
            pl.BlockSpec((group, REGION, WINDOW), lambda g: (g, 0, 0)),
            cols(REGION),
        ),
        scratch_shapes=[pltpu.VMEM((4, REGION, WINDOW), F32)],
        compiler_params=params(40),
        cost_estimate=cost(3_500_000_000, 30_000_000, 3_600_000),
        name="attend",
    )(place, normed, from_row, from_core, from_chip, wq, wk, wv, bias)


SHARDS = 128
HALF = 64
TILE = 512
PIECE = 16
MERGED = 1152


def inverse_of(value):
    return lax.rsqrt(jnp.mean(value * value, axis=-1, keepdims=True) + EPS)


def ffn_kernel(
    ids, tokens, attended, wo, gain, cotangent, wg, wu, wd,
    layer_out, d_middle, d_attended, d_branch, gain_grad, normed,
    mixed_send, mixed_keep, gate_send, gate_keep, up_send, up_keep,
    middle, total_out, total_back,
):
    step = pl.program_id(0)

    @pl.when(step == 0)
    def _():
        value = tokens[...].astype(F32) + mm(attended[...], wo[...])
        middle[...] = value
        normed[...] = (value * inverse_of(value) * gain[...].reshape(1, WIDTH).astype(F32)).astype(BF)
        total_out[...] = value
        total_back[...] = jnp.zeros_like(total_back)

    low = normed[...]
    gate = mm(low, wg[...])
    up_part = mm(low, wu[...])
    d_mixed = mm_nt(cotangent[...], wd[...])
    curve = jnp.tanh(gate * (0.7978845608 + (0.7978845608 * 0.044715) * (gate * gate)))
    half_up = 0.5 * (1.0 + curve)
    act = gate * half_up
    slope = half_up + 0.5 * gate * (1.0 - curve * curve) * (
        0.7978845608 + (3 * 0.7978845608 * 0.044715) * gate * gate
    )
    mixed = (act * up_part).astype(BF)
    d_gate = (d_mixed * up_part * slope).astype(BF)
    d_up = (d_mixed * act).astype(BF)
    total_out[...] += mm(mixed, wd[...])
    total_back[...] += mm_nt(d_gate, wg[...]) + mm_nt(d_up, wu[...])

    @pl.when(step < 2)
    def _():
        mixed_send[...] = mixed
        gate_send[...] = d_gate
        up_send[...] = d_up

    @pl.when(step >= 2)
    def _():
        mixed_keep[...] = mixed
        gate_keep[...] = d_gate
        up_keep[...] = d_up

    @pl.when(step == 3)
    def _():
        layer_out[...] = total_out[...].astype(BF)
        value = middle[...]
        inverse = inverse_of(value)
        back = total_back[...]
        gain_grad[...] = jnp.sum(back * value * inverse, axis=0, keepdims=True)
        scaled = back * gain[...].reshape(1, WIDTH).astype(F32)
        shared = jnp.mean(scaled * value, axis=-1, keepdims=True)
        whole_grad = (
            cotangent[...].astype(F32)
            + inverse * scaled
            - value * (inverse * inverse * inverse) * shared
        )
        d_middle[...] = whole_grad
        branch = whole_grad.astype(BF)
        d_branch[...] = branch
        d_attended[...] = mm_nt(branch, wo[...]).astype(BF)


def ffn_call(ids, tokens, attended, wo, gain, cotangent, wg, wu, wd):
    def tile(g, ids):
        return jnp.where(g < 2, 1 - ids[0], ids[0]) * 2 + (g & 1)

    cols = pl.BlockSpec((WIDTH, TILE), lambda g, ids: (0, tile(g, ids)))
    sent = pl.BlockSpec((REGION, TILE), lambda g, ids: (0, jnp.minimum(g, 1)))
    kept = pl.BlockSpec((REGION, TILE), lambda g, ids: (0, jnp.maximum(g - 2, 0)))
    full = whole((REGION, WIDTH))
    return pl.pallas_call(
        ffn_kernel,
        grid_spec=pltpu.PrefetchScalarGridSpec(
            num_scalar_prefetch=1,
            grid=(FF // TILE,),
            in_specs=[
                full, full, whole((WIDTH, WIDTH)), whole((WIDTH,)), full, cols, cols,
                pl.BlockSpec((TILE, WIDTH), lambda g, ids: (tile(g, ids), 0)),
            ],
            out_specs=[full, full, full, full, whole((1, WIDTH)), full]
            + [sent, kept, sent, kept, sent, kept],
            scratch_shapes=[pltpu.VMEM((REGION, WIDTH), F32)] * 3,
        ),
        out_shape=[
            main((REGION, WIDTH)),
            main((REGION, WIDTH), F32),
            near_by((REGION, WIDTH)),
            near_by((REGION, WIDTH)),
            main((1, WIDTH), F32),
            main((REGION, WIDTH)),
        ]
        + [main((REGION, FF // 2))] * 6,
        compiler_params=params(36),
        cost_estimate=cost(8_000_000_000, 20_000_000, 800_000),
        name="feed_forward",
    )(ids, tokens, attended, wo, gain, cotangent, wg, here(wu), here(wd))


def grads_kernel(ids, *refs):
    normeds, cots = refs[0:2], refs[2:4]
    hidden = (refs[4:6], refs[6:8], refs[8:10])
    att, outs = refs[10:13], refs[13:19]
    normed, grad_out, right, normed_t, kept, in_sem = refs[19:]

    def pair_in(sources, target, number):
        return [
            pltpu.make_async_copy(
                sources[k], target.at[k * REGION : k * REGION + REGION], in_sem.at[number]
            )
            for k in range(2)
        ]

    copies = [pair_in(normeds, normed, 0)]
    copies += [pair_in(hidden[k], right.at[k], 1 + k) for k in range(3)]
    copies += [pair_in(cots, grad_out, 4)]
    copies += [[pltpu.make_async_copy(att[k], kept.at[k], in_sem.at[5]) for k in range(3)]]
    for number in (0, 1, 5, 2, 4, 3):
        for copy in copies[number]:
            copy.start()

    def wait(number):
        for copy in copies[number]:
            copy.wait()

    def put(out, k, grad, flip):
        for piece in range(32):
            col, row = piece // 16, piece % 16
            if k == 2:
                out[piece ^ flip, :, :WIDTH] = grad[piece * 16 : piece * 16 + 16]
                continue
            for third in range(3):
                begin = row * 48 + third * 16
                out[piece ^ flip, :, third * 256 : third * 256 + 256] = grad[
                    begin : begin + 16, col * 256 : col * 256 + 256
                ]

    wait(0)
    normed_t[...] = normed[...].T
    for k in range(3):
        wait(1 + k)
        if k == 2:
            wait(4)
        place = ids[1 + k]
        top, flip = (place >> 5) & 1, place & 31
        for tile in range(2):
            cols = slice(tile * TILE, tile * TILE + TILE)
            if k < 2:
                grad = mm(normed_t[...], right[k, :, cols]).astype(BF)
            else:
                grad = mm_tn(right[k, :, cols], grad_out[...]).astype(BF)
            away = top != tile

            @pl.when(away)
            def _():
                put(outs[k], k, grad, flip)

            @pl.when(jnp.logical_not(away))
            def _():
                put(outs[3 + k], k, grad, flip)

        if k == 0:
            wait(5)
        for spot in range(32):
            out = outs[3 * (1 - spot // 16) + k]
            for group in range(2):
                out[(spot % 16) * 2 + group, :, WIDTH:] = kept[k, spot, group]


def grads_call(ids, normed, normed_other, cotangent, cotangent_other, pairs, att):
    merged = (32, PIECE, MERGED)
    anywhere = pl.BlockSpec(memory_space=pl.ANY)
    vmem = pl.BlockSpec(memory_space=pltpu.VMEM)
    pairs = [here(v) if k % 2 == 0 else v for k, v in enumerate(pairs)]
    return pl.pallas_call(
        grads_kernel,
        in_specs=[smem()] + [anywhere] * 13,
        out_specs=[vmem] * 6,
        scratch_shapes=[
            pltpu.VMEM((2 * REGION, WIDTH), BF),
            pltpu.VMEM((2 * REGION, WIDTH), BF),
            pltpu.VMEM((3, 2 * REGION, FF // 2), BF),
            pltpu.VMEM((WIDTH, 2 * REGION), BF),
            pltpu.VMEM((3, 32, 2, PIECE, COLS), BF),
            pltpu.SemaphoreType.DMA((6,)),
        ],
        out_shape=[near_by(merged)] * 6,
        compiler_params=params(20),
        cost_estimate=cost(3_700_000_000, 16_000_000),
        name="feed_forward_grads",
    )(
        ids, here(normed), normed_other, here(cotangent), cotangent_other, *pairs, *map(here, att)
    )


def merge_kernel(*refs):
    att_other, pieces, outs = refs[0:3], refs[3:9], refs[9:15]
    for k in range(3):
        for side in range(2):
            half = att_other[k][16 - 16 * side : 32 - 16 * side].astype(F32)
            half = half.reshape(32, PIECE, COLS)
            number = 3 * side + k
            total = pieces[number][:, :, WIDTH:].astype(F32) + half
            outs[number][:, :, WIDTH:] = total.astype(BF)


def merge_call(att_other, pieces):
    vmem = pl.BlockSpec(memory_space=pltpu.VMEM)
    return pl.pallas_call(
        merge_kernel,
        in_specs=[vmem] * 9,
        out_specs=[vmem] * 6,
        out_shape=[near_by((32, PIECE, MERGED))] * 6,
        input_output_aliases={3 + number: number for number in range(6)},
        compiler_params=params(8),
        cost_estimate=cost(10_000_000, 10_000_000),
        name="merge_cores",
    )(*att_other, *pieces)


GROUP = 6
COLS = GROUP * 64


def back_kernel(
    ids, window, query, keys, values, probs, attended, d_attended, attended_all, d_branch, *refs
):
    d_query, d_keys_t, d_values_t, d_logits = refs[:4]
    sends, keeps = refs[4:7], refs[7:10]
    window_t, slopes, attended_t = refs[10:]

    @pl.when(pl.program_id(0) == 0)
    def _():
        window_t[...] = window[...].T
        attended_t[...] = attended_all[...].T

    query_t = query[...].T
    d_att_t = d_attended[...].T
    nothing = jnp.zeros((64, REGION), BF)

    def both_heads(rows):
        return jnp.concatenate(
            [
                jnp.concatenate([rows[:64], nothing], axis=1),
                jnp.concatenate([nothing, rows[64:]], axis=1),
            ]
        )

    lane = lax.broadcasted_iota(jnp.int32, (REGION, 128), 1)
    for pair in range(GROUP // 2):
        lanes = slice(pair * 128, pair * 128 + 128)
        halves = []
        for half in range(2):
            head = 2 * pair + half
            mine = (lane < 64) if half == 0 else (lane >= 64)
            one = jnp.where(mine, d_attended[:, lanes], jnp.zeros((), BF))
            shared = jnp.sum(
                one.astype(F32) * attended[:, lanes].astype(F32), axis=-1, keepdims=True
            )
            slot = head % 2
            slopes[slot] = mm_nt(one, values[:, lanes])
            for begin in range(0, REGION, 32):
                part = slice(begin, begin + 32)
                grad = probs[head, part].astype(F32) * (slopes[slot, part] - shared[part])
                d_logits[head, part] = grad.astype(BF)
            halves.append(mm(d_logits[head], keys[:, lanes]))
        heads = slice(2 * pair, 2 * pair + 2)
        stacked = d_logits[heads].reshape(2 * REGION, WINDOW)
        d_keys_t[lanes] = (mm(both_heads(query_t[lanes]), stacked) * 0.125).astype(BF)
        stacked = probs[heads].reshape(2 * REGION, WINDOW)
        d_values_t[lanes] = mm(both_heads(d_att_t[lanes]), stacked).astype(BF)
        d_query[:, lanes] = (jnp.where(lane < 64, halves[0], halves[1]) * 0.125).astype(BF)
    grads = (
        mm(window_t[:, :REGION], d_query[...]).astype(BF),
        mm_nt(window_t[...], d_keys_t[...]).astype(BF),
        mm_nt(window_t[...], d_values_t[...]).astype(BF),
        mm(attended_t[...], d_branch[...]).astype(BF),
    )

    def put(numbers, outs, first):
        for third in range(3):
            flip = (ids[first + third] >> 1) & 31
            for number in numbers:
                for row in range(16):
                    shard = (number & 1) * 16 + row
                    begin = third * 256 + row * 16
                    outs[third][shard ^ flip, 0] = grads[number][begin : begin + 16]

    first = ids[0] == 0

    @pl.when(first)
    def _():
        put((0, 1), keeps, 1)
        put((2, 3), sends, 4)

    @pl.when(jnp.logical_not(first))
    def _():
        put((0, 1), sends, 4)
        put((2, 3), keeps, 1)


def back_call(ids, window, query, keys, values, probs, attended, d_attended, d_branch):
    cols = lambda rows: pl.BlockSpec((rows, COLS), lambda g: (0, g))
    feats = pl.BlockSpec((COLS, WINDOW), lambda g: (g, 0))
    heads = pl.BlockSpec((GROUP, REGION, WINDOW), lambda g: (g, 0, 0))
    return pl.pallas_call(
        back_kernel,
        grid=(2,),
        in_specs=[
            smem(), whole((WINDOW, WIDTH)), cols(REGION), cols(WINDOW), cols(WINDOW), heads,
            cols(REGION), cols(REGION), whole((REGION, WIDTH)), cols(REGION),
        ],
        out_specs=[cols(REGION), feats, feats, heads]
        + [pl.BlockSpec((32, 1, PIECE, COLS), lambda g: (0, g, 0, 0))] * 6,
        out_shape=[
            main((REGION, WIDTH)),
            main((WIDTH, WINDOW)),
            main((WIDTH, WINDOW)),
            main((HEADS, REGION, WINDOW)),
        ]
        + [main((32, 2, PIECE, COLS))] * 6,
        scratch_shapes=[
            pltpu.VMEM((WIDTH, WINDOW), BF),
            pltpu.VMEM((2, REGION, WINDOW), F32),
            pltpu.VMEM((WIDTH, REGION), BF),
        ],
        compiler_params=params(44),
        cost_estimate=cost(6_000_000_000, 30_000_000),
        name="attend_back",
    )(
        ids, here(window), here(query), here(keys), here(values), here(probs), attended, d_attended,
        attended, d_branch,
    )


ROWS = 16
BLOCKS = 4


def table_kernel(d_logits, relative, layout, out, onehot, total):
    step = pl.program_id(0)

    @pl.when(step == 0)
    def _():
        total[...] = jnp.zeros_like(total)

    bucket = lax.broadcasted_iota(jnp.int32, (32, WINDOW), 0)
    added = []
    for block in range(BLOCKS):
        for row in range(ROWS):
            for offset, source in ((0, relative), (32, layout)):
                at = block * ROWS + row
                hit = source[at : at + 1, :] == bucket
                begin = row * 64 + offset
                onehot[block, begin : begin + 32] = jnp.where(hit, 1.0, 0.0).astype(BF)
        rows = slice(block * ROWS, block * ROWS + ROWS)
        left = d_logits[:, rows, :].reshape(HEADS * ROWS, WINDOW)
        added.append(mm_nt(left, onehot[block]))
    total[...] += (added[0] + added[1]) + (added[2] + added[3])

    @pl.when(step == pl.num_programs(0) - 1)
    def _():
        shape = total.shape
        left_row = lax.broadcasted_iota(jnp.int32, shape, 0) % ROWS
        right_row = lax.broadcasted_iota(jnp.int32, shape, 1) // 64
        kept = jnp.where(left_row == right_row, total[...], 0.0)
        by_head = jnp.sum(kept.reshape(HEADS, ROWS, shape[1]), axis=1)
        folded = by_head[:, 0:128]
        for tile in range(1, shape[1] // 128):
            folded = folded + by_head[:, tile * 128 : tile * 128 + 128]
        out[...] = folded[:, :64] + folded[:, 64:]


def table_call(third, d_logits, relative, layout):
    rows = ROWS * BLOCKS
    steps = REGION // 3 // rows
    heads = pl.BlockSpec((HEADS, rows, WINDOW), lambda i: (0, third * steps + i, 0))
    buckets = pl.BlockSpec((rows, WINDOW), lambda i: (third * steps + i, 0))
    return pl.pallas_call(
        table_kernel,
        grid=(steps,),
        in_specs=[heads, buckets, buckets],
        out_specs=whole((HEADS, 64)),
        out_shape=struct((HEADS, 64), F32),
        scratch_shapes=[
            pltpu.VMEM((BLOCKS, ROWS * 64, WINDOW), BF),
            pltpu.VMEM((HEADS * ROWS, ROWS * 64), F32),
        ],
        compiler_params=params(20),
        cost_estimate=cost(2_500_000_000, 4_000_000),
        name="table_grads",
    )(d_logits, relative, layout)


def small_kernel(one, two, three, gain_grad, out):
    out[...] = jnp.zeros_like(out)
    gain = jnp.concatenate([gain_grad[:, row * 64 : row * 64 + 64] for row in range(HEADS)])
    value = jnp.concatenate([one[...] + two[...] + three[...], gain], axis=1)
    value = jnp.concatenate([value, jnp.zeros((PIECE - HEADS, 128), F32)])
    high = value.astype(BF)
    out[0, :, :128] = high
    out[0, :, 128:256] = (value - high.astype(F32)).astype(BF)


def small_call(one, two, three, gain_grad):
    return pl.pallas_call(
        small_kernel,
        in_specs=[pl.BlockSpec(memory_space=pltpu.VMEM)] * 4,
        out_specs=pl.BlockSpec(memory_space=pltpu.VMEM),
        out_shape=struct((1, PIECE, MERGED)),
        compiler_params=params(8),
        name="small_sums",
    )(one, two, three, gain_grad)


def window_kernel(place, d_query, d_keys_t, d_values_t, wq, wk, wv, own, for_row, for_core, for_chip, rest):
    full = mm(wk[...], d_keys_t[...]) + mm(wv[...], d_values_t[...])
    own[...] = (full[:, :REGION] + mm_nt(wq[...], d_query[...])).T
    rest[...] = full[:, REGION:].T
    row, odd = place[7], place[0]
    for out, begin in (
        (for_row, HALO - HALO * row),
        (for_core, 3 * HALO - HALO * odd),
        (for_chip, 2 * HALO + HALO * odd),
    ):
        out[...] = rest[pl.ds(pl.multiple_of(begin, HALO), HALO)].astype(BF)


def window_call(place, d_query, d_keys_t, d_values_t, wq, wk, wv):
    return pl.pallas_call(
        window_kernel,
        in_specs=[smem()] + [pl.BlockSpec(memory_space=pltpu.VMEM)] * 6,
        out_specs=[pl.BlockSpec(memory_space=pltpu.VMEM)] * 4,
        out_shape=[struct((REGION, WIDTH), F32)] + [struct((HALO, WIDTH))] * 3,
        scratch_shapes=[pltpu.VMEM((WINDOW - REGION, WIDTH), F32)],
        compiler_params=params(24),
        cost_estimate=cost(2_300_000_000, 10_000_000),
        name="window_back",
    )(place, d_query, d_keys_t, d_values_t, wq, wk, wv)


def input_kernel(
    place, tokens, gain, index, own, d_middle, from_row, from_core, from_chip, input_grad
):
    row, odd = place[7], place[0]
    back = own[...]
    for received, block in ((from_row, row), (from_core, 2 + odd), (from_chip, 3 - odd)):
        picks = index[pl.ds(block, 1), :]
        chosen = lax.broadcasted_iota(jnp.int32, (REGION, HALO), 0) == picks
        back = back + mm(jnp.where(chosen, 1.0, 0.0).astype(BF), received[...])
    value = tokens[...].astype(F32)
    inverse = lax.rsqrt(jnp.mean(value * value, axis=-1, keepdims=True) + EPS)
    scaled = back * gain[...].reshape(1, WIDTH).astype(F32)
    shared = jnp.mean(scaled * value, axis=-1, keepdims=True)
    input_grad[...] = (
        d_middle[...] + inverse * scaled - value * (inverse * inverse * inverse) * shared
    ).astype(BF)


def input_call(place, tokens, gain, index, own, d_middle, from_row, from_core, from_chip):
    return pl.pallas_call(
        input_kernel,
        in_specs=[smem()] + [pl.BlockSpec(memory_space=pltpu.VMEM)] * 8,
        out_specs=pl.BlockSpec(memory_space=pltpu.VMEM),
        out_shape=struct((REGION, WIDTH)),
        compiler_params=params(16),
        cost_estimate=cost(500_000_000, 6_000_000),
        name="input_back",
    )(place, tokens, gain, index, own, d_middle, from_row, from_core, from_chip)


def halves_kernel(ids, *refs, stage):
    sides = (range(2), range(1), range(1, 2))[stage]
    far = 1 if stage else 0
    units = [(side, k) for side in sides for k in range(3)]
    weights, gain, before, words = refs[0:3], refs[3], refs[4], refs[5:7]
    parts = dict(zip([3 * side + k for side, k in units], refs[7:]))
    skip = 7 + len(units) + (7 if stage else 0)
    outs, gain_out = refs[skip : skip + 7], refs[skip + 7]
    if stage == 2:
        ffn_gain, rel, lay = refs[skip + 8 : skip + 11]
        skip += 3
    weight, wide, tall, att, total, weight_sem, ffn_sem, att_sem = refs[skip + 8 :]

    def place_of(side, k):
        half = ids[0] ^ side
        return 2 * half + (((ids[1 + 3 * side + k] >> 5) & 1) ^ far)

    def weight_copy(side, k, number):
        rows = pl.ds(256 * k, 256)
        unit = 3 * side + k
        return pltpu.make_async_copy(
            weights[number].at[rows], weight.at[unit], weight_sem.at[unit]
        )

    def ffn_copy(side, k):
        begin = pl.multiple_of(place_of(side, k) * TILE, TILE)
        window = pl.ds(begin, TILE)
        if k == 2:
            return pltpu.make_async_copy(tall.at[side], outs[2].at[window], ffn_sem.at[3 * side + 2])
        return pltpu.make_async_copy(
            wide.at[side, k], outs[k].at[:, window], ffn_sem.at[3 * side + k]
        )

    def att_copy(side, k, number):
        rows = pl.ds(256 * k, 256)
        unit = 3 * side + k
        return pltpu.make_async_copy(att.at[unit], outs[3 + number].at[rows], att_sem.at[unit])

    def each_number(side, k, count, act):
        for number in range(count):

            @pl.when(place_of(side, k) == number)
            def _():
                act(number)

    for side, k in units:
        each_number(side, k, 3, lambda number: weight_copy(side, k, number).start())
    total[...] = jnp.zeros_like(total)
    for side, k in units:
        unit = 3 * side + k
        flip = ids[1 + 3 * side + k] & 31
        for piece in range(32):
            block = parts[unit][piece ^ flip, :, :WIDTH].astype(F32)
            if k == 2:
                tall[side, piece * 16 : piece * 16 + 16] = block
                continue
            col, row = piece // 16, piece % 16
            for third in range(3):
                begin = row * 48 + third * 16
                wide[side, k, begin : begin + 16, col * 256 : col * 256 + 256] = block[
                    :, third * 256 : third * 256 + 256
                ]
        ffn_copy(side, k).start()
        flip = flip >> 1
        for row in range(16):
            for group in range(2):
                att[unit, row * 16 : row * 16 + 16, group * COLS : group * COLS + COLS] = parts[unit][
                    (row ^ flip) * 2 + group, :, WIDTH:
                ].astype(F32)
        each_number(side, k, 4, lambda number: att_copy(side, k, number).start())

        def add_gain(number):
            weight_copy(side, k, number).wait()
            product = att[unit] * weight[unit].astype(F32)
            total[:, 256 * k : 256 * k + 256] += lax.dot_general(
                jnp.ones((8, WIDTH), F32), product, (((1,), (1,)), ((), ())),
                precision=lax.Precision.HIGHEST, preferred_element_type=F32,
            )

        each_number(side, k, 3, add_gain)
    if stage == 2:
        sums = total[0:1] + before[...]
        gain_out[...] = (sums / gain[...].reshape(1, WIDTH).astype(F32)).reshape(WIDTH)
        both = [word[0, :, :128].astype(F32) + word[0, :, 128:256].astype(F32) for word in words]
        small = both[0] + both[1]
        ffn_gain[...] = jnp.concatenate(
            [small[row : row + 1, 64:128] for row in range(HEADS)], axis=1
        ).reshape(WIDTH)
        rel[...] = small[:HEADS, 0:32]
        lay[...] = small[:HEADS, 32:64]
    else:
        gain_out[...] = total[0:1] + (before[...] if stage else 0.0)
    for side, k in units:
        ffn_copy(side, k).wait()
        att_copy(side, k, 0).wait()


def halves_call(stage, ids, weights, gain, before, words, parts, firsts=()):
    anywhere = pl.BlockSpec(memory_space=pl.ANY)
    vmem = pl.BlockSpec(memory_space=pltpu.VMEM)
    ends = [struct((WIDTH,), F32), struct((HEADS, 32), F32), struct((HEADS, 32), F32)]
    last = stage == 2
    return pl.pallas_call(
        functools.partial(halves_kernel, stage=stage),
        in_specs=[smem()] + [anywhere] * 3 + [vmem] * (4 + len(parts)) + [anywhere] * len(firsts),
        out_specs=[anywhere] * 7 + [vmem] * (4 if last else 1),
        scratch_shapes=[
            pltpu.VMEM((6, 256, WIDTH), BF),
            pltpu.VMEM((2, 2, WIDTH, TILE), F32),
            pltpu.VMEM((2, TILE, WIDTH), F32),
            pltpu.VMEM((6, 256, WIDTH), F32),
            pltpu.VMEM((8, WIDTH), F32),
            pltpu.SemaphoreType.DMA((6,)),
            pltpu.SemaphoreType.DMA((6,)),
            pltpu.SemaphoreType.DMA((6,)),
        ],
        out_shape=[struct((WIDTH, FF), F32), struct((WIDTH, FF), F32), struct((FF, WIDTH), F32)]
        + [struct((WIDTH, WIDTH), F32)] * 4
        + [struct((WIDTH,) if last else (1, WIDTH), F32)]
        + (ends if last else []),
        input_output_aliases={8 + len(parts) + k: k for k in range(len(firsts))},
        compiler_params=params(28),
        cost_estimate=cost(10_000_000, 24_000_000),
        name=("outputs_near", "outputs_far_own", "outputs_far_other")[stage],
    )(ids, *weights, gain, before, *words, *parts, *firsts)


AXES = ("row", "col")
OTHER_PAIRS = {0: 3, 3: 0, 1: 2, 2: 1}


def ring_pairs(axes, bit):
    pairs = []
    for chip in range(64):
        for core in range(2):
            spot = [chip // 16, chip // 4 % 4, chip % 4]
            first = (bit + core) % 2 == 0
            for axis in axes:
                spot[axis] = spot[axis] ^ 1 if first else OTHER_PAIRS[spot[axis]]
            partner = (spot[0] * 4 + spot[1]) * 4 + spot[2]
            pairs.append((2 * chip + core, 2 * partner + core))
    return pairs


CORE_PAIRS = [(d, d ^ 1) for d in range(SHARDS)]


def swap(value, pairs):
    return lax.ppermute(value, AXES, pairs)


def added(mine, received):
    return (mine.astype(F32) + received.astype(F32)).astype(BF)


def after(first, *values):
    held = lax.optimization_barrier((first, values))[1]
    return held[0] if len(values) == 1 else held


def words_sum(one, two):
    one_value, two_value = (v[..., :128].astype(F32) + v[..., 128:256].astype(F32) for v in (one, two))
    value = one_value + two_value
    high = value.astype(BF)
    low = (value - high.astype(F32)).astype(BF)
    return jnp.concatenate([high, low, jnp.zeros(one.shape[:2] + (MERGED - 256,), BF)], axis=-1)


def body(
    tokens, attn_gain, query_weight, key_weight, value_weight, output_weight, ffn_gain, gate_weight,
    up_weight, down_weight, relative_table, layout_table, cotangent, rel_bucket, layout_bucket,
    halo_index,
):
    tokens, cotangent = tokens[0], cotangent[0]
    relative, layout = rel_bucket[0], layout_bucket[0]
    index = halo_index[0, 0]
    columns = lax.axis_size("col")
    row_pairs = [(0, 1), (1, 0)]
    core_pairs = [(c, c ^ 1) for c in range(columns)]
    chip_pairs = [p for c in range(1, columns - 1, 2) for p in ((c, c + 1), (c + 1, c))]

    exchange_row = lambda v: lax.ppermute(v, "row", row_pairs)
    exchange_core = lambda v: lax.ppermute(v, "col", core_pairs)
    exchange_chip = lambda v: lax.ppermute(v, "col", chip_pairs)

    def ring(axis, bit):
        return ring_pairs((axis,), bit)

    normed, *sends, ids = norm_call(tokens, attn_gain, index)
    received = (exchange_row(sends[0]), exchange_core(sends[1]), exchange_chip(sends[2]))
    bias = bias_call(relative_table, layout_table, relative, layout)
    cotangent_other = swap(cotangent, CORE_PAIRS)
    window, query, keys, values, probs, attended = attend_call(
        ids, normed, *received, query_weight, key_weight, value_weight, bias, 4
    )
    (
        layer_out, d_middle, d_attended, d_branch, gain_two_grad, normed_two, *halves
    ) = ffn_call(
        ids, tokens, attended, output_weight, ffn_gain, cotangent, gate_weight, up_weight, down_weight
    )
    mixed_send, mixed, gate_send, d_gate, up_send, d_up = halves
    normed_two_other, mixed_other, d_gate_other, d_up_other = [
        swap(v, CORE_PAIRS) for v in (normed_two, mixed_send, gate_send, up_send)
    ]
    d_query, d_keys_t, d_values_t, d_logits, *att = back_call(
        ids, window, query, keys, values, probs, attended, d_attended, d_branch
    )
    att_other = [swap(v, CORE_PAIRS) for v in att[:3]]
    normed_two = after(d_query, normed_two)
    merged = grads_call(
        ids, normed_two, normed_two_other, cotangent, cotangent_other,
        (d_gate, d_gate_other, d_up, d_up_other, mixed, mixed_other), att[3:],
    )
    merged = merge_call(att_other, merged)
    sent, kept = list(merged[:3]), list(merged[3:])

    last = tuple(sent)
    got = [swap(sent[k], ring(k, 0)) for k in range(3)]
    tables = []
    for third in range(2):
        tables.append(table_call(third, d_logits, after(last, relative), layout))
        last = tables[-1]

    def halve(turn, got):
        half = kept[0].shape[0] // 2
        sent = [added(kept[k][half:], got[k][half:]) for k in range(3)]
        for k in range(3):
            kept[k] = added(kept[k][:half], got[k][:half])
        return tuple(sent), [swap(sent[k], ring((k + turn) % 3, 0)) for k in range(3)]

    own, *returns = window_call(
        ids, d_query, d_keys_t, d_values_t, query_weight, key_weight, after(last, value_weight)
    )
    last, got = halve(1, after(own, *got))
    tables.append(table_call(2, d_logits, after(last, relative), layout))
    last, got = halve(2, after(tables[-1], *got))
    small = small_call(*tables, after(last, gain_two_grad))
    got = after(small, *got)
    quarters = [
        jnp.stack([added(kept[k][2 * q : 2 * q + 2], got[k][2 * q : 2 * q + 2]) for k in range(3)])
        .reshape(6, PIECE, MERGED)
        for q in range(4)
    ]
    partners = {1: ring_pairs((1,), 1), 2: ring_pairs((0,), 1), 3: ring_pairs((0, 1), 1)}
    quarters[1] = jnp.concatenate([quarters[1], small])
    quarters[3] = after((quarters[1], quarters[2]), quarters[3])
    got = {q: swap(quarters[q], partners[q]) for q in (1, 2, 3)}
    mine = (
        (quarters[0].astype(F32) + got[1][:6].astype(F32))
        + (got[2].astype(F32) + got[3].astype(F32))
    ).astype(BF)
    small = words_sum(small, got[1][6:])
    got = swap(jnp.concatenate([mine, small]), ring(2, 1))
    mine = added(mine, got[:6])
    small = words_sum(small, got[6:])
    with_small = jnp.concatenate([mine, small])
    got = {q: swap(with_small if q == 2 else mine, partners[q]) for q in (1, 2, 3)}
    small = words_sum(small, got[2][6:])
    four = [v[:6].reshape(3, 2, PIECE, MERGED) for v in (mine, got[1], got[2], got[3])]
    near = [jnp.concatenate([v[k] for v in four]) for k in range(3)]
    for turn in (2, 1, 0):
        near[0] = jnp.concatenate([near[0], small])
        last = tuple(near)
        got = [swap(near[k], ring((k + turn) % 3, 0)) for k in range(3)]
        if turn == 0:
            break
        if turn == 1:
            returns = after(last, *returns)
            from_row, from_chip = exchange_row(returns[0]), exchange_chip(returns[2])
            *got, from_row, from_chip = after(last, *got, from_row, from_chip)
        got = after(last, *got)
        small = words_sum(small, got[0][-1:])
        near = [jnp.concatenate([near[k][: got[1].shape[0]], got[k][: got[1].shape[0]]]) for k in range(3)]
    near_other = [swap(near[k], CORE_PAIRS) for k in range(3)]
    weights = (query_weight, key_weight, value_weight)
    common = (ids, weights, attn_gain)
    *outs, gain_part = halves_call(
        0, *common, gain_two_grad, (small, small), (*near, *near_other)
    )
    from_core = exchange_core(after(gain_part, returns[1]))
    input_grad = input_call(
        ids, after(gain_part, tokens), attn_gain, index, own, d_middle, from_row, from_core, from_chip
    )
    far, far_other, last = [], [], input_grad
    for k in range(3):
        far.append(after(last, got[k]))
        if k == 0:
            small = words_sum(small, far[0][-1:])
            small_other = swap(small, CORE_PAIRS)
        far_other.append(swap(far[k], CORE_PAIRS))
        last = far[k]
    words = (small, small)
    *outs, gain_part = halves_call(1, *common, gain_part, words, far, outs)
    words = (small, small_other)
    *outs, gain_one, gain_two, relative_grad, layout_grad = halves_call(
        2, *common, gain_part, words, after(gain_part, *far_other), outs
    )
    gate_grad, up_grad, down_grad, query_grad, key_grad, value_grad, output_grad = outs
    return (
        layer_out[None], input_grad[None], gain_one, query_grad, key_grad, value_grad,
        output_grad, gain_two, gate_grad, up_grad, down_grad, relative_grad.T, layout_grad.T,
    )


def solution(mesh):
    tokens = P("row", "col", None)
    whole_array = P()
    return jax.shard_map(
        body,
        mesh=mesh,
        in_specs=(tokens,) + (whole_array,) * 11 + (tokens,) * 3 + (P("row", "col", None, None),),
        out_specs=(tokens, tokens) + (whole_array,) * 11,
        check_vma=False,
    )
```

```python
import functools

import jax
import jax.numpy as jnp
from jax import lax
from jax.experimental import pallas as pl
from jax.experimental.pallas import tpu as pltpu
from jax.sharding import PartitionSpec as P

BF = jnp.bfloat16
F32 = jnp.float32
EPS = 1e-06
LOG2E = 1.4426950408889634
REGION = 384
WIDTH = 768
WINDOW = 768
HEADS = 12
HALO = 96
FF = 2048


def params(mib):
    return pltpu.CompilerParams(vmem_limit_bytes=mib * 2**20)


def cost(flops, moved, transcendentals=0):
    return pl.CostEstimate(flops=flops, bytes_accessed=moved, transcendentals=transcendentals)


def smem():
    return pl.BlockSpec(memory_space=pltpu.SMEM)


def whole(shape):
    return pl.BlockSpec(shape, lambda *_: (0,) * len(shape))


def mm(a, b):
    return jnp.dot(a, b, preferred_element_type=F32)


def mm_nt(a, b):
    return lax.dot_general(a, b, (((1,), (1,)), ((), ())), preferred_element_type=F32)


def mm_tn(a, b):
    return lax.dot_general(a, b, (((0,), (0,)), ((), ())), preferred_element_type=F32)


def struct(shape, dtype=BF):
    return jax.ShapeDtypeStruct(shape, dtype)


def near_by(shape, dtype=BF):
    return pltpu.VMEM(shape, dtype)


def main(shape, dtype=BF):
    return pltpu.HBM(shape, dtype)


def here(value):
    return pltpu.with_memory_space_constraint(value, pltpu.HBM)


def norm_kernel(tokens, gain, index, normed, send_row, send_core, send_chip, ids):
    value = tokens[...].astype(F32)
    inverse = lax.rsqrt(jnp.mean(value * value, axis=-1, keepdims=True) + EPS)
    low = (value * inverse * gain[...].reshape(1, WIDTH).astype(F32)).astype(BF)
    normed[...] = low
    row, col = lax.axis_index("row"), lax.axis_index("col")
    core = col & 1
    for out, block in ((send_row, row), (send_core, 2 + core), (send_chip, 3 - core)):
        picks = index[pl.ds(block, 1), :]
        chosen = lax.broadcasted_iota(jnp.int32, (REGION, HALO), 0) == picks
        out[...] = mm_tn(jnp.where(chosen, 1.0, 0.0).astype(BF), low).astype(BF)
    spots = (2 * row + (col >> 5), (col >> 3) & 3, (col >> 1) & 3)
    near = [((v + 1) >> 1) & 1 for v in spots]
    far = [v >> 1 for v in spots]
    ids[0] = core
    ids[7] = row
    for other in range(2):
        side = core ^ other
        first = [jnp.where(side == 1, f, n) for n, f in zip(near, far)]
        second = [jnp.where(side == 1, n, f) for n, f in zip(near, far)]
        for chunk in range(3):
            turned = [first[(chunk + turn) % 3] for turn in range(3)]
            ids[1 + 3 * other + chunk] = (
                turned[0] * 32 + turned[1] * 16 + turned[2] * 8 + second[0] * 4 + second[1] * 2
            )


def norm_call(tokens, gain, index):
    vmem = pl.BlockSpec(memory_space=pltpu.VMEM)
    return pl.pallas_call(
        norm_kernel,
        out_shape=(struct((REGION, WIDTH)),) + (struct((HALO, WIDTH)),) * 3 + (struct((8,), jnp.int32),),
        in_specs=[vmem] * 3,
        out_specs=(vmem,) * 4 + (smem(),),
        compiler_params=params(56),
        cost_estimate=cost(700_000_000, 2_000_000),
        name="norm_one",
    )(tokens, gain, index)


STEP = 2.0**-11
SHIFT = 9000
MASKED = -(2**31)
ROW_BLOCK = 32


def bias_kernel(relative_table, layout_table, relative, layout, out, table):
    rows = relative.shape[0]

    @pl.when(pl.program_id(0) == 0)
    def _():
        for number, source in enumerate((relative_table, layout_table)):
            values = jnp.round(source[...].astype(F32) * (LOG2E / STEP))
            fixed = jnp.concatenate([values, jnp.zeros((4, 32), F32)]).T.astype(jnp.int32)
            for pair in range(HEADS // 2):
                high = jnp.broadcast_to(fixed[:, 2 * pair : 2 * pair + 1], (32, 128))
                low = jnp.broadcast_to(fixed[:, 2 * pair + 1 : 2 * pair + 2], (32, 128))
                table[pair, number] = high * 65536 + (low + SHIFT)

    def look(words, low, bit3, bit4):
        four = [jnp.take_along_axis(words[8 * k : 8 * k + 8], low, axis=0) for k in range(4)]
        return jnp.where(
            bit4, jnp.where(bit3, four[3], four[2]), jnp.where(bit3, four[1], four[0])
        )

    def step(number, carry):
        begin = pl.multiple_of(number * 8, 8)
        for tile in range(WINDOW // 128):
            lanes = slice(tile * 128, tile * 128 + 128)
            rel = relative[pl.ds(begin, 8), lanes]
            lay = layout[pl.ds(begin, 8), lanes]
            rel_low, lay_low = rel & 7, lay & 7
            rel3, rel4 = (rel & 8) != 0, (rel & 16) != 0
            lay3, lay4 = (lay & 8) != 0, (lay & 16) != 0
            masked = rel >= 32
            for pair in range(HEADS // 2):
                word = look(table[pair, 0], rel_low, rel3, rel4)
                word = word + look(table[pair, 1], lay_low, lay3, lay4)
                out[pair, pl.ds(begin, 8), lanes] = jnp.where(masked, MASKED, word)
        return carry

    lax.fori_loop(0, rows // 8, step, 0)


def bias_call(relative_table, layout_table, relative, layout):
    block = 128
    buckets = pl.BlockSpec((block, WINDOW), lambda i: (i, 0))
    return pl.pallas_call(
        bias_kernel,
        grid=(REGION // block,),
        out_shape=struct((HEADS // 2, REGION, WINDOW), jnp.int32),
        in_specs=[whole((HEADS, 32)), whole((HEADS, 32)), buckets, buckets],
        out_specs=pl.BlockSpec((HEADS // 2, block, WINDOW), lambda i: (0, i, 0)),
        scratch_shapes=[pltpu.VMEM((HEADS // 2, 2, 32, 128), jnp.int32)],
        compiler_params=params(24),
        cost_estimate=cost(100_000_000, 17_000_000),
        name="bias",
    )(relative_table.T, layout_table.T, relative, layout)


def attend_kernel(
    place, normed, from_row, from_core, from_chip, wq, wk, wv, bias,
    window, query, keys, values, probs, attended, scores,
):
    width = wq.shape[1]

    @pl.when(pl.program_id(0) == 0)
    def _():
        row, odd = place[7], place[0]
        window[:REGION] = normed[...]
        window[REGION : REGION + 2 * HALO] = jnp.zeros((2 * HALO, WIDTH), BF)
        window[pl.ds(pl.multiple_of(REGION + HALO - HALO * row, HALO), HALO)] = from_row[...]
        window[pl.ds(pl.multiple_of(REGION + 3 * HALO - HALO * odd, HALO), HALO)] = from_core[...]
        window[pl.ds(pl.multiple_of(REGION + 2 * HALO + HALO * odd, HALO), HALO)] = from_chip[...]

    rows = window[...]
    query[...] = mm(rows[:REGION], wq[...]).astype(BF)
    keys[...] = mm(rows, wk[...]).astype(BF)
    lane = lax.broadcasted_iota(jnp.int32, (REGION, 128), 1)
    pairs = width // 128

    def score(pair):
        lanes = slice(pair * 128, pair * 128 + 128)
        for half in range(2):
            mine = (lane < 64) if half == 0 else (lane >= 64)
            one = jnp.where(mine, query[:, lanes], jnp.zeros((), BF))
            scores[2 * (pair % 2) + half] = mm_nt(one, keys[:, lanes])

    def soften(pair, half, begin):
        part = slice(begin, begin + ROW_BLOCK)
        word = bias[pair, part]
        fixed = (word >> 16) if half == 0 else (word & 0xFFFF)
        logits = scores[2 * (pair % 2) + half, part] * (0.125 * LOG2E) + fixed.astype(F32) * STEP
        logits = jnp.where(word == MASKED, -1.5e9, logits)
        highest = jnp.max(logits, axis=-1, keepdims=True)
        powered = jnp.exp2(logits - highest)
        total = jnp.sum(powered, axis=-1, keepdims=True)
        probs[2 * pair + half, part] = (powered * (1.0 / total)).astype(BF)

    score(0)
    values[...] = mm(rows, wv[...]).astype(BF)
    for pair in range(pairs):
        if pair + 1 < pairs:
            score(pair + 1)
        for begin in range(0, REGION, ROW_BLOCK):
            for half in range(2):
                soften(pair, half, begin)
        lanes = slice(pair * 128, pair * 128 + 128)
        halves = [mm(probs[2 * pair + half], values[:, lanes]) for half in range(2)]
        attended[:, lanes] = jnp.where(lane < 64, halves[0], halves[1]).astype(BF)


def attend_call(place, normed, from_row, from_core, from_chip, wq, wk, wv, bias, group):
    count = HEADS // group
    width = group * 64
    cols = lambda rows: pl.BlockSpec((rows, width), lambda g: (0, g))
    return pl.pallas_call(
        attend_kernel,
        grid=(count,),
        out_shape=(
            main((WINDOW, WIDTH)),
            main((REGION, WIDTH)),
            main((WINDOW, WIDTH)),
            main((WINDOW, WIDTH)),
            main((HEADS, REGION, WINDOW)),
            near_by((REGION, WIDTH)),
        ),
        in_specs=[smem(), whole((REGION, WIDTH))]
        + [whole((HALO, WIDTH))] * 3
        + [cols(WIDTH)] * 3
        + [pl.BlockSpec((group // 2, REGION, WINDOW), lambda g: (g, 0, 0))],
        out_specs=(
            whole((WINDOW, WIDTH)),
            cols(REGION),
            cols(WINDOW),
            cols(WINDOW),
            pl.BlockSpec((group, REGION, WINDOW), lambda g: (g, 0, 0)),
            cols(REGION),
        ),
        scratch_shapes=[pltpu.VMEM((4, REGION, WINDOW), F32)],
        compiler_params=params(40),
        cost_estimate=cost(3_500_000_000, 30_000_000, 3_600_000),
        name="attend",
    )(place, normed, from_row, from_core, from_chip, wq, wk, wv, bias)


SHARDS = 128
HALF = 64
TILE = 512
PIECE = 16
MERGED = 1152


def inverse_of(value):
    return lax.rsqrt(jnp.mean(value * value, axis=-1, keepdims=True) + EPS)


def ffn_kernel(
    ids, tokens, attended, wo, gain, cotangent, wg, wu, wd,
    layer_out, d_middle, d_attended, d_branch, gain_grad, normed,
    mixed_send, mixed_keep, gate_send, gate_keep, up_send, up_keep,
    middle, total_out, total_back,
):
    step = pl.program_id(0)

    @pl.when(step == 0)
    def _():
        value = tokens[...].astype(F32) + mm(attended[...], wo[...])
        middle[...] = value
        normed[...] = (value * inverse_of(value) * gain[...].reshape(1, WIDTH).astype(F32)).astype(BF)
        total_out[...] = value
        total_back[...] = jnp.zeros_like(total_back)

    low = normed[...]
    gate = mm(low, wg[...])
    up_part = mm(low, wu[...])
    d_mixed = mm_nt(cotangent[...], wd[...])
    curve = jnp.tanh(gate * (0.7978845608 + (0.7978845608 * 0.044715) * (gate * gate)))
    half_up = 0.5 * (1.0 + curve)
    act = gate * half_up
    slope = half_up + 0.5 * gate * (1.0 - curve * curve) * (
        0.7978845608 + (3 * 0.7978845608 * 0.044715) * gate * gate
    )
    mixed = (act * up_part).astype(BF)
    d_gate = (d_mixed * up_part * slope).astype(BF)
    d_up = (d_mixed * act).astype(BF)
    total_out[...] += mm(mixed, wd[...])
    total_back[...] += mm_nt(d_gate, wg[...]) + mm_nt(d_up, wu[...])

    @pl.when(step < 2)
    def _():
        mixed_send[...] = mixed
        gate_send[...] = d_gate
        up_send[...] = d_up

    @pl.when(step >= 2)
    def _():
        mixed_keep[...] = mixed
        gate_keep[...] = d_gate
        up_keep[...] = d_up

    @pl.when(step == 3)
    def _():
        layer_out[...] = total_out[...].astype(BF)
        value = middle[...]
        inverse = inverse_of(value)
        back = total_back[...]
        gain_grad[...] = jnp.sum(back * value * inverse, axis=0, keepdims=True)
        scaled = back * gain[...].reshape(1, WIDTH).astype(F32)
        shared = jnp.mean(scaled * value, axis=-1, keepdims=True)
        whole_grad = (
            cotangent[...].astype(F32)
            + inverse * scaled
            - value * (inverse * inverse * inverse) * shared
        )
        d_middle[...] = whole_grad
        branch = whole_grad.astype(BF)
        d_branch[...] = branch
        d_attended[...] = mm_nt(branch, wo[...]).astype(BF)


def ffn_call(ids, tokens, attended, wo, gain, cotangent, wg, wu, wd):
    def tile(g, ids):
        return jnp.where(g < 2, 1 - ids[0], ids[0]) * 2 + (g & 1)

    cols = pl.BlockSpec((WIDTH, TILE), lambda g, ids: (0, tile(g, ids)))
    sent = pl.BlockSpec((REGION, TILE), lambda g, ids: (0, jnp.minimum(g, 1)))
    kept = pl.BlockSpec((REGION, TILE), lambda g, ids: (0, jnp.maximum(g - 2, 0)))
    full = whole((REGION, WIDTH))
    return pl.pallas_call(
        ffn_kernel,
        grid_spec=pltpu.PrefetchScalarGridSpec(
            num_scalar_prefetch=1,
            grid=(FF // TILE,),
            in_specs=[
                full, full, whole((WIDTH, WIDTH)), whole((WIDTH,)), full, cols, cols,
                pl.BlockSpec((TILE, WIDTH), lambda g, ids: (tile(g, ids), 0)),
            ],
            out_specs=[full, full, full, full, whole((1, WIDTH)), full]
            + [sent, kept, sent, kept, sent, kept],
            scratch_shapes=[pltpu.VMEM((REGION, WIDTH), F32)] * 3,
        ),
        out_shape=[
            main((REGION, WIDTH)),
            main((REGION, WIDTH), F32),
            near_by((REGION, WIDTH)),
            near_by((REGION, WIDTH)),
            main((1, WIDTH), F32),
            main((REGION, WIDTH)),
        ]
        + [main((REGION, FF // 2))] * 6,
        compiler_params=params(36),
        cost_estimate=cost(8_000_000_000, 20_000_000, 800_000),
        name="feed_forward",
    )(ids, tokens, attended, wo, gain, cotangent, wg, here(wu), here(wd))


def grads_kernel(ids, *refs):
    normeds, cots = refs[0:2], refs[2:4]
    hidden = (refs[4:6], refs[6:8], refs[8:10])
    att, outs = refs[10:13], refs[13:19]
    normed, grad_out, right, normed_t, kept, in_sem = refs[19:]

    def pair_in(sources, target, number):
        return [
            pltpu.make_async_copy(
                sources[k], target.at[k * REGION : k * REGION + REGION], in_sem.at[number]
            )
            for k in range(2)
        ]

    copies = [pair_in(normeds, normed, 0)]
    copies += [pair_in(hidden[k], right.at[k], 1 + k) for k in range(3)]
    copies += [pair_in(cots, grad_out, 4)]
    copies += [[pltpu.make_async_copy(att[k], kept.at[k], in_sem.at[5]) for k in range(3)]]
    for number in (0, 1, 5, 2, 4, 3):
        for copy in copies[number]:
            copy.start()

    def wait(number):
        for copy in copies[number]:
            copy.wait()

    def put(out, k, grad, flip):
        for piece in range(32):
            col, row = piece // 16, piece % 16
            if k == 2:
                out[piece ^ flip, :, :WIDTH] = grad[piece * 16 : piece * 16 + 16]
                continue
            for third in range(3):
                begin = row * 48 + third * 16
                out[piece ^ flip, :, third * 256 : third * 256 + 256] = grad[
                    begin : begin + 16, col * 256 : col * 256 + 256
                ]

    wait(0)
    normed_t[...] = normed[...].T
    for k in range(3):
        wait(1 + k)
        if k == 2:
            wait(4)
        place = ids[1 + k]
        top, flip = (place >> 5) & 1, place & 31
        for tile in range(2):
            cols = slice(tile * TILE, tile * TILE + TILE)
            if k < 2:
                grad = mm(normed_t[...], right[k, :, cols]).astype(BF)
            else:
                grad = mm_tn(right[k, :, cols], grad_out[...]).astype(BF)
            away = top != tile

            @pl.when(away)
            def _():
                put(outs[k], k, grad, flip)

            @pl.when(jnp.logical_not(away))
            def _():
                put(outs[3 + k], k, grad, flip)

        if k == 0:
            wait(5)
        for spot in range(32):
            out = outs[3 * (1 - spot // 16) + k]
            for group in range(2):
                out[(spot % 16) * 2 + group, :, WIDTH:] = kept[k, spot, group]


def grads_call(ids, normed, normed_other, cotangent, cotangent_other, pairs, att):
    merged = (32, PIECE, MERGED)
    anywhere = pl.BlockSpec(memory_space=pl.ANY)
    vmem = pl.BlockSpec(memory_space=pltpu.VMEM)
    pairs = [here(v) if k % 2 == 0 else v for k, v in enumerate(pairs)]
    return pl.pallas_call(
        grads_kernel,
        in_specs=[smem()] + [anywhere] * 13,
        out_specs=[vmem] * 6,
        scratch_shapes=[
            pltpu.VMEM((2 * REGION, WIDTH), BF),
            pltpu.VMEM((2 * REGION, WIDTH), BF),
            pltpu.VMEM((3, 2 * REGION, FF // 2), BF),
            pltpu.VMEM((WIDTH, 2 * REGION), BF),
            pltpu.VMEM((3, 32, 2, PIECE, COLS), BF),
            pltpu.SemaphoreType.DMA((6,)),
        ],
        out_shape=[near_by(merged)] * 6,
        compiler_params=params(20),
        cost_estimate=cost(3_700_000_000, 16_000_000),
        name="feed_forward_grads",
    )(
        ids, here(normed), normed_other, here(cotangent), cotangent_other, *pairs, *map(here, att)
    )


def merge_kernel(*refs, side):
    att_other, pieces, outs = refs[0:3], refs[3:6], refs[6:9]
    for k in range(3):
        half = att_other[k][16 - 16 * side : 32 - 16 * side].astype(F32)
        total = pieces[k][:, :, WIDTH:].astype(F32) + half.reshape(32, PIECE, COLS)
        outs[k][:, :, WIDTH:] = total.astype(BF)


def merge_call(side, att_other, pieces):
    vmem = pl.BlockSpec(memory_space=pltpu.VMEM)
    return pl.pallas_call(
        functools.partial(merge_kernel, side=side),
        in_specs=[vmem] * 6,
        out_specs=[vmem] * 3,
        out_shape=[near_by((32, PIECE, MERGED))] * 3,
        input_output_aliases={3 + number: number for number in range(3)},
        compiler_params=params(8),
        cost_estimate=cost(5_000_000, 5_000_000),
        name="merge_cores",
    )(*att_other, *pieces)


GROUP = 6
COLS = GROUP * 64


def back_kernel(
    ids, window, query, keys, values, probs, attended, d_attended, attended_all, d_branch, *refs
):
    d_query, d_keys_t, d_values_t, d_logits = refs[:4]
    sends, keeps = refs[4:7], refs[7:10]
    window_t, slopes, attended_t = refs[10:]

    @pl.when(pl.program_id(0) == 0)
    def _():
        window_t[...] = window[...].T
        attended_t[...] = attended_all[...].T

    query_t = query[...].T
    d_att_t = d_attended[...].T
    nothing = jnp.zeros((64, REGION), BF)

    def both_heads(rows):
        return jnp.concatenate(
            [
                jnp.concatenate([rows[:64], nothing], axis=1),
                jnp.concatenate([nothing, rows[64:]], axis=1),
            ]
        )

    lane = lax.broadcasted_iota(jnp.int32, (REGION, 128), 1)
    for pair in range(GROUP // 2):
        lanes = slice(pair * 128, pair * 128 + 128)
        halves = []
        for half in range(2):
            head = 2 * pair + half
            mine = (lane < 64) if half == 0 else (lane >= 64)
            one = jnp.where(mine, d_attended[:, lanes], jnp.zeros((), BF))
            shared = jnp.sum(
                one.astype(F32) * attended[:, lanes].astype(F32), axis=-1, keepdims=True
            )
            slot = head % 2
            slopes[slot] = mm_nt(one, values[:, lanes])
            for begin in range(0, REGION, 32):
                part = slice(begin, begin + 32)
                grad = probs[head, part].astype(F32) * (slopes[slot, part] - shared[part])
                d_logits[head, part] = grad.astype(BF)
            halves.append(mm(d_logits[head], keys[:, lanes]))
        heads = slice(2 * pair, 2 * pair + 2)
        stacked = d_logits[heads].reshape(2 * REGION, WINDOW)
        d_keys_t[lanes] = (mm(both_heads(query_t[lanes]), stacked) * 0.125).astype(BF)
        stacked = probs[heads].reshape(2 * REGION, WINDOW)
        d_values_t[lanes] = mm(both_heads(d_att_t[lanes]), stacked).astype(BF)
        d_query[:, lanes] = (jnp.where(lane < 64, halves[0], halves[1]) * 0.125).astype(BF)
    grads = (
        mm(window_t[:, :REGION], d_query[...]).astype(BF),
        mm_nt(window_t[...], d_keys_t[...]).astype(BF),
        mm_nt(window_t[...], d_values_t[...]).astype(BF),
        mm(attended_t[...], d_branch[...]).astype(BF),
    )

    def put(numbers, outs, first):
        for third in range(3):
            flip = (ids[first + third] >> 1) & 31
            for number in numbers:
                for row in range(16):
                    shard = (number & 1) * 16 + row
                    begin = third * 256 + row * 16
                    outs[third][shard ^ flip, 0] = grads[number][begin : begin + 16]

    first = ids[0] == 0

    @pl.when(first)
    def _():
        put((0, 1), keeps, 1)
        put((2, 3), sends, 4)

    @pl.when(jnp.logical_not(first))
    def _():
        put((0, 1), sends, 4)
        put((2, 3), keeps, 1)


def back_call(ids, window, query, keys, values, probs, attended, d_attended, d_branch):
    cols = lambda rows: pl.BlockSpec((rows, COLS), lambda g: (0, g))
    feats = pl.BlockSpec((COLS, WINDOW), lambda g: (g, 0))
    heads = pl.BlockSpec((GROUP, REGION, WINDOW), lambda g: (g, 0, 0))
    return pl.pallas_call(
        back_kernel,
        grid=(2,),
        in_specs=[
            smem(), whole((WINDOW, WIDTH)), cols(REGION), cols(WINDOW), cols(WINDOW), heads,
            cols(REGION), cols(REGION), whole((REGION, WIDTH)), cols(REGION),
        ],
        out_specs=[cols(REGION), feats, feats, heads]
        + [pl.BlockSpec((32, 1, PIECE, COLS), lambda g: (0, g, 0, 0))] * 6,
        out_shape=[
            main((REGION, WIDTH)),
            main((WIDTH, WINDOW)),
            main((WIDTH, WINDOW)),
            main((HEADS, REGION, WINDOW)),
        ]
        + [main((32, 2, PIECE, COLS))] * 6,
        scratch_shapes=[
            pltpu.VMEM((WIDTH, WINDOW), BF),
            pltpu.VMEM((2, REGION, WINDOW), F32),
            pltpu.VMEM((WIDTH, REGION), BF),
        ],
        compiler_params=params(44),
        cost_estimate=cost(6_000_000_000, 30_000_000),
        name="attend_back",
    )(
        ids, here(window), here(query), here(keys), here(values), here(probs), attended, d_attended,
        attended, d_branch,
    )


ROWS = 16
BLOCKS = 4


def table_kernel(d_logits, relative, layout, out, onehot, total):
    step = pl.program_id(0)

    @pl.when(step == 0)
    def _():
        total[...] = jnp.zeros_like(total)

    bucket = lax.broadcasted_iota(jnp.int32, (32, WINDOW), 0)
    added = []
    for block in range(BLOCKS):
        for row in range(ROWS):
            for offset, source in ((0, relative), (32, layout)):
                at = block * ROWS + row
                hit = source[at : at + 1, :] == bucket
                begin = row * 64 + offset
                onehot[block, begin : begin + 32] = jnp.where(hit, 1.0, 0.0).astype(BF)
        rows = slice(block * ROWS, block * ROWS + ROWS)
        left = d_logits[:, rows, :].reshape(HEADS * ROWS, WINDOW)
        added.append(mm_nt(left, onehot[block]))
    total[...] += (added[0] + added[1]) + (added[2] + added[3])

    @pl.when(step == pl.num_programs(0) - 1)
    def _():
        shape = total.shape
        left_row = lax.broadcasted_iota(jnp.int32, shape, 0) % ROWS
        right_row = lax.broadcasted_iota(jnp.int32, shape, 1) // 64
        kept = jnp.where(left_row == right_row, total[...], 0.0)
        by_head = jnp.sum(kept.reshape(HEADS, ROWS, shape[1]), axis=1)
        folded = by_head[:, 0:128]
        for tile in range(1, shape[1] // 128):
            folded = folded + by_head[:, tile * 128 : tile * 128 + 128]
        out[...] = folded[:, :64] + folded[:, 64:]


def table_call(third, d_logits, relative, layout):
    rows = ROWS * BLOCKS
    steps = REGION // 3 // rows
    heads = pl.BlockSpec((HEADS, rows, WINDOW), lambda i: (0, third * steps + i, 0))
    buckets = pl.BlockSpec((rows, WINDOW), lambda i: (third * steps + i, 0))
    return pl.pallas_call(
        table_kernel,
        grid=(steps,),
        in_specs=[heads, buckets, buckets],
        out_specs=whole((HEADS, 64)),
        out_shape=struct((HEADS, 64), F32),
        scratch_shapes=[
            pltpu.VMEM((BLOCKS, ROWS * 64, WINDOW), BF),
            pltpu.VMEM((HEADS * ROWS, ROWS * 64), F32),
        ],
        compiler_params=params(20),
        cost_estimate=cost(2_500_000_000, 4_000_000),
        name="table_grads",
    )(d_logits, relative, layout)


def small_kernel(one, two, three, gain_grad, out):
    out[...] = jnp.zeros_like(out)
    gain = jnp.concatenate([gain_grad[:, row * 64 : row * 64 + 64] for row in range(HEADS)])
    value = jnp.concatenate([one[...] + two[...] + three[...], gain], axis=1)
    value = jnp.concatenate([value, jnp.zeros((PIECE - HEADS, 128), F32)])
    high = value.astype(BF)
    out[0, :, :128] = high
    out[0, :, 128:256] = (value - high.astype(F32)).astype(BF)


def small_call(one, two, three, gain_grad):
    return pl.pallas_call(
        small_kernel,
        in_specs=[pl.BlockSpec(memory_space=pltpu.VMEM)] * 4,
        out_specs=pl.BlockSpec(memory_space=pltpu.VMEM),
        out_shape=struct((1, PIECE, MERGED)),
        compiler_params=params(8),
        name="small_sums",
    )(one, two, three, gain_grad)


def window_kernel(place, d_query, d_keys_t, d_values_t, wq, wk, wv, own, for_row, for_core, for_chip, rest):
    full = mm(wk[...], d_keys_t[...]) + mm(wv[...], d_values_t[...])
    own[...] = (full[:, :REGION] + mm_nt(wq[...], d_query[...])).T
    rest[...] = full[:, REGION:].T
    row, odd = place[7], place[0]
    for out, begin in (
        (for_row, HALO - HALO * row),
        (for_core, 3 * HALO - HALO * odd),
        (for_chip, 2 * HALO + HALO * odd),
    ):
        out[...] = rest[pl.ds(pl.multiple_of(begin, HALO), HALO)].astype(BF)


def window_call(place, d_query, d_keys_t, d_values_t, wq, wk, wv):
    return pl.pallas_call(
        window_kernel,
        in_specs=[smem()] + [pl.BlockSpec(memory_space=pltpu.VMEM)] * 6,
        out_specs=[pl.BlockSpec(memory_space=pltpu.VMEM)] * 4,
        out_shape=[struct((REGION, WIDTH), F32)] + [struct((HALO, WIDTH))] * 3,
        scratch_shapes=[pltpu.VMEM((WINDOW - REGION, WIDTH), F32)],
        compiler_params=params(24),
        cost_estimate=cost(2_300_000_000, 10_000_000),
        name="window_back",
    )(place, d_query, d_keys_t, d_values_t, wq, wk, wv)


def input_kernel(
    place, tokens, gain, index, own, d_middle, from_row, from_core, from_chip, input_grad
):
    row, odd = place[7], place[0]
    back = own[...]
    for received, block in ((from_row, row), (from_core, 2 + odd), (from_chip, 3 - odd)):
        picks = index[pl.ds(block, 1), :]
        chosen = lax.broadcasted_iota(jnp.int32, (REGION, HALO), 0) == picks
        back = back + mm(jnp.where(chosen, 1.0, 0.0).astype(BF), received[...])
    value = tokens[...].astype(F32)
    inverse = lax.rsqrt(jnp.mean(value * value, axis=-1, keepdims=True) + EPS)
    scaled = back * gain[...].reshape(1, WIDTH).astype(F32)
    shared = jnp.mean(scaled * value, axis=-1, keepdims=True)
    input_grad[...] = (
        d_middle[...] + inverse * scaled - value * (inverse * inverse * inverse) * shared
    ).astype(BF)


def input_call(place, tokens, gain, index, own, d_middle, from_row, from_core, from_chip):
    return pl.pallas_call(
        input_kernel,
        in_specs=[smem()] + [pl.BlockSpec(memory_space=pltpu.VMEM)] * 8,
        out_specs=pl.BlockSpec(memory_space=pltpu.VMEM),
        out_shape=struct((REGION, WIDTH)),
        compiler_params=params(16),
        cost_estimate=cost(500_000_000, 6_000_000),
        name="input_back",
    )(place, tokens, gain, index, own, d_middle, from_row, from_core, from_chip)


def halves_kernel(ids, *refs, stage):
    sides = (range(2), range(1), range(1, 2))[stage]
    far = 1 if stage else 0
    units = [(side, k) for side in sides for k in range(3)]
    weights, gain, before, words = refs[0:3], refs[3], refs[4], refs[5:7]
    parts = dict(zip([3 * side + k for side, k in units], refs[7:]))
    skip = 7 + len(units) + (7 if stage else 0)
    outs, gain_out = refs[skip : skip + 7], refs[skip + 7]
    if stage == 2:
        ffn_gain, rel, lay = refs[skip + 8 : skip + 11]
        skip += 3
    weight, wide, tall, att, total, weight_sem, ffn_sem, att_sem = refs[skip + 8 :]

    def place_of(side, k):
        half = ids[0] ^ side
        return 2 * half + (((ids[1 + 3 * side + k] >> 5) & 1) ^ far)

    def weight_copy(side, k, number):
        rows = pl.ds(256 * k, 256)
        unit = 3 * side + k
        return pltpu.make_async_copy(
            weights[number].at[rows], weight.at[unit], weight_sem.at[unit]
        )

    def ffn_copy(side, k):
        begin = pl.multiple_of(place_of(side, k) * TILE, TILE)
        window = pl.ds(begin, TILE)
        if k == 2:
            return pltpu.make_async_copy(tall.at[side], outs[2].at[window], ffn_sem.at[3 * side + 2])
        return pltpu.make_async_copy(
            wide.at[side, k], outs[k].at[:, window], ffn_sem.at[3 * side + k]
        )

    def att_copy(side, k, number):
        rows = pl.ds(256 * k, 256)
        unit = 3 * side + k
        return pltpu.make_async_copy(att.at[unit], outs[3 + number].at[rows], att_sem.at[unit])

    def each_number(side, k, count, act):
        for number in range(count):

            @pl.when(place_of(side, k) == number)
            def _():
                act(number)

    for side, k in units:
        each_number(side, k, 3, lambda number: weight_copy(side, k, number).start())
    total[...] = jnp.zeros_like(total)
    for side, k in units:
        unit = 3 * side + k
        flip = ids[1 + 3 * side + k] & 31
        for piece in range(32):
            block = parts[unit][piece ^ flip, :, :WIDTH].astype(F32)
            if k == 2:
                tall[side, piece * 16 : piece * 16 + 16] = block
                continue
            col, row = piece // 16, piece % 16
            for third in range(3):
                begin = row * 48 + third * 16
                wide[side, k, begin : begin + 16, col * 256 : col * 256 + 256] = block[
                    :, third * 256 : third * 256 + 256
                ]
        ffn_copy(side, k).start()
        flip = flip >> 1
        for row in range(16):
            for group in range(2):
                att[unit, row * 16 : row * 16 + 16, group * COLS : group * COLS + COLS] = parts[unit][
                    (row ^ flip) * 2 + group, :, WIDTH:
                ].astype(F32)
        each_number(side, k, 4, lambda number: att_copy(side, k, number).start())

        def add_gain(number):
            weight_copy(side, k, number).wait()
            product = att[unit] * weight[unit].astype(F32)
            total[:, 256 * k : 256 * k + 256] += lax.dot_general(
                jnp.ones((8, WIDTH), F32), product, (((1,), (1,)), ((), ())),
                precision=lax.Precision.HIGHEST, preferred_element_type=F32,
            )

        each_number(side, k, 3, add_gain)
    if stage == 2:
        sums = total[0:1] + before[...]
        gain_out[...] = (sums / gain[...].reshape(1, WIDTH).astype(F32)).reshape(WIDTH)
        both = [word[0, :, :128].astype(F32) + word[0, :, 128:256].astype(F32) for word in words]
        small = both[0] + both[1]
        ffn_gain[...] = jnp.concatenate(
            [small[row : row + 1, 64:128] for row in range(HEADS)], axis=1
        ).reshape(WIDTH)
        rel[...] = small[:HEADS, 0:32]
        lay[...] = small[:HEADS, 32:64]
    else:
        gain_out[...] = total[0:1] + (before[...] if stage else 0.0)
    for side, k in units:
        ffn_copy(side, k).wait()
        att_copy(side, k, 0).wait()


def halves_call(stage, ids, weights, gain, before, words, parts, firsts=()):
    anywhere = pl.BlockSpec(memory_space=pl.ANY)
    vmem = pl.BlockSpec(memory_space=pltpu.VMEM)
    ends = [struct((WIDTH,), F32), struct((HEADS, 32), F32), struct((HEADS, 32), F32)]
    last = stage == 2
    return pl.pallas_call(
        functools.partial(halves_kernel, stage=stage),
        in_specs=[smem()] + [anywhere] * 3 + [vmem] * (4 + len(parts)) + [anywhere] * len(firsts),
        out_specs=[anywhere] * 7 + [vmem] * (4 if last else 1),
        scratch_shapes=[
            pltpu.VMEM((6, 256, WIDTH), BF),
            pltpu.VMEM((2, 2, WIDTH, TILE), F32),
            pltpu.VMEM((2, TILE, WIDTH), F32),
            pltpu.VMEM((6, 256, WIDTH), F32),
            pltpu.VMEM((8, WIDTH), F32),
            pltpu.SemaphoreType.DMA((6,)),
            pltpu.SemaphoreType.DMA((6,)),
            pltpu.SemaphoreType.DMA((6,)),
        ],
        out_shape=[struct((WIDTH, FF), F32), struct((WIDTH, FF), F32), struct((FF, WIDTH), F32)]
        + [struct((WIDTH, WIDTH), F32)] * 4
        + [struct((WIDTH,) if last else (1, WIDTH), F32)]
        + (ends if last else []),
        input_output_aliases={8 + len(parts) + k: k for k in range(len(firsts))},
        compiler_params=params(28),
        cost_estimate=cost(10_000_000, 24_000_000),
        name=("outputs_near", "outputs_far_own", "outputs_far_other")[stage],
    )(ids, *weights, gain, before, *words, *parts, *firsts)


AXES = ("row", "col")
OTHER_PAIRS = {0: 3, 3: 0, 1: 2, 2: 1}


def ring_pairs(axes, bit):
    pairs = []
    for chip in range(64):
        for core in range(2):
            spot = [chip // 16, chip // 4 % 4, chip % 4]
            first = (bit + core) % 2 == 0
            for axis in axes:
                spot[axis] = spot[axis] ^ 1 if first else OTHER_PAIRS[spot[axis]]
            partner = (spot[0] * 4 + spot[1]) * 4 + spot[2]
            pairs.append((2 * chip + core, 2 * partner + core))
    return pairs


CORE_PAIRS = [(d, d ^ 1) for d in range(SHARDS)]


def swap(value, pairs):
    return lax.ppermute(value, AXES, pairs)


def added(mine, received):
    return (mine.astype(F32) + received.astype(F32)).astype(BF)


def after(first, *values):
    held = lax.optimization_barrier((first, values))[1]
    return held[0] if len(values) == 1 else held


def words_sum(one, two):
    one_value, two_value = (v[..., :128].astype(F32) + v[..., 128:256].astype(F32) for v in (one, two))
    value = one_value + two_value
    high = value.astype(BF)
    low = (value - high.astype(F32)).astype(BF)
    return jnp.concatenate([high, low, jnp.zeros(one.shape[:2] + (MERGED - 256,), BF)], axis=-1)


def body(
    tokens, attn_gain, query_weight, key_weight, value_weight, output_weight, ffn_gain, gate_weight,
    up_weight, down_weight, relative_table, layout_table, cotangent, rel_bucket, layout_bucket,
    halo_index,
):
    tokens, cotangent = tokens[0], cotangent[0]
    relative, layout = rel_bucket[0], layout_bucket[0]
    index = halo_index[0, 0]
    columns = lax.axis_size("col")
    row_pairs = [(0, 1), (1, 0)]
    core_pairs = [(c, c ^ 1) for c in range(columns)]
    chip_pairs = [p for c in range(1, columns - 1, 2) for p in ((c, c + 1), (c + 1, c))]

    exchange_row = lambda v: lax.ppermute(v, "row", row_pairs)
    exchange_core = lambda v: lax.ppermute(v, "col", core_pairs)
    exchange_chip = lambda v: lax.ppermute(v, "col", chip_pairs)

    def ring(axis, bit):
        return ring_pairs((axis,), bit)

    normed, *sends, ids = norm_call(tokens, attn_gain, index)
    received = (exchange_row(sends[0]), exchange_core(sends[1]), exchange_chip(sends[2]))
    bias = bias_call(relative_table, layout_table, relative, layout)
    cotangent_other = swap(cotangent, CORE_PAIRS)
    window, query, keys, values, probs, attended = attend_call(
        ids, normed, *received, query_weight, key_weight, value_weight, bias, 4
    )
    (
        layer_out, d_middle, d_attended, d_branch, gain_two_grad, normed_two, *halves
    ) = ffn_call(
        ids, tokens, attended, output_weight, ffn_gain, cotangent, gate_weight, up_weight, down_weight
    )
    mixed_send, mixed, gate_send, d_gate, up_send, d_up = halves
    normed_two_other, mixed_other, d_gate_other, d_up_other = [
        swap(v, CORE_PAIRS) for v in (normed_two, mixed_send, gate_send, up_send)
    ]
    d_query, d_keys_t, d_values_t, d_logits, *att = back_call(
        ids, window, query, keys, values, probs, attended, d_attended, d_branch
    )
    att_other = [swap(v, CORE_PAIRS) for v in att[:3]]
    normed_two = after(d_query, normed_two)
    merged = grads_call(
        ids, normed_two, normed_two_other, cotangent, cotangent_other,
        (d_gate, d_gate_other, d_up, d_up_other, mixed, mixed_other), att[3:],
    )
    sent, kept = merge_call(0, att_other, merged[:3]), merged[3:]

    last = tuple(sent)
    got = [swap(sent[k], ring(k, 0)) for k in range(3)]
    tables = []
    for third in range(2):
        tables.append(table_call(third, d_logits, after(last, relative), layout))
        last = tables[-1]
        if third == 0:
            kept = list(merge_call(1, att_other, after(last, *kept)))
            last = kept[0]

    def halve(turn, got):
        half = kept[0].shape[0] // 2
        sent = [added(kept[k][half:], got[k][half:]) for k in range(3)]
        for k in range(3):
            kept[k] = added(kept[k][:half], got[k][:half])
        return tuple(sent), [swap(sent[k], ring((k + turn) % 3, 0)) for k in range(3)]

    own, *returns = window_call(
        ids, d_query, d_keys_t, d_values_t, query_weight, key_weight, after(last, value_weight)
    )
    last, got = halve(1, after(own, *got))
    from_row, from_chip = exchange_row(returns[0]), exchange_chip(returns[2])
    tables.append(table_call(2, d_logits, after(last, relative), layout))
    *got, from_row, from_chip = after(tables[-1], *got, from_row, from_chip)
    last, got = halve(2, got)
    small = small_call(*tables, after(last, gain_two_grad))
    got = after(small, *got)
    quarters = [
        jnp.stack([added(kept[k][2 * q : 2 * q + 2], got[k][2 * q : 2 * q + 2]) for k in range(3)])
        .reshape(6, PIECE, MERGED)
        for q in range(4)
    ]
    partners = {1: ring_pairs((1,), 1), 2: ring_pairs((0,), 1), 3: ring_pairs((0, 1), 1)}
    quarters[1] = jnp.concatenate([quarters[1], small])
    quarters[3] = after((quarters[1], quarters[2]), quarters[3])
    got = {q: swap(quarters[q], partners[q]) for q in (1, 2, 3)}
    mine = (
        (quarters[0].astype(F32) + got[1][:6].astype(F32))
        + (got[2].astype(F32) + got[3].astype(F32))
    ).astype(BF)
    small = words_sum(small, got[1][6:])
    got = swap(jnp.concatenate([mine, small]), ring(2, 1))
    mine = added(mine, got[:6])
    small = words_sum(small, got[6:])
    with_small = jnp.concatenate([mine, small])
    got = {q: swap(with_small if q == 2 else mine, partners[q]) for q in (1, 2, 3)}
    small = words_sum(small, got[2][6:])
    four = [v[:6].reshape(3, 2, PIECE, MERGED) for v in (mine, got[1], got[2], got[3])]
    near = [jnp.concatenate([v[k] for v in four]) for k in range(3)]
    for turn in (2, 1, 0):
        near[0] = jnp.concatenate([near[0], small])
        last = tuple(near)
        got = [swap(near[k], ring((k + turn) % 3, 0)) for k in range(3)]
        if turn == 0:
            break
        count = got[1].shape[0]
        for k in range(3):
            new = after(last, got[k])
            if k == 0:
                small = words_sum(small, new[-1:])
            near[k] = last = jnp.concatenate([near[k][:count], new[:count]])
    near_other = [swap(near[k], CORE_PAIRS) for k in range(3)]
    weights = (query_weight, key_weight, value_weight)
    common = (ids, weights, attn_gain)
    *outs, gain_part = halves_call(
        0, *common, gain_two_grad, (small, small), (*near, *near_other)
    )
    from_core = exchange_core(after(gain_part, returns[1]))
    input_grad = input_call(
        ids, after(gain_part, tokens), attn_gain, index, own, d_middle, from_row, from_core, from_chip
    )
    far, far_other, last = [], [], input_grad
    for k in range(3):
        far.append(after(last, got[k]))
        if k == 0:
            small = words_sum(small, far[0][-1:])
            small_other = swap(small, CORE_PAIRS)
        far_other.append(swap(far[k], CORE_PAIRS))
        last = far[k]
    words = (small, small)
    *outs, gain_part = halves_call(1, *common, gain_part, words, far, outs)
    words = (small, small_other)
    *outs, gain_one, gain_two, relative_grad, layout_grad = halves_call(
        2, *common, gain_part, words, after(gain_part, *far_other), outs
    )
    gate_grad, up_grad, down_grad, query_grad, key_grad, value_grad, output_grad = outs
    return (
        layer_out[None], input_grad[None], gain_one, query_grad, key_grad, value_grad,
        output_grad, gain_two, gate_grad, up_grad, down_grad, relative_grad.T, layout_grad.T,
    )


def solution(mesh):
    tokens = P("row", "col", None)
    whole_array = P()
    return jax.shard_map(
        body,
        mesh=mesh,
        in_specs=(tokens,) + (whole_array,) * 11 + (tokens,) * 3 + (P("row", "col", None, None),),
        out_specs=(tokens, tokens) + (whole_array,) * 11,
        check_vma=False,
    )
```

```python
import functools

import jax
import jax.numpy as jnp
from jax import lax
from jax.experimental import pallas as pl
from jax.experimental.pallas import tpu as pltpu
from jax.sharding import PartitionSpec as P

BF = jnp.bfloat16
F32 = jnp.float32
EPS = 1e-06
LOG2E = 1.4426950408889634
REGION = 384
WIDTH = 768
WINDOW = 768
HEADS = 12
HALO = 96
FF = 2048


def params(mib):
    return pltpu.CompilerParams(vmem_limit_bytes=mib * 2**20)


def cost(flops, moved, transcendentals=0):
    return pl.CostEstimate(flops=flops, bytes_accessed=moved, transcendentals=transcendentals)


def smem():
    return pl.BlockSpec(memory_space=pltpu.SMEM)


def whole(shape):
    return pl.BlockSpec(shape, lambda *_: (0,) * len(shape))


def mm(a, b):
    return jnp.dot(a, b, preferred_element_type=F32)


def mm_nt(a, b):
    return lax.dot_general(a, b, (((1,), (1,)), ((), ())), preferred_element_type=F32)


def mm_tn(a, b):
    return lax.dot_general(a, b, (((0,), (0,)), ((), ())), preferred_element_type=F32)


def struct(shape, dtype=BF):
    return jax.ShapeDtypeStruct(shape, dtype)


def near_by(shape, dtype=BF):
    return pltpu.VMEM(shape, dtype)


def main(shape, dtype=BF):
    return pltpu.HBM(shape, dtype)


def here(value):
    return pltpu.with_memory_space_constraint(value, pltpu.HBM)


def norm_kernel(tokens, gain, index, normed, send_row, send_core, send_chip, ids):
    value = tokens[...].astype(F32)
    inverse = lax.rsqrt(jnp.mean(value * value, axis=-1, keepdims=True) + EPS)
    low = (value * inverse * gain[...].reshape(1, WIDTH).astype(F32)).astype(BF)
    normed[...] = low
    row, col = lax.axis_index("row"), lax.axis_index("col")
    core = col & 1
    for out, block in ((send_row, row), (send_core, 2 + core), (send_chip, 3 - core)):
        picks = index[pl.ds(block, 1), :]
        chosen = lax.broadcasted_iota(jnp.int32, (REGION, HALO), 0) == picks
        out[...] = mm_tn(jnp.where(chosen, 1.0, 0.0).astype(BF), low).astype(BF)
    spots = (2 * row + (col >> 5), (col >> 3) & 3, (col >> 1) & 3)
    near = [((v + 1) >> 1) & 1 for v in spots]
    far = [v >> 1 for v in spots]
    ids[0] = core
    ids[7] = row
    for other in range(2):
        side = core ^ other
        first = [jnp.where(side == 1, f, n) for n, f in zip(near, far)]
        second = [jnp.where(side == 1, n, f) for n, f in zip(near, far)]
        for chunk in range(3):
            turned = [first[(chunk + turn) % 3] for turn in range(3)]
            ids[1 + 3 * other + chunk] = (
                turned[0] * 32 + turned[1] * 16 + turned[2] * 8 + second[0] * 4 + second[1] * 2
            )


def norm_call(tokens, gain, index):
    vmem = pl.BlockSpec(memory_space=pltpu.VMEM)
    return pl.pallas_call(
        norm_kernel,
        out_shape=(struct((REGION, WIDTH)),) + (struct((HALO, WIDTH)),) * 3 + (struct((8,), jnp.int32),),
        in_specs=[vmem] * 3,
        out_specs=(vmem,) * 4 + (smem(),),
        compiler_params=params(56),
        cost_estimate=cost(700_000_000, 2_000_000),
        name="norm_one",
    )(tokens, gain, index)


STEP = 2.0**-11
SHIFT = 9000
MASKED = -(2**31)
ROW_BLOCK = 32


def bias_kernel(relative_table, layout_table, relative, layout, out, table):
    rows = relative.shape[0]

    @pl.when(pl.program_id(0) == 0)
    def _():
        for number, source in enumerate((relative_table, layout_table)):
            values = jnp.round(source[...].astype(F32) * (LOG2E / STEP))
            fixed = jnp.concatenate([values, jnp.zeros((4, 32), F32)]).T.astype(jnp.int32)
            for pair in range(HEADS // 2):
                high = jnp.broadcast_to(fixed[:, 2 * pair : 2 * pair + 1], (32, 128))
                low = jnp.broadcast_to(fixed[:, 2 * pair + 1 : 2 * pair + 2], (32, 128))
                table[pair, number] = high * 65536 + (low + SHIFT)

    def look(words, low, bit3, bit4):
        four = [jnp.take_along_axis(words[8 * k : 8 * k + 8], low, axis=0) for k in range(4)]
        return jnp.where(
            bit4, jnp.where(bit3, four[3], four[2]), jnp.where(bit3, four[1], four[0])
        )

    def step(number, carry):
        begin = pl.multiple_of(number * 8, 8)
        for tile in range(WINDOW // 128):
            lanes = slice(tile * 128, tile * 128 + 128)
            rel = relative[pl.ds(begin, 8), lanes]
            lay = layout[pl.ds(begin, 8), lanes]
            rel_low, lay_low = rel & 7, lay & 7
            rel3, rel4 = (rel & 8) != 0, (rel & 16) != 0
            lay3, lay4 = (lay & 8) != 0, (lay & 16) != 0
            masked = rel >= 32
            for pair in range(HEADS // 2):
                word = look(table[pair, 0], rel_low, rel3, rel4)
                word = word + look(table[pair, 1], lay_low, lay3, lay4)
                out[pair, pl.ds(begin, 8), lanes] = jnp.where(masked, MASKED, word)
        return carry

    lax.fori_loop(0, rows // 8, step, 0)


def bias_call(relative_table, layout_table, relative, layout):
    block = 128
    buckets = pl.BlockSpec((block, WINDOW), lambda i: (i, 0))
    return pl.pallas_call(
        bias_kernel,
        grid=(REGION // block,),
        out_shape=struct((HEADS // 2, REGION, WINDOW), jnp.int32),
        in_specs=[whole((HEADS, 32)), whole((HEADS, 32)), buckets, buckets],
        out_specs=pl.BlockSpec((HEADS // 2, block, WINDOW), lambda i: (0, i, 0)),
        scratch_shapes=[pltpu.VMEM((HEADS // 2, 2, 32, 128), jnp.int32)],
        compiler_params=params(24),
        cost_estimate=cost(100_000_000, 17_000_000),
        name="bias",
    )(relative_table.T, layout_table.T, relative, layout)


def attend_kernel(
    place, normed, from_row, from_core, from_chip, wq, wk, wv, bias,
    window, query, keys, values, probs, attended, scores,
):
    width = wq.shape[1]

    @pl.when(pl.program_id(0) == 0)
    def _():
        row, odd = place[7], place[0]
        window[:REGION] = normed[...]
        window[REGION : REGION + 2 * HALO] = jnp.zeros((2 * HALO, WIDTH), BF)
        window[pl.ds(pl.multiple_of(REGION + HALO - HALO * row, HALO), HALO)] = from_row[...]
        window[pl.ds(pl.multiple_of(REGION + 3 * HALO - HALO * odd, HALO), HALO)] = from_core[...]
        window[pl.ds(pl.multiple_of(REGION + 2 * HALO + HALO * odd, HALO), HALO)] = from_chip[...]

    rows = window[...]
    query[...] = mm(rows[:REGION], wq[...]).astype(BF)
    keys[...] = mm(rows, wk[...]).astype(BF)
    lane = lax.broadcasted_iota(jnp.int32, (REGION, 128), 1)
    pairs = width // 128

    def score(pair):
        lanes = slice(pair * 128, pair * 128 + 128)
        for half in range(2):
            mine = (lane < 64) if half == 0 else (lane >= 64)
            one = jnp.where(mine, query[:, lanes], jnp.zeros((), BF))
            scores[2 * (pair % 2) + half] = mm_nt(one, keys[:, lanes])

    def soften(pair, half, begin):
        part = slice(begin, begin + ROW_BLOCK)
        word = bias[pair, part]
        fixed = (word >> 16) if half == 0 else (word & 0xFFFF)
        logits = scores[2 * (pair % 2) + half, part] * (0.125 * LOG2E) + fixed.astype(F32) * STEP
        logits = jnp.where(word == MASKED, -1.5e9, logits)
        highest = jnp.max(logits, axis=-1, keepdims=True)
        powered = jnp.exp2(logits - highest)
        total = jnp.sum(powered, axis=-1, keepdims=True)
        probs[2 * pair + half, part] = (powered * (1.0 / total)).astype(BF)

    score(0)
    values[...] = mm(rows, wv[...]).astype(BF)
    for pair in range(pairs):
        if pair + 1 < pairs:
            score(pair + 1)
        for begin in range(0, REGION, ROW_BLOCK):
            for half in range(2):
                soften(pair, half, begin)
        lanes = slice(pair * 128, pair * 128 + 128)
        halves = [mm(probs[2 * pair + half], values[:, lanes]) for half in range(2)]
        attended[:, lanes] = jnp.where(lane < 64, halves[0], halves[1]).astype(BF)


def attend_call(place, normed, from_row, from_core, from_chip, wq, wk, wv, bias, group):
    count = HEADS // group
    width = group * 64
    cols = lambda rows: pl.BlockSpec((rows, width), lambda g: (0, g))
    return pl.pallas_call(
        attend_kernel,
        grid=(count,),
        out_shape=(
            main((WINDOW, WIDTH)),
            main((REGION, WIDTH)),
            main((WINDOW, WIDTH)),
            main((WINDOW, WIDTH)),
            main((HEADS, REGION, WINDOW)),
            near_by((REGION, WIDTH)),
        ),
        in_specs=[smem(), whole((REGION, WIDTH))]
        + [whole((HALO, WIDTH))] * 3
        + [cols(WIDTH)] * 3
        + [pl.BlockSpec((group // 2, REGION, WINDOW), lambda g: (g, 0, 0))],
        out_specs=(
            whole((WINDOW, WIDTH)),
            cols(REGION),
            cols(WINDOW),
            cols(WINDOW),
            pl.BlockSpec((group, REGION, WINDOW), lambda g: (g, 0, 0)),
            cols(REGION),
        ),
        scratch_shapes=[pltpu.VMEM((4, REGION, WINDOW), F32)],
        compiler_params=params(40),
        cost_estimate=cost(3_500_000_000, 30_000_000, 3_600_000),
        name="attend",
    )(place, normed, from_row, from_core, from_chip, wq, wk, wv, bias)


SHARDS = 128
HALF = 64
TILE = 512
PIECE = 16
MERGED = 1152


def inverse_of(value):
    return lax.rsqrt(jnp.mean(value * value, axis=-1, keepdims=True) + EPS)


def ffn_kernel(
    ids, tokens, attended, wo, gain, cotangent, wg, wu, wd,
    layer_out, d_middle, d_attended, d_branch, gain_grad, normed,
    mixed_send, mixed_keep, gate_send, gate_keep, up_send, up_keep,
    middle, total_out, total_back,
):
    step = pl.program_id(0)

    @pl.when(step == 0)
    def _():
        value = tokens[...].astype(F32) + mm(attended[...], wo[...])
        middle[...] = value
        normed[...] = (value * inverse_of(value) * gain[...].reshape(1, WIDTH).astype(F32)).astype(BF)
        total_out[...] = value
        total_back[...] = jnp.zeros_like(total_back)

    low = normed[...]
    gate = mm(low, wg[...])
    up_part = mm(low, wu[...])
    d_mixed = mm_nt(cotangent[...], wd[...])
    curve = jnp.tanh(gate * (0.7978845608 + (0.7978845608 * 0.044715) * (gate * gate)))
    half_up = 0.5 * (1.0 + curve)
    act = gate * half_up
    slope = half_up + 0.5 * gate * (1.0 - curve * curve) * (
        0.7978845608 + (3 * 0.7978845608 * 0.044715) * gate * gate
    )
    mixed = (act * up_part).astype(BF)
    d_gate = (d_mixed * up_part * slope).astype(BF)
    d_up = (d_mixed * act).astype(BF)
    total_out[...] += mm(mixed, wd[...])
    total_back[...] += mm_nt(d_gate, wg[...]) + mm_nt(d_up, wu[...])

    @pl.when(step < 2)
    def _():
        mixed_send[...] = mixed
        gate_send[...] = d_gate
        up_send[...] = d_up

    @pl.when(step >= 2)
    def _():
        mixed_keep[...] = mixed
        gate_keep[...] = d_gate
        up_keep[...] = d_up

    @pl.when(step == 3)
    def _():
        layer_out[...] = total_out[...].astype(BF)
        value = middle[...]
        inverse = inverse_of(value)
        back = total_back[...]
        gain_grad[...] = jnp.sum(back * value * inverse, axis=0, keepdims=True)
        scaled = back * gain[...].reshape(1, WIDTH).astype(F32)
        shared = jnp.mean(scaled * value, axis=-1, keepdims=True)
        whole_grad = (
            cotangent[...].astype(F32)
            + inverse * scaled
            - value * (inverse * inverse * inverse) * shared
        )
        d_middle[...] = whole_grad
        branch = whole_grad.astype(BF)
        d_branch[...] = branch
        d_attended[...] = mm_nt(branch, wo[...]).astype(BF)


def ffn_call(ids, tokens, attended, wo, gain, cotangent, wg, wu, wd):
    def tile(g, ids):
        return jnp.where(g < 2, 1 - ids[0], ids[0]) * 2 + (g & 1)

    cols = pl.BlockSpec((WIDTH, TILE), lambda g, ids: (0, tile(g, ids)))
    sent = pl.BlockSpec((REGION, TILE), lambda g, ids: (0, jnp.minimum(g, 1)))
    kept = pl.BlockSpec((REGION, TILE), lambda g, ids: (0, jnp.maximum(g - 2, 0)))
    full = whole((REGION, WIDTH))
    return pl.pallas_call(
        ffn_kernel,
        grid_spec=pltpu.PrefetchScalarGridSpec(
            num_scalar_prefetch=1,
            grid=(FF // TILE,),
            in_specs=[
                full, full, whole((WIDTH, WIDTH)), whole((WIDTH,)), full, cols, cols,
                pl.BlockSpec((TILE, WIDTH), lambda g, ids: (tile(g, ids), 0)),
            ],
            out_specs=[full, full, full, full, whole((1, WIDTH)), full]
            + [sent, kept, sent, kept, sent, kept],
            scratch_shapes=[pltpu.VMEM((REGION, WIDTH), F32)] * 3,
        ),
        out_shape=[
            main((REGION, WIDTH)),
            main((REGION, WIDTH), F32),
            near_by((REGION, WIDTH)),
            near_by((REGION, WIDTH)),
            main((1, WIDTH), F32),
            main((REGION, WIDTH)),
        ]
        + [main((REGION, FF // 2))] * 6,
        compiler_params=params(36),
        cost_estimate=cost(8_000_000_000, 20_000_000, 800_000),
        name="feed_forward",
    )(ids, tokens, attended, wo, gain, cotangent, wg, here(wu), here(wd))


def grads_kernel(ids, *refs):
    normeds, cots = refs[0:2], refs[2:4]
    hidden = (refs[4:6], refs[6:8], refs[8:10])
    att, outs = refs[10:13], refs[13:19]
    normed, grad_out, right, normed_t, kept, in_sem = refs[19:]

    def pair_in(sources, target, number):
        return [
            pltpu.make_async_copy(
                sources[k], target.at[k * REGION : k * REGION + REGION], in_sem.at[number]
            )
            for k in range(2)
        ]

    copies = [pair_in(normeds, normed, 0)]
    copies += [pair_in(hidden[k], right.at[k], 1 + k) for k in range(3)]
    copies += [pair_in(cots, grad_out, 4)]
    copies += [[pltpu.make_async_copy(att[k], kept.at[k], in_sem.at[5]) for k in range(3)]]
    for number in (0, 1, 5, 2, 4, 3):
        for copy in copies[number]:
            copy.start()

    def wait(number):
        for copy in copies[number]:
            copy.wait()

    def put(out, k, grad, flip):
        for piece in range(32):
            col, row = piece // 16, piece % 16
            if k == 2:
                out[piece ^ flip, :, :WIDTH] = grad[piece * 16 : piece * 16 + 16]
                continue
            for third in range(3):
                begin = row * 48 + third * 16
                out[piece ^ flip, :, third * 256 : third * 256 + 256] = grad[
                    begin : begin + 16, col * 256 : col * 256 + 256
                ]

    wait(0)
    normed_t[...] = normed[...].T
    for k in range(3):
        wait(1 + k)
        if k == 2:
            wait(4)
        place = ids[1 + k]
        top, flip = (place >> 5) & 1, place & 31
        for tile in range(2):
            cols = slice(tile * TILE, tile * TILE + TILE)
            if k < 2:
                grad = mm(normed_t[...], right[k, :, cols]).astype(BF)
            else:
                grad = mm_tn(right[k, :, cols], grad_out[...]).astype(BF)
            away = top != tile

            @pl.when(away)
            def _():
                put(outs[k], k, grad, flip)

            @pl.when(jnp.logical_not(away))
            def _():
                put(outs[3 + k], k, grad, flip)

        if k == 0:
            wait(5)
        for spot in range(32):
            out = outs[3 * (1 - spot // 16) + k]
            for group in range(2):
                out[(spot % 16) * 2 + group, :, WIDTH:] = kept[k, spot, group]


def grads_call(ids, normed, normed_other, cotangent, cotangent_other, pairs, att):
    merged = (32, PIECE, MERGED)
    anywhere = pl.BlockSpec(memory_space=pl.ANY)
    vmem = pl.BlockSpec(memory_space=pltpu.VMEM)
    pairs = [here(v) if k % 2 == 0 else v for k, v in enumerate(pairs)]
    return pl.pallas_call(
        grads_kernel,
        in_specs=[smem()] + [anywhere] * 13,
        out_specs=[vmem] * 6,
        scratch_shapes=[
            pltpu.VMEM((2 * REGION, WIDTH), BF),
            pltpu.VMEM((2 * REGION, WIDTH), BF),
            pltpu.VMEM((3, 2 * REGION, FF // 2), BF),
            pltpu.VMEM((WIDTH, 2 * REGION), BF),
            pltpu.VMEM((3, 32, 2, PIECE, COLS), BF),
            pltpu.SemaphoreType.DMA((6,)),
        ],
        out_shape=[near_by(merged)] * 6,
        compiler_params=params(20),
        cost_estimate=cost(3_700_000_000, 16_000_000),
        name="feed_forward_grads",
    )(
        ids, here(normed), normed_other, here(cotangent), cotangent_other, *pairs, *map(here, att)
    )


def merge_kernel(*refs, side):
    att_other, pieces, outs = refs[0:3], refs[3:6], refs[6:9]
    for k in range(3):
        half = att_other[k][16 - 16 * side : 32 - 16 * side].astype(F32)
        total = pieces[k][:, :, WIDTH:].astype(F32) + half.reshape(32, PIECE, COLS)
        outs[k][:, :, WIDTH:] = total.astype(BF)


def merge_call(side, att_other, pieces):
    vmem = pl.BlockSpec(memory_space=pltpu.VMEM)
    return pl.pallas_call(
        functools.partial(merge_kernel, side=side),
        in_specs=[vmem] * 6,
        out_specs=[vmem] * 3,
        out_shape=[near_by((32, PIECE, MERGED))] * 3,
        input_output_aliases={3 + number: number for number in range(3)},
        compiler_params=params(8),
        cost_estimate=cost(5_000_000, 5_000_000),
        name="merge_cores",
    )(*att_other, *pieces)


GROUP = 6
COLS = GROUP * 64


def back_kernel(
    ids, window, query, keys, values, probs, attended, d_attended, attended_all, d_branch, *refs
):
    d_query, d_keys_t, d_values_t, d_logits = refs[:4]
    sends, keeps = refs[4:7], refs[7:10]
    window_t, slopes, attended_t = refs[10:]

    @pl.when(pl.program_id(0) == 0)
    def _():
        window_t[...] = window[...].T
        attended_t[...] = attended_all[...].T

    query_t = query[...].T
    d_att_t = d_attended[...].T
    nothing = jnp.zeros((64, REGION), BF)

    def both_heads(rows):
        return jnp.concatenate(
            [
                jnp.concatenate([rows[:64], nothing], axis=1),
                jnp.concatenate([nothing, rows[64:]], axis=1),
            ]
        )

    lane = lax.broadcasted_iota(jnp.int32, (REGION, 128), 1)
    for pair in range(GROUP // 2):
        lanes = slice(pair * 128, pair * 128 + 128)
        halves = []
        for half in range(2):
            head = 2 * pair + half
            mine = (lane < 64) if half == 0 else (lane >= 64)
            one = jnp.where(mine, d_attended[:, lanes], jnp.zeros((), BF))
            shared = jnp.sum(
                one.astype(F32) * attended[:, lanes].astype(F32), axis=-1, keepdims=True
            )
            slot = head % 2
            slopes[slot] = mm_nt(one, values[:, lanes])
            for begin in range(0, REGION, 32):
                part = slice(begin, begin + 32)
                grad = probs[head, part].astype(F32) * (slopes[slot, part] - shared[part])
                d_logits[head, part] = grad.astype(BF)
            halves.append(mm(d_logits[head], keys[:, lanes]))
        heads = slice(2 * pair, 2 * pair + 2)
        stacked = d_logits[heads].reshape(2 * REGION, WINDOW)
        d_keys_t[lanes] = (mm(both_heads(query_t[lanes]), stacked) * 0.125).astype(BF)
        stacked = probs[heads].reshape(2 * REGION, WINDOW)
        d_values_t[lanes] = mm(both_heads(d_att_t[lanes]), stacked).astype(BF)
        d_query[:, lanes] = (jnp.where(lane < 64, halves[0], halves[1]) * 0.125).astype(BF)
    grads = (
        mm(window_t[:, :REGION], d_query[...]).astype(BF),
        mm_nt(window_t[...], d_keys_t[...]).astype(BF),
        mm_nt(window_t[...], d_values_t[...]).astype(BF),
        mm(attended_t[...], d_branch[...]).astype(BF),
    )

    def put(numbers, outs, first):
        for third in range(3):
            flip = (ids[first + third] >> 1) & 31
            for number in numbers:
                for row in range(16):
                    shard = (number & 1) * 16 + row
                    begin = third * 256 + row * 16
                    outs[third][shard ^ flip, 0] = grads[number][begin : begin + 16]

    first = ids[0] == 0

    @pl.when(first)
    def _():
        put((0, 1), keeps, 1)
        put((2, 3), sends, 4)

    @pl.when(jnp.logical_not(first))
    def _():
        put((0, 1), sends, 4)
        put((2, 3), keeps, 1)


def back_call(ids, window, query, keys, values, probs, attended, d_attended, d_branch):
    cols = lambda rows: pl.BlockSpec((rows, COLS), lambda g: (0, g))
    feats = pl.BlockSpec((COLS, WINDOW), lambda g: (g, 0))
    heads = pl.BlockSpec((GROUP, REGION, WINDOW), lambda g: (g, 0, 0))
    return pl.pallas_call(
        back_kernel,
        grid=(2,),
        in_specs=[
            smem(), whole((WINDOW, WIDTH)), cols(REGION), cols(WINDOW), cols(WINDOW), heads,
            cols(REGION), cols(REGION), whole((REGION, WIDTH)), cols(REGION),
        ],
        out_specs=[cols(REGION), feats, feats, heads]
        + [pl.BlockSpec((32, 1, PIECE, COLS), lambda g: (0, g, 0, 0))] * 6,
        out_shape=[
            main((REGION, WIDTH)),
            main((WIDTH, WINDOW)),
            main((WIDTH, WINDOW)),
            main((HEADS, REGION, WINDOW)),
        ]
        + [main((32, 2, PIECE, COLS))] * 6,
        scratch_shapes=[
            pltpu.VMEM((WIDTH, WINDOW), BF),
            pltpu.VMEM((2, REGION, WINDOW), F32),
            pltpu.VMEM((WIDTH, REGION), BF),
        ],
        compiler_params=params(44),
        cost_estimate=cost(6_000_000_000, 30_000_000),
        name="attend_back",
    )(
        ids, here(window), here(query), here(keys), here(values), here(probs), attended, d_attended,
        attended, d_branch,
    )


ROWS = 16
BLOCKS = 4


def table_kernel(d_logits, relative, layout, out, onehot, total):
    step = pl.program_id(0)

    @pl.when(step == 0)
    def _():
        total[...] = jnp.zeros_like(total)

    bucket = lax.broadcasted_iota(jnp.int32, (32, WINDOW), 0)
    added = []
    for block in range(BLOCKS):
        for row in range(ROWS):
            for offset, source in ((0, relative), (32, layout)):
                at = block * ROWS + row
                hit = source[at : at + 1, :] == bucket
                begin = row * 64 + offset
                onehot[block, begin : begin + 32] = jnp.where(hit, 1.0, 0.0).astype(BF)
        rows = slice(block * ROWS, block * ROWS + ROWS)
        left = d_logits[:, rows, :].reshape(HEADS * ROWS, WINDOW)
        added.append(mm_nt(left, onehot[block]))
    total[...] += (added[0] + added[1]) + (added[2] + added[3])

    @pl.when(step == pl.num_programs(0) - 1)
    def _():
        shape = total.shape
        left_row = lax.broadcasted_iota(jnp.int32, shape, 0) % ROWS
        right_row = lax.broadcasted_iota(jnp.int32, shape, 1) // 64
        kept = jnp.where(left_row == right_row, total[...], 0.0)
        by_head = jnp.sum(kept.reshape(HEADS, ROWS, shape[1]), axis=1)
        folded = by_head[:, 0:128]
        for tile in range(1, shape[1] // 128):
            folded = folded + by_head[:, tile * 128 : tile * 128 + 128]
        out[...] = folded[:, :64] + folded[:, 64:]


def table_call(third, d_logits, relative, layout):
    rows = ROWS * BLOCKS
    steps = REGION // 3 // rows
    heads = pl.BlockSpec((HEADS, rows, WINDOW), lambda i: (0, third * steps + i, 0))
    buckets = pl.BlockSpec((rows, WINDOW), lambda i: (third * steps + i, 0))
    return pl.pallas_call(
        table_kernel,
        grid=(steps,),
        in_specs=[heads, buckets, buckets],
        out_specs=whole((HEADS, 64)),
        out_shape=struct((HEADS, 64), F32),
        scratch_shapes=[
            pltpu.VMEM((BLOCKS, ROWS * 64, WINDOW), BF),
            pltpu.VMEM((HEADS * ROWS, ROWS * 64), F32),
        ],
        compiler_params=params(20),
        cost_estimate=cost(2_500_000_000, 4_000_000),
        name="table_grads",
    )(d_logits, relative, layout)


def small_kernel(one, two, three, gain_grad, out):
    out[...] = jnp.zeros_like(out)
    gain = jnp.concatenate([gain_grad[:, row * 64 : row * 64 + 64] for row in range(HEADS)])
    value = jnp.concatenate([one[...] + two[...] + three[...], gain], axis=1)
    value = jnp.concatenate([value, jnp.zeros((PIECE - HEADS, 128), F32)])
    high = value.astype(BF)
    out[0, :, :128] = high
    out[0, :, 128:256] = (value - high.astype(F32)).astype(BF)


def small_call(one, two, three, gain_grad):
    return pl.pallas_call(
        small_kernel,
        in_specs=[pl.BlockSpec(memory_space=pltpu.VMEM)] * 4,
        out_specs=pl.BlockSpec(memory_space=pltpu.VMEM),
        out_shape=struct((1, PIECE, MERGED)),
        compiler_params=params(8),
        name="small_sums",
    )(one, two, three, gain_grad)


def window_kernel(place, d_query, d_keys_t, d_values_t, wq, wk, wv, own, for_row, for_core, for_chip, rest):
    full = mm(wk[...], d_keys_t[...]) + mm(wv[...], d_values_t[...])
    own[...] = (full[:, :REGION] + mm_nt(wq[...], d_query[...])).T
    rest[...] = full[:, REGION:].T
    row, odd = place[7], place[0]
    for out, begin in (
        (for_row, HALO - HALO * row),
        (for_core, 3 * HALO - HALO * odd),
        (for_chip, 2 * HALO + HALO * odd),
    ):
        out[...] = rest[pl.ds(pl.multiple_of(begin, HALO), HALO)].astype(BF)


def window_call(place, d_query, d_keys_t, d_values_t, wq, wk, wv):
    return pl.pallas_call(
        window_kernel,
        in_specs=[smem()] + [pl.BlockSpec(memory_space=pltpu.VMEM)] * 6,
        out_specs=[pl.BlockSpec(memory_space=pltpu.VMEM)] * 4,
        out_shape=[struct((REGION, WIDTH), F32)] + [struct((HALO, WIDTH))] * 3,
        scratch_shapes=[pltpu.VMEM((WINDOW - REGION, WIDTH), F32)],
        compiler_params=params(24),
        cost_estimate=cost(2_300_000_000, 10_000_000),
        name="window_back",
    )(place, d_query, d_keys_t, d_values_t, wq, wk, wv)


def input_kernel(
    place, tokens, gain, index, own, d_middle, from_row, from_core, from_chip, input_grad
):
    row, odd = place[7], place[0]
    back = own[...]
    for received, block in ((from_row, row), (from_core, 2 + odd), (from_chip, 3 - odd)):
        picks = index[pl.ds(block, 1), :]
        chosen = lax.broadcasted_iota(jnp.int32, (REGION, HALO), 0) == picks
        back = back + mm(jnp.where(chosen, 1.0, 0.0).astype(BF), received[...])
    value = tokens[...].astype(F32)
    inverse = lax.rsqrt(jnp.mean(value * value, axis=-1, keepdims=True) + EPS)
    scaled = back * gain[...].reshape(1, WIDTH).astype(F32)
    shared = jnp.mean(scaled * value, axis=-1, keepdims=True)
    input_grad[...] = (
        d_middle[...] + inverse * scaled - value * (inverse * inverse * inverse) * shared
    ).astype(BF)


def input_call(place, tokens, gain, index, own, d_middle, from_row, from_core, from_chip):
    return pl.pallas_call(
        input_kernel,
        in_specs=[smem()] + [pl.BlockSpec(memory_space=pltpu.VMEM)] * 8,
        out_specs=pl.BlockSpec(memory_space=pltpu.VMEM),
        out_shape=struct((REGION, WIDTH)),
        compiler_params=params(16),
        cost_estimate=cost(500_000_000, 6_000_000),
        name="input_back",
    )(place, tokens, gain, index, own, d_middle, from_row, from_core, from_chip)


def halves_kernel(ids, *refs, stage):
    sides = (range(2), range(1), range(1, 2))[stage]
    far = 1 if stage else 0
    units = [(side, k) for side in sides for k in range(3)]
    weights, gain, before, words = refs[0:3], refs[3], refs[4], refs[5:7]
    parts = dict(zip([3 * side + k for side, k in units], refs[7:]))
    skip = 7 + len(units) + (7 if stage else 0)
    outs, gain_out = refs[skip : skip + 7], refs[skip + 7]
    if stage == 2:
        ffn_gain, rel, lay = refs[skip + 8 : skip + 11]
        skip += 3
    weight, wide, tall, att, total, weight_sem, ffn_sem, att_sem = refs[skip + 8 :]

    def place_of(side, k):
        half = ids[0] ^ side
        return 2 * half + (((ids[1 + 3 * side + k] >> 5) & 1) ^ far)

    def weight_copy(side, k, number):
        rows = pl.ds(256 * k, 256)
        unit = 3 * side + k
        return pltpu.make_async_copy(
            weights[number].at[rows], weight.at[unit], weight_sem.at[unit]
        )

    def ffn_copy(side, k):
        begin = pl.multiple_of(place_of(side, k) * TILE, TILE)
        window = pl.ds(begin, TILE)
        if k == 2:
            return pltpu.make_async_copy(tall.at[side], outs[2].at[window], ffn_sem.at[3 * side + 2])
        return pltpu.make_async_copy(
            wide.at[side, k], outs[k].at[:, window], ffn_sem.at[3 * side + k]
        )

    def att_copy(side, k, number):
        rows = pl.ds(256 * k, 256)
        unit = 3 * side + k
        return pltpu.make_async_copy(att.at[unit], outs[3 + number].at[rows], att_sem.at[unit])

    def each_number(side, k, count, act):
        for number in range(count):

            @pl.when(place_of(side, k) == number)
            def _():
                act(number)

    for side, k in units:
        each_number(side, k, 3, lambda number: weight_copy(side, k, number).start())
    total[...] = jnp.zeros_like(total)
    for side, k in units:
        unit = 3 * side + k
        flip = ids[1 + 3 * side + k] & 31
        for piece in range(32):
            block = parts[unit][piece ^ flip, :, :WIDTH].astype(F32)
            if k == 2:
                tall[side, piece * 16 : piece * 16 + 16] = block
                continue
            col, row = piece // 16, piece % 16
            for third in range(3):
                begin = row * 48 + third * 16
                wide[side, k, begin : begin + 16, col * 256 : col * 256 + 256] = block[
                    :, third * 256 : third * 256 + 256
                ]
        ffn_copy(side, k).start()
        flip = flip >> 1
        for row in range(16):
            for group in range(2):
                att[unit, row * 16 : row * 16 + 16, group * COLS : group * COLS + COLS] = parts[unit][
                    (row ^ flip) * 2 + group, :, WIDTH:
                ].astype(F32)
        each_number(side, k, 4, lambda number: att_copy(side, k, number).start())
    for side, k in units:
        unit = 3 * side + k

        def add_gain(number):
            weight_copy(side, k, number).wait()
            product = att[unit] * weight[unit].astype(F32)
            total[:, 256 * k : 256 * k + 256] += lax.dot_general(
                jnp.ones((8, WIDTH), F32), product, (((1,), (1,)), ((), ())),
                precision=lax.Precision.HIGHEST, preferred_element_type=F32,
            )

        each_number(side, k, 3, add_gain)
    if stage == 2:
        sums = total[0:1] + before[...]
        gain_out[...] = (sums / gain[...].reshape(1, WIDTH).astype(F32)).reshape(WIDTH)
        both = [word[0, :, :128].astype(F32) + word[0, :, 128:256].astype(F32) for word in words]
        small = both[0] + both[1]
        ffn_gain[...] = jnp.concatenate(
            [small[row : row + 1, 64:128] for row in range(HEADS)], axis=1
        ).reshape(WIDTH)
        rel[...] = small[:HEADS, 0:32]
        lay[...] = small[:HEADS, 32:64]
    else:
        gain_out[...] = total[0:1] + (before[...] if stage else 0.0)
    for side, k in units:
        ffn_copy(side, k).wait()
        att_copy(side, k, 0).wait()


def halves_call(stage, ids, weights, gain, before, words, parts, firsts=()):
    anywhere = pl.BlockSpec(memory_space=pl.ANY)
    vmem = pl.BlockSpec(memory_space=pltpu.VMEM)
    ends = [struct((WIDTH,), F32), struct((HEADS, 32), F32), struct((HEADS, 32), F32)]
    last = stage == 2
    return pl.pallas_call(
        functools.partial(halves_kernel, stage=stage),
        in_specs=[smem()] + [anywhere] * 3 + [vmem] * (4 + len(parts)) + [anywhere] * len(firsts),
        out_specs=[anywhere] * 7 + [vmem] * (4 if last else 1),
        scratch_shapes=[
            pltpu.VMEM((6, 256, WIDTH), BF),
            pltpu.VMEM((2, 2, WIDTH, TILE), F32),
            pltpu.VMEM((2, TILE, WIDTH), F32),
            pltpu.VMEM((6, 256, WIDTH), F32),
            pltpu.VMEM((8, WIDTH), F32),
            pltpu.SemaphoreType.DMA((6,)),
            pltpu.SemaphoreType.DMA((6,)),
            pltpu.SemaphoreType.DMA((6,)),
        ],
        out_shape=[struct((WIDTH, FF), F32), struct((WIDTH, FF), F32), struct((FF, WIDTH), F32)]
        + [struct((WIDTH, WIDTH), F32)] * 4
        + [struct((WIDTH,) if last else (1, WIDTH), F32)]
        + (ends if last else []),
        input_output_aliases={8 + len(parts) + k: k for k in range(len(firsts))},
        compiler_params=params(28),
        cost_estimate=cost(10_000_000, 24_000_000),
        name=("outputs_near", "outputs_far_own", "outputs_far_other")[stage],
    )(ids, *weights, gain, before, *words, *parts, *firsts)


AXES = ("row", "col")
OTHER_PAIRS = {0: 3, 3: 0, 1: 2, 2: 1}


def ring_pairs(axes, bit):
    pairs = []
    for chip in range(64):
        for core in range(2):
            spot = [chip // 16, chip // 4 % 4, chip % 4]
            first = (bit + core) % 2 == 0
            for axis in axes:
                spot[axis] = spot[axis] ^ 1 if first else OTHER_PAIRS[spot[axis]]
            partner = (spot[0] * 4 + spot[1]) * 4 + spot[2]
            pairs.append((2 * chip + core, 2 * partner + core))
    return pairs


CORE_PAIRS = [(d, d ^ 1) for d in range(SHARDS)]


def swap(value, pairs):
    return lax.ppermute(value, AXES, pairs)


def added(mine, received):
    return (mine.astype(F32) + received.astype(F32)).astype(BF)


def after(first, *values):
    held = lax.optimization_barrier((first, values))[1]
    return held[0] if len(values) == 1 else held


def words_sum(one, two):
    one_value, two_value = (v[..., :128].astype(F32) + v[..., 128:256].astype(F32) for v in (one, two))
    value = one_value + two_value
    high = value.astype(BF)
    low = (value - high.astype(F32)).astype(BF)
    return jnp.concatenate([high, low, jnp.zeros(one.shape[:2] + (MERGED - 256,), BF)], axis=-1)


def body(
    tokens, attn_gain, query_weight, key_weight, value_weight, output_weight, ffn_gain, gate_weight,
    up_weight, down_weight, relative_table, layout_table, cotangent, rel_bucket, layout_bucket,
    halo_index,
):
    tokens, cotangent = tokens[0], cotangent[0]
    relative, layout = rel_bucket[0], layout_bucket[0]
    index = halo_index[0, 0]
    columns = lax.axis_size("col")
    row_pairs = [(0, 1), (1, 0)]
    core_pairs = [(c, c ^ 1) for c in range(columns)]
    chip_pairs = [p for c in range(1, columns - 1, 2) for p in ((c, c + 1), (c + 1, c))]

    exchange_row = lambda v: lax.ppermute(v, "row", row_pairs)
    exchange_core = lambda v: lax.ppermute(v, "col", core_pairs)
    exchange_chip = lambda v: lax.ppermute(v, "col", chip_pairs)

    def ring(axis, bit):
        return ring_pairs((axis,), bit)

    normed, *sends, ids = norm_call(tokens, attn_gain, index)
    received = (exchange_row(sends[0]), exchange_core(sends[1]), exchange_chip(sends[2]))
    bias = bias_call(relative_table, layout_table, relative, layout)
    cotangent_other = swap(cotangent, CORE_PAIRS)
    window, query, keys, values, probs, attended = attend_call(
        ids, normed, *received, query_weight, key_weight, value_weight, bias, 4
    )
    (
        layer_out, d_middle, d_attended, d_branch, gain_two_grad, normed_two, *halves
    ) = ffn_call(
        ids, tokens, attended, output_weight, ffn_gain, cotangent, gate_weight, up_weight, down_weight
    )
    mixed_send, mixed, gate_send, d_gate, up_send, d_up = halves
    normed_two_other, mixed_other, d_gate_other, d_up_other = [
        swap(v, CORE_PAIRS) for v in (normed_two, mixed_send, gate_send, up_send)
    ]
    d_query, d_keys_t, d_values_t, d_logits, *att = back_call(
        ids, window, query, keys, values, probs, attended, d_attended, d_branch
    )
    att_other = [swap(v, CORE_PAIRS) for v in att[:3]]
    normed_two = after(d_query, normed_two)
    merged = grads_call(
        ids, normed_two, normed_two_other, cotangent, cotangent_other,
        (d_gate, d_gate_other, d_up, d_up_other, mixed, mixed_other), att[3:],
    )
    sent, kept = merge_call(0, att_other, merged[:3]), merged[3:]

    last = tuple(sent)
    got = [swap(sent[k], ring(k, 0)) for k in range(3)]
    tables = []
    for third in range(2):
        tables.append(table_call(third, d_logits, after(last, relative), layout))
        last = tables[-1]
        if third == 0:
            kept = list(merge_call(1, att_other, after(last, *kept)))
            last = kept[0]

    def halve(turn, got):
        half = kept[0].shape[0] // 2
        sent = [added(kept[k][half:], got[k][half:]) for k in range(3)]
        for k in range(3):
            kept[k] = added(kept[k][:half], got[k][:half])
        return tuple(sent), [swap(sent[k], ring((k + turn) % 3, 0)) for k in range(3)]

    own, *returns = window_call(
        ids, d_query, d_keys_t, d_values_t, query_weight, key_weight, after(last, value_weight)
    )
    last, got = halve(1, after(own, *got))
    from_row, from_chip = exchange_row(returns[0]), exchange_chip(returns[2])
    tables.append(table_call(2, d_logits, after(last, relative), layout))
    *got, from_row, from_chip = after(tables[-1], *got, from_row, from_chip)
    last, got = halve(2, got)
    small = small_call(*tables, after(last, gain_two_grad))
    got = after(small, *got)
    quarters = [
        jnp.stack([added(kept[k][2 * q : 2 * q + 2], got[k][2 * q : 2 * q + 2]) for k in range(3)])
        .reshape(6, PIECE, MERGED)
        for q in range(4)
    ]
    partners = {1: ring_pairs((1,), 1), 2: ring_pairs((0,), 1), 3: ring_pairs((0, 1), 1)}
    quarters[1] = jnp.concatenate([quarters[1], small])
    quarters[3] = after((quarters[1], quarters[2]), quarters[3])
    got = {q: swap(quarters[q], partners[q]) for q in (1, 2, 3)}
    mine = (
        (quarters[0].astype(F32) + got[1][:6].astype(F32))
        + (got[2].astype(F32) + got[3].astype(F32))
    ).astype(BF)
    small = words_sum(small, got[1][6:])
    got = swap(jnp.concatenate([mine, small]), ring(2, 1))
    mine = added(mine, got[:6])
    small = words_sum(small, got[6:])
    with_small = jnp.concatenate([mine, small])
    got = {q: swap(with_small if q == 2 else mine, partners[q]) for q in (1, 2, 3)}
    small = words_sum(small, got[2][6:])
    four = [v[:6].reshape(3, 2, PIECE, MERGED) for v in (mine, got[1], got[2], got[3])]
    near = [jnp.concatenate([v[k] for v in four]) for k in range(3)]
    for turn in (2, 1, 0):
        near[0] = jnp.concatenate([near[0], small])
        last = tuple(near)
        got = [swap(near[k], ring((k + turn) % 3, 0)) for k in range(3)]
        if turn == 0:
            break
        count = got[1].shape[0]
        for k in range(3):
            new = after(last, got[k])
            if k == 0:
                small = words_sum(small, new[-1:])
            near[k] = last = jnp.concatenate([near[k][:count], new[:count]])
    near_other = [swap(near[k], CORE_PAIRS) for k in range(3)]
    weights = (query_weight, key_weight, value_weight)
    common = (ids, weights, attn_gain)
    *outs, gain_part = halves_call(
        0, *common, gain_two_grad, (small, small), (*near, *near_other)
    )
    from_core = exchange_core(after(gain_part, returns[1]))
    input_grad = input_call(
        ids, after(gain_part, tokens), attn_gain, index, own, d_middle, from_row, from_core, from_chip
    )
    far, far_other, last = [], [], input_grad
    for k in range(3):
        far.append(after(last, got[k]))
        if k == 0:
            small = words_sum(small, far[0][-1:])
            small_other = swap(small, CORE_PAIRS)
        far_other.append(swap(far[k], CORE_PAIRS))
        last = far[k]
    words = (small, small)
    *outs, gain_part = halves_call(1, *common, gain_part, words, far, outs)
    words = (small, small_other)
    *outs, gain_one, gain_two, relative_grad, layout_grad = halves_call(
        2, *common, gain_part, words, after(gain_part, *far_other), outs
    )
    gate_grad, up_grad, down_grad, query_grad, key_grad, value_grad, output_grad = outs
    return (
        layer_out[None], input_grad[None], gain_one, query_grad, key_grad, value_grad,
        output_grad, gain_two, gate_grad, up_grad, down_grad, relative_grad.T, layout_grad.T,
    )


def solution(mesh):
    tokens = P("row", "col", None)
    whole_array = P()
    return jax.shard_map(
        body,
        mesh=mesh,
        in_specs=(tokens,) + (whole_array,) * 11 + (tokens,) * 3 + (P("row", "col", None, None),),
        out_specs=(tokens, tokens) + (whole_array,) * 11,
        check_vma=False,
    )
```
